256 devices in a mesh: dp: 8 (over y, core), bucket: 32 (over x, z).
Axes of the slice: x: 4, y: 4, z: 8, core: 2. Of those that a mesh axis runs over, the one named last changes fastest.
Arguments:
- frames: bfloat16 [393216, 512], P(('dp', 'bucket')), may hold values from -60 to 60, as said below
- lengths: int32 [8, 1024], P('dp'), may hold values from 1 to 48, as said below
- owners: int32 [8, 1024], P('dp'), may hold values from 0 to 31, as said below
- upstream: bfloat16 [196608, 512], P(('dp', 'bucket')), may hold values from -6 to 6
- ln_gain: float32 [512], replicated, may hold values from 0.1 to 1.9
- w_in: bfloat16 [512, 1024], replicated, may hold values from -0.25 to 0.25
- w_dw: float32 [512, 31], replicated, may hold values from -1 to 1
- bn_gain: float32 [512], replicated, may hold values from 0.1 to 1.9
- bn_bias: float32 [512], replicated, may hold values from -3 to 3
- w_out: bfloat16 [512, 512], replicated, may hold values from -0.25 to 0.25
Outputs:
- out_frames: bfloat16 [196608, 512], P(('dp', 'bucket'))
- grad_frames: bfloat16 [393216, 512], P(('dp', 'bucket'))
- grad_w_in: float32 [512, 1024], P('bucket')
- grad_w_out: float32 [512, 512], P('bucket')
- grad_w_dw: float32 [512, 31], P('bucket')
- grad_ln_gain: float32 [512], P('bucket')
- grad_bn_gain: float32 [512], replicated
- grad_bn_bias: float32 [512], replicated
The draws below stay inside these ranges and needn't reach their ends.
Inputs may be any that keep to these rules, and one draw needn't show every extreme that they name: `frames`: frame rows past an utterance's length are not read. In each group every owner receives exactly 1 utterances from each loader shard, their lengths sum to exactly 768 with one of exactly 48, and the lengths an owner receives do not fall with the loader index. `owners`: in each group and loader shard every owner index appears exactly 1 times.
All inputs are finite; a program needn't handle non-finite values.
Results may differ from the reference program's by a relative error of at most 0.013.
Values may be sent and summed in bfloat16 or wider, within the bound.
No kernel may reach another device: no remote copies, remote signals or barrier semaphores. Data moves between devices by JAX's collectives and lax.ppermute only.
A program may use at most 128 MiB of HBM per device.

```python
import math
import jax
import jax.numpy as jnp
from jax import lax

D = 512
K = 31
SLOTS = 32
LMAX = 48
GROUPS = 8
LOADERS = 32
PAIR = 1
OWN_ROWS = 768
OWNED_ALL = 196608


def plan_layout(key):
    base_key = jax.random.fold_in(key, 11)
    len_key, perm_key = jax.random.split(base_key)
    cell_count = (SLOTS - 1) * (LMAX - 1)
    deficit = SLOTS * LMAX - OWN_ROWS

    def owner_lengths(sub_key):
        bias_key, noise_key = jax.random.split(sub_key)
        biases = jax.random.randint(bias_key, (SLOTS - 1, 1), 0, 1024)
        noises = jax.random.randint(noise_key, (SLOTS - 1, LMAX - 1), 0, 512)
        scores = ((biases + noises) * cell_count).reshape(-1) + jnp.arange(cell_count, dtype=jnp.int32)
        cell_rank = jnp.argsort(jnp.argsort(scores))
        chosen = (cell_rank < deficit).astype(jnp.int32).reshape(SLOTS - 1, LMAX - 1)
        shorter = LMAX - jnp.sum(chosen, axis=1)
        full_set = jnp.concatenate([jnp.full((1,), LMAX, jnp.int32), shorter.astype(jnp.int32)])
        return jnp.sort(full_set)
    owner_keys = jax.random.split(len_key, GROUPS * LOADERS)
    sorted_lengths = jax.vmap(owner_lengths)(owner_keys).reshape(GROUPS, LOADERS * SLOTS)
    perm_keys = jax.random.split(perm_key, GROUPS * LOADERS)
    entries = jax.vmap(lambda sub_key: jax.random.permutation(sub_key, SLOTS))(perm_keys)
    entries = entries.reshape(GROUPS, LOADERS, SLOTS).astype(jnp.int32)
    owner_of = entries // PAIR
    pair_of = entries % PAIR
    loader_ids = jnp.arange(LOADERS, dtype=jnp.int32)[None, :, None]
    pick_index = (owner_of * SLOTS + loader_ids * PAIR + pair_of).reshape(GROUPS, LOADERS * SLOTS)
    picked = jnp.take_along_axis(sorted_lengths, pick_index, axis=1)
    return (picked.astype(jnp.int32), owner_of.reshape(GROUPS, LOADERS * SLOTS).astype(jnp.int32))


def draw_lengths(key, part):
    return plan_layout(key)[0]


def draw_owners(key, part):
    return plan_layout(key)[1]


def draw_frames(key, part):
    picked, owner_of = plan_layout(key)
    frame_key = jax.random.fold_in(key, 23)
    noise_key, vector_key, row_key = jax.random.split(frame_key, 3)
    row_total = GROUPS * LOADERS * SLOTS * LMAX
    device_rank = jnp.arange(GROUPS, dtype=jnp.int32)[:, None] * LOADERS + owner_of
    ramp_value = device_rank.astype(jnp.float32).reshape(-1) / float(max(GROUPS * LOADERS - 1, 1))
    noise_part = jax.random.normal(noise_key, (row_total, D), jnp.float32)
    row_scale = jnp.exp(jax.random.uniform(row_key, (row_total,), jnp.float32, 0.0, math.log(3.0)))
    amplitude = jnp.exp(ramp_value * math.log(3.0))
    common = jnp.clip(jax.random.normal(vector_key, (D,), jnp.float32), -3.0, 3.0)
    strength = 0.25 * jnp.repeat(amplitude, LMAX) * row_scale
    return (noise_part + strength[:, None] * common[None, :]).astype(jnp.bfloat16)


def levels(own_key, dims, cuts, least, high):
    gain, own = 1.0, jax.random.fold_in(own_key, 6)
    for axis_at, shards_of in cuts:
        heights = jnp.exp(jax.random.uniform(jax.random.fold_in(own, axis_at), (shards_of,), jnp.float32, least / len(cuts), high / len(cuts)))
        gain = gain * jnp.repeat(heights, dims[axis_at] // shards_of).reshape([-1 if axis == axis_at else 1 for axis in range(len(dims))])
    return gain


def noise(own_key, extent, deviation, most, shards=(), kind=jnp.bfloat16):
    values = jax.random.normal(own_key, extent, jnp.float32) * deviation
    if len(shards) > 0:
        values = levels(own_key, extent, shards, -0.22, 0.18) * values
    return jnp.clip(values, min=-most, max=most).astype(kind)


def setup_inputs(seed: int = 0) -> dict:
    seeds = jax.random.split(jax.random.key(seed), 11)
    return {
        "frames": draw_frames(jax.random.fold_in(seeds[10], 71), 0),
        "lengths": draw_lengths(jax.random.fold_in(seeds[10], 71), 0),
        "owners": draw_owners(jax.random.fold_in(seeds[10], 71), 0),
        "upstream": noise(seeds[3], (OWNED_ALL, D), 1.0, 6.0, ((0, 256),)),
        "ln_gain": jnp.clip(1.0 + 0.18 * jax.random.normal(seeds[4], (D,), jnp.float32), 0.1, 1.9),
        "w_in": noise(seeds[5], (D, 2 * D), D ** -0.5, 0.25),
        "w_dw": noise(seeds[6], (D, K), K ** -0.5, 1.0, (), jnp.float32),
        "bn_gain": jnp.clip(1.0 + 0.18 * jax.random.normal(seeds[7], (D,), jnp.float32), 0.1, 1.9),
        "bn_bias": noise(seeds[8], (D,), 0.5, 3.0, (), jnp.float32),
        "w_out": noise(seeds[9], (D, D), D ** -0.5, 0.25),
    }


EPSILON = 1e-05

def normalize_rows(frame_rows, ln_gain):
    values = frame_rows.astype(jnp.float32)
    centred = values - lax.optimization_barrier(jnp.mean(values, axis=1, keepdims=True))
    inverse = lax.rsqrt(lax.optimization_barrier(jnp.mean(centred * centred, axis=1, keepdims=True)) + EPSILON)
    normed = centred * inverse
    return ((normed * ln_gain).astype(jnp.bfloat16), normed, inverse)

def normalize_back(grad_h, normed, inverse, ln_gain):
    scaled = grad_h * ln_gain
    inner_sum = lax.optimization_barrier(jnp.mean(scaled * normed, axis=1, keepdims=True))
    return inverse * (scaled - lax.optimization_barrier(jnp.mean(scaled, axis=1, keepdims=True)) - normed * inner_sum)

def conv_forward(gated_rows, segment, w_dw):
    width_half = w_dw.shape[1] // 2
    length_all = gated_rows.shape[1]
    padded = jnp.pad(gated_rows, ((0, 0), (width_half, width_half), (0, 0)))
    seg_pad = jnp.pad(segment, ((0, 0), (width_half, width_half)), constant_values=-1)
    result = jnp.zeros(gated_rows.shape, jnp.float32)
    for offset in range(w_dw.shape[1]):
        same_seg = (seg_pad[:, offset:offset + length_all] == segment)[:, :, None]
        shifted = padded[:, offset:offset + length_all].astype(jnp.float32)
        result = result + jnp.where(same_seg, shifted, 0.0) * w_dw[:, offset]
    return result

def conv_backward(grad_conv, gated_rows, segment, w_dw):
    width_half = w_dw.shape[1] // 2
    length_all = gated_rows.shape[1]
    padded = jnp.pad(gated_rows, ((0, 0), (width_half, width_half), (0, 0)))
    grad_pad = jnp.pad(grad_conv, ((0, 0), (width_half, width_half), (0, 0)))
    seg_pad = jnp.pad(segment, ((0, 0), (width_half, width_half)), constant_values=-1)
    grad_gated = jnp.zeros(grad_conv.shape, jnp.float32)
    grad_cols = []
    for offset in range(w_dw.shape[1]):
        same_fwd = (seg_pad[:, offset:offset + length_all] == segment)[:, :, None]
        shifted = jnp.where(same_fwd, padded[:, offset:offset + length_all].astype(jnp.float32), 0.0)
        grad_cols.append(lax.optimization_barrier(jnp.sum(shifted * grad_conv, axis=(0, 1))))
        back_start = 2 * width_half - offset
        same_back = (seg_pad[:, back_start:back_start + length_all] == segment)[:, :, None]
        grad_gated = grad_gated + jnp.where(same_back, grad_pad[:, back_start:back_start + length_all], 0.0) * w_dw[:, offset]
    return (grad_gated, jnp.stack(grad_cols, axis=1))

def reference(frames, lengths, owners, upstream, ln_gain, w_in, w_dw, bn_gain, bn_bias, w_out):
    utterances = LOADERS * SLOTS
    frame_groups = frames.reshape(GROUPS, utterances * LMAX, D)
    grad_groups = upstream.reshape(GROUPS, LOADERS * OWN_ROWS, D)
    position = jnp.arange(LMAX, dtype=jnp.int32)
    segment = jnp.broadcast_to(jnp.arange(utterances, dtype=jnp.int32)[:, None], (utterances, LMAX))
    total_frames = float(GROUPS * LOADERS * OWN_ROWS)
    owner_ids = jnp.arange(LOADERS, dtype=jnp.int32)

    def layout(lens_group, dest_group):
        valid_rows = position[None, :] < lens_group[:, None]
        onehot = (dest_group[:, None] == owner_ids[None, :]).astype(jnp.int32)
        weighted = onehot * lens_group[:, None]
        earlier = jnp.cumsum(weighted, axis=0) - weighted
        starts = lax.optimization_barrier(jnp.sum(earlier * onehot, axis=1))
        target = dest_group[:, None] * OWN_ROWS + starts[:, None] + position[None, :]
        target = jnp.where(valid_rows, target, LOADERS * OWN_ROWS)
        return target.reshape(-1).astype(jnp.int32)

    def forward(frame_block, lens_group):
        valid_rows = (position[None, :] < lens_group[:, None]).reshape(-1)
        normed_h, normed, inverse = normalize_rows(frame_block, ln_gain)
        projected = jnp.dot(normed_h, w_in, preferred_element_type=jnp.float32)
        linear = projected[:, :D]
        gate_sig = jax.nn.sigmoid(projected[:, D:])
        gated_rows = jnp.where(valid_rows[:, None], linear * gate_sig, 0.0).astype(jnp.bfloat16)
        conv_rows = conv_forward(gated_rows.reshape(utterances, LMAX, D), segment, w_dw).reshape(-1, D)
        return (valid_rows, normed_h, normed, inverse, linear, gate_sig, gated_rows, conv_rows)

    def moments(inputs_group):
        frame_block, lens_group = inputs_group
        valid_rows = forward(frame_block, lens_group)[0]
        conv_rows = forward(frame_block, lens_group)[7]
        masked = jnp.where(valid_rows[:, None], conv_rows, 0.0)
        return (lax.optimization_barrier(jnp.sum(masked, axis=0)), lax.optimization_barrier(jnp.sum(masked * masked, axis=0)))
    first_parts, second_parts = lax.map(moments, (frame_groups, lengths))
    centre = lax.optimization_barrier(jnp.sum(first_parts, axis=0)) / total_frames
    variance = lax.optimization_barrier(jnp.sum(second_parts, axis=0)) / total_frames - centre * centre
    bn_inverse = lax.rsqrt(variance + EPSILON)

    def batch_part(conv_rows):
        bn_normed = (conv_rows - centre) * bn_inverse
        bn_value = bn_normed * bn_gain + bn_bias
        bn_sig = jax.nn.sigmoid(bn_value)
        swished = (bn_value * bn_sig).astype(jnp.bfloat16)
        return (bn_normed, bn_value, bn_sig, swished)

    def grad_slots(grad_block, valid_rows, target):
        picked = jnp.take(grad_block, jnp.minimum(target, LOADERS * OWN_ROWS - 1), axis=0)
        return jnp.where(valid_rows[:, None], picked, 0.0).astype(jnp.bfloat16)

    def second_pass(inputs_group):
        frame_block, grad_block, lens_group, dest_group = inputs_group
        target = layout(lens_group, dest_group)
        valid_rows, normed_h, normed, inverse, linear, gate_sig, gated_rows, conv_rows = forward(frame_block, lens_group)
        bn_normed, bn_value, bn_sig, swished = batch_part(conv_rows)
        out_rows = jnp.dot(swished, w_out, preferred_element_type=jnp.float32).astype(jnp.bfloat16)
        packed = jnp.zeros((LOADERS * OWN_ROWS, D), jnp.bfloat16).at[target].set(out_rows, mode='drop')
        grad_out = grad_slots(grad_block, valid_rows, target)
        grad_swish = jnp.dot(grad_out, w_out.T, preferred_element_type=jnp.float32)
        grad_bn_rows = grad_swish * (bn_sig * (1.0 + bn_value * (1.0 - bn_sig)))
        return (packed, lax.optimization_barrier(jnp.sum(grad_bn_rows, axis=0)), lax.optimization_barrier(jnp.sum(grad_bn_rows * bn_normed, axis=0)))
    packed_all, bias_parts, gain_parts = lax.map(second_pass, (frame_groups, grad_groups, lengths, owners))
    bias_total = lax.optimization_barrier(jnp.sum(bias_parts, axis=0))
    gain_total = lax.optimization_barrier(jnp.sum(gain_parts, axis=0))

    def third_pass(inputs_group):
        frame_block, grad_block, lens_group, dest_group = inputs_group
        target = layout(lens_group, dest_group)
        valid_rows, normed_h, normed, inverse, linear, gate_sig, gated_rows, conv_rows = forward(frame_block, lens_group)
        bn_normed, bn_value, bn_sig, swished = batch_part(conv_rows)
        grad_out = grad_slots(grad_block, valid_rows, target)
        grad_wout = jnp.dot(swished.T, grad_out, preferred_element_type=jnp.float32)
        grad_swish = jnp.dot(grad_out, w_out.T, preferred_element_type=jnp.float32)
        grad_bn_rows = grad_swish * (bn_sig * (1.0 + bn_value * (1.0 - bn_sig)))
        grad_conv = jnp.where(valid_rows[:, None], bn_gain * bn_inverse * (grad_bn_rows - bias_total / total_frames - bn_normed * (gain_total / total_frames)), 0.0)
        grad_gated, grad_wdw = conv_backward(grad_conv.reshape(utterances, LMAX, D), gated_rows.reshape(utterances, LMAX, D), segment, w_dw)
        grad_gated = jnp.where(valid_rows[:, None], grad_gated.reshape(-1, D), 0.0)
        grad_proj = jnp.concatenate([grad_gated * gate_sig, grad_gated * linear * gate_sig * (1.0 - gate_sig)], axis=1).astype(jnp.bfloat16)
        grad_win = jnp.dot(normed_h.T, grad_proj, preferred_element_type=jnp.float32)
        grad_h = jnp.dot(grad_proj, w_in.T, preferred_element_type=jnp.float32)
        grad_ln = lax.optimization_barrier(jnp.sum(grad_h * normed, axis=0))
        grad_rows = normalize_back(grad_h, normed, inverse, ln_gain)
        grad_rows = jnp.where(valid_rows[:, None], grad_rows, 0.0).astype(jnp.bfloat16)
        return (grad_rows, grad_win, grad_wout, grad_wdw, grad_ln)
    grad_all, win_parts, wout_parts, wdw_parts, ln_parts = lax.map(third_pass, (frame_groups, grad_groups, lengths, owners))
    return (packed_all.reshape(-1, D), grad_all.reshape(-1, D), lax.optimization_barrier(jnp.sum(win_parts, axis=0)), lax.optimization_barrier(jnp.sum(wout_parts, axis=0)), lax.optimization_barrier(jnp.sum(wdw_parts, axis=0)), lax.optimization_barrier(jnp.sum(ln_parts, axis=0)), gain_total, bias_total)
```

```python
import functools
import math

import jax
import jax.numpy as jnp
import numpy as np
from jax import lax
from jax.experimental import pallas as pl
from jax.experimental.pallas import tpu as pltpu
from jax.sharding import Mesh
from jax.sharding import PartitionSpec as P

BUCKET = ("x", "z")
DP = ("y", "c")
EVERY = ("y", "c", "x", "z")
FIRST = ("c", "z")
SECOND = ("y", "x")

EPSILON = 1e-05
SPAN = 48
POINTS = 64
HALF = POINTS // 2
PER_DFT = 4
PER_STEP = 8
VMEM_LIMIT = 40 * 2**20

F32 = jnp.float32
BF16 = jnp.bfloat16


def dot(a, b, dims=((1,), (0,)), precision=None):
    return lax.dot_general(a, b, (dims, ((), ())), preferred_element_type=F32, precision=precision)


def tables(taps):
    f = np.arange(HALF)[:, None]
    t = np.arange(SPAN)[None, :]
    angle = 2 * np.pi * f * t / POINTS
    real = np.cos(angle) * math.sqrt(2 / POINTS)
    imag = -np.sin(angle) * math.sqrt(2 / POINTS)
    real[0] = math.sqrt(1 / POINTS)
    imag[0] = math.sqrt(1 / POINTS) * (-1.0) ** np.arange(SPAN)
    block = np.zeros((2 * HALF * PER_DFT, SPAN * PER_DFT))
    for u in range(PER_DFT):
        block[u * HALF : (u + 1) * HALF, u * SPAN : (u + 1) * SPAN] = real
        block[(PER_DFT + u) * HALF : (PER_DFT + u + 1) * HALF, u * SPAN : (u + 1) * SPAN] = imag
    lag = np.arange(taps)[None, :] - taps // 2
    turn = 2 * np.pi * f * lag / POINTS
    cos, sin = np.cos(turn), np.sin(turn)
    cos_last = cos.copy()
    cos_last[0] = np.cos(np.pi * lag[0])
    taps_to = np.concatenate([cos, sin, cos_last], axis=0)
    back = np.zeros((2 * HALF + 8, 128))
    back[:HALF, :taps] = cos
    back[HALF : 2 * HALF, :taps] = -sin
    back[HALF, :taps] = np.cos(np.pi * lag[0])
    back[2 * HALF :, taps] = 1.0
    high = block.astype(jnp.bfloat16)
    low = (block - high.astype(np.float64)).astype(jnp.bfloat16)
    return (
        high,
        low,
        np.ascontiguousarray(high.T),
        np.ascontiguousarray(low.T),
        taps_to.astype(np.float32),
        back.astype(np.float32),
    )


def masked(value, lens):
    t = lax.broadcasted_iota(jnp.int32, (SPAN, value.shape[1]), 0)
    return jnp.concatenate(
        [
            jnp.where(t < n, value[u * SPAN : (u + 1) * SPAN], jnp.zeros((), value.dtype))
            for u, n in enumerate(lens)
        ],
        axis=0,
    )


def folded(value):
    return jnp.sum(value.reshape(-1, 8, value.shape[1]), axis=0)


def as_tile(first, second):
    rows = [v[:, k * 128 : (k + 1) * 128] for v in (first, second) for k in range(4)]
    return jnp.concatenate(rows, axis=0)


def from_tile(tile):
    rows = [tile[k : k + 1] for k in range(8)]
    return (jnp.concatenate(rows[:4], axis=1), jnp.concatenate(rows[4:], axis=1))


def normalize(x, gain):
    centred = x - jnp.mean(x, axis=1, keepdims=True)
    inverse = lax.rsqrt(jnp.mean(centred * centred, axis=1, keepdims=True) + EPSILON)
    normed = centred * inverse
    return (normed * gain).astype(BF16), normed, inverse


def spread(wf, part):
    rows = wf[part * HALF : (part + 1) * HALF]
    return jnp.concatenate([rows] * PER_DFT, axis=0)


def unpack_kernel(lens_ref, upstream_ref, out_ref, wide):
    rows = upstream_ref.shape[0]
    wide[:rows, :] = upstream_ref[...].astype(F32)
    wide[rows:, :] = jnp.zeros((8, wide.shape[1]), F32)
    count = out_ref.shape[0] // SPAN

    def step(i, start):
        base = pl.multiple_of(start // 8 * 8, 8)
        window = pltpu.roll(wide[pl.ds(base, SPAN + 8), :], SPAN + 8 - start % 8, 0)
        out_ref[pl.ds(pl.multiple_of(i * SPAN, 16), SPAN), :] = window[:SPAN].astype(BF16)
        return start + lens_ref[i]

    lax.fori_loop(0, count, step, jnp.int32(0))


def pack_kernel(lens_ref, got_ref, out_ref, wide):
    count = got_ref.shape[0] // SPAN
    top = lax.broadcasted_iota(jnp.int32, (8, got_ref.shape[1]), 0)

    def step(i, start):
        base = pl.multiple_of(start // 8 * 8, 8)
        rows = got_ref[pl.ds(pl.multiple_of(i * SPAN, 16), SPAN), :].astype(F32)
        window = jnp.concatenate([rows, jnp.zeros((8, rows.shape[1]), F32)], axis=0)
        window = pltpu.roll(window, start % 8, 0)
        kept = jnp.where(top < start % 8, wide[pl.ds(base, 8), :], window[:8])
        wide[pl.ds(base, 8), :] = kept
        wide[pl.ds(base + 8, SPAN), :] = window[8:]
        return start + lens_ref[i]

    lax.fori_loop(0, count, step, jnp.int32(0))
    out_ref[...] = wide[: out_ref.shape[0], :].astype(BF16)


def step_lens(lens_ref):
    return [lens_ref[pl.program_id(0) * PER_STEP + u] for u in range(PER_STEP)]


def slot_rows(slots_ref, u):
    slot = slots_ref[pl.program_id(0) * PER_STEP + u]
    return pl.ds(pl.multiple_of(slot * SPAN, 16), SPAN)


def forward_kernel(
    lens_ref, slots_ref, frames_ref, gain_ref, win_ref, qh_ref, ql_ref, ih_ref, il_ref, to_ref, wdw_ref,
    lin_ref, sig_ref, freq_ref, conv_ref, wf_ref, stats_ref, acc,
):
    step = pl.program_id(0)

    @pl.when(step == 0)
    def _():
        wf_ref[...] = dot(to_ref[...], wdw_ref[...], ((1,), (1,)), lax.Precision.HIGHEST)
        acc[...] = jnp.zeros_like(acc)

    d = frames_ref.shape[1]
    lens = step_lens(lens_ref)
    x = jnp.concatenate([frames_ref[slot_rows(slots_ref, u), :] for u in range(PER_STEP)], axis=0)
    h, _, _ = normalize(x.astype(F32), gain_ref[...])
    a = dot(h, win_ref[...])
    lin = a[:, :d]
    sig = jax.nn.sigmoid(a[:, d:])
    lin_ref[...] = lin.astype(BF16)
    sig_ref[...] = sig.astype(BF16)
    gated = masked(lin * sig, lens).astype(BF16)
    wa, wb, wl = (spread(wf_ref[...], k) for k in range(3))
    for b in range(PER_STEP // PER_DFT):
        rows = slice(b * SPAN * PER_DFT, (b + 1) * SPAN * PER_DFT)
        part = gated[rows]
        spec = dot(qh_ref[...], part) + dot(ql_ref[...], part)
        freq_ref[b * POINTS * PER_DFT : (b + 1) * POINTS * PER_DFT, :] = spec.astype(BF16)
        re, im = spec[: HALF * PER_DFT], spec[HALF * PER_DFT :]
        turned = jnp.concatenate([re * wa - im * wb, im * wl + re * wb], axis=0)
        high = turned.astype(BF16)
        low = (turned - high.astype(F32)).astype(BF16)
        conv = dot(ih_ref[...], high) + dot(il_ref[...], high) + dot(ih_ref[...], low)
        conv_ref[rows, :] = conv
        live = masked(conv, lens[b * PER_DFT : (b + 1) * PER_DFT])
        acc[0] += folded(live)
        acc[1] += folded(live * live)

    @pl.when(step == pl.num_programs(0) - 1)
    def _():
        sums = [jnp.sum(acc[k], axis=0, keepdims=True) for k in range(2)]
        stats_ref[...] = jnp.broadcast_to(as_tile(*sums)[None], stats_ref.shape)


def relay_kernel(got_ref, out_ref):
    out_ref[...] = jnp.broadcast_to(jnp.sum(got_ref[...], axis=0)[None], out_ref.shape)


def bn_terms(stats, gain_ref, total):
    first, second = from_tile(jnp.sum(stats, axis=0))
    centre = first / total
    inverse = lax.rsqrt(second / total - centre * centre + EPSILON)
    return centre, inverse


def middle_kernel(
    total, lens_ref, conv_ref, dy_ref, stats_ref, gain_ref, bias_ref, wout_ref,
    out_ref, gbn_ref, gwout_ref, sums_ref, acc, sw_all, dy_all,
):
    step = pl.program_id(0)

    @pl.when(step == 0)
    def _():
        acc[...] = jnp.zeros_like(acc)

    centre, inverse = bn_terms(stats_ref[...], gain_ref, total)
    normed = (conv_ref[...] - centre) * inverse
    value = normed * gain_ref[...] + bias_ref[...]
    sig = jax.nn.sigmoid(value)
    swished = (value * sig).astype(BF16)
    out_ref[...] = dot(swished, wout_ref[...]).astype(BF16)
    dy = masked(dy_ref[...].astype(F32), step_lens(lens_ref)).astype(BF16)
    rows = pl.ds(pl.multiple_of(step * PER_STEP * SPAN, 16), PER_STEP * SPAN)
    sw_all[rows, :] = swished
    dy_all[rows, :] = dy
    grad = dot(dy, wout_ref[...], ((1,), (1,))) * (sig * (1.0 + value * (1.0 - sig)))
    gbn_ref[...] = grad
    acc[0] += folded(grad)
    acc[1] += folded(grad * normed)

    @pl.when(step == pl.num_programs(0) - 1)
    def _():
        sums = [jnp.sum(acc[k], axis=0, keepdims=True) for k in range(2)]
        sums_ref[...] = jnp.broadcast_to(as_tile(*sums)[None], sums_ref.shape)
        gwout_ref[...] = dot(sw_all[...], dy_all[...], ((0,), (0,))).astype(BF16)


def backward_kernel(
    total, lens_ref, slots_ref, frames_ref, lin_ref, sig_ref, freq_ref, conv_ref, gbn_ref, wf_ref, stats_ref, sums_ref,
    bn_gain_ref, gain_ref, win_ref, qh_ref, ih_ref, back_ref,
    gframes_ref, gwin_ref, small_ref, bias_ref, bn_out_ref, acc, h_all, ga_all,
):
    step = pl.program_id(0)

    @pl.when(step == 0)
    def _():
        acc[...] = jnp.zeros_like(acc)

    lens = step_lens(lens_ref)
    centre, inverse = bn_terms(stats_ref[...], None, total)
    bias_total, gain_total = from_tile(jnp.sum(sums_ref[...], axis=0))
    bias_ref[...] = bias_total
    bn_out_ref[...] = gain_total
    normed_bn = (conv_ref[...] - centre) * inverse
    scale = bn_gain_ref[...] * inverse
    grad_conv = scale * (gbn_ref[...] - bias_total / total - normed_bn * (gain_total / total))
    grad_conv = masked(grad_conv, lens).astype(BF16)
    wa, wb, wl = (spread(wf_ref[...], k) for k in range(3))
    n = HALF * PER_DFT
    edge = lax.broadcasted_iota(jnp.int32, (n, wa.shape[1]), 0) % HALF == 0
    parts = []
    for b in range(PER_STEP // PER_DFT):
        rows = slice(b * SPAN * PER_DFT, (b + 1) * SPAN * PER_DFT)
        spec = dot(qh_ref[...], grad_conv[rows])
        re, im = spec[:n], spec[n:]
        own = freq_ref[b * 2 * n : (b + 1) * 2 * n, :].astype(F32)
        own_re, own_im = own[:n], own[n:]
        both = im * own_im
        corr_re = re * own_re + jnp.where(edge, 0.0, both)
        corr_im = jnp.where(edge, both, re * own_im - im * own_re)
        acc[0:HALF] += jnp.sum(corr_re.reshape(PER_DFT, HALF, -1), axis=0)
        acc[HALF : 2 * HALF] += jnp.sum(corr_im.reshape(PER_DFT, HALF, -1), axis=0)
        turned = jnp.concatenate([re * wa + im * wb, im * wl - re * wb], axis=0).astype(BF16)
        parts.append(dot(ih_ref[...], turned))
    grad_gated = masked(jnp.concatenate(parts, axis=0), lens)
    lin = lin_ref[...].astype(F32)
    sig = sig_ref[...].astype(F32)
    first = grad_gated * sig
    grad_a = jnp.concatenate([first, first * lin * (1.0 - sig)], axis=1).astype(BF16)
    grad_h = dot(grad_a, win_ref[...], ((1,), (1,)))
    x = jnp.concatenate([frames_ref[slot_rows(slots_ref, u), :] for u in range(PER_STEP)], axis=0)
    gain = gain_ref[...]
    h, normed, inv = normalize(x.astype(F32), gain)
    rows = pl.ds(pl.multiple_of(step * PER_STEP * SPAN, 16), PER_STEP * SPAN)
    h_all[rows, :] = h
    ga_all[rows, :] = grad_a
    acc[2 * HALF :] += folded(grad_h * normed)
    scaled = grad_h * gain
    inner = jnp.mean(scaled * normed, axis=1, keepdims=True)
    grad_x = inv * (scaled - jnp.mean(scaled, axis=1, keepdims=True) - normed * inner)
    grad_x = masked(grad_x, lens).astype(BF16)
    for u in range(PER_STEP):
        gframes_ref[slot_rows(slots_ref, u), :] = grad_x[u * SPAN : (u + 1) * SPAN]

    @pl.when(step == pl.num_programs(0) - 1)
    def _():
        gwin_ref[...] = dot(h_all[...], ga_all[...], ((0,), (0,))).astype(BF16)
        small_ref[...] = dot(acc[...], back_ref[...], ((0,), (0,)), lax.Precision.HIGHEST).astype(BF16)


SMEM = pl.BlockSpec(memory_space=pltpu.SMEM)


def whole(shape):
    return pl.BlockSpec(shape, lambda i: (0,) * len(shape))


def rows_of(shape, steps):
    return pl.BlockSpec((shape[0] // steps, shape[1]), lambda i: (i, 0))


def params():
    return pltpu.CompilerParams(dimension_semantics=("arbitrary",), vmem_limit_bytes=VMEM_LIMIT)


def sds(shape, dtype):
    return jax.ShapeDtypeStruct(shape, dtype)


def unpack(lens, upstream, rows):
    return pl.pallas_call(
        unpack_kernel,
        out_shape=sds((rows, upstream.shape[1]), BF16),
        in_specs=[SMEM, pl.BlockSpec(memory_space=pltpu.VMEM)],
        out_specs=pl.BlockSpec(memory_space=pltpu.VMEM),
        scratch_shapes=[pltpu.VMEM((upstream.shape[0] + 8, upstream.shape[1]), F32)],
        compiler_params=pltpu.CompilerParams(vmem_limit_bytes=VMEM_LIMIT),
        name="unpack",
    )(lens, upstream)


def pack(lens, got, rows):
    return pl.pallas_call(
        pack_kernel,
        out_shape=sds((rows, got.shape[1]), BF16),
        in_specs=[SMEM, pl.BlockSpec(memory_space=pltpu.VMEM)],
        out_specs=pl.BlockSpec(memory_space=pltpu.VMEM),
        scratch_shapes=[pltpu.VMEM((rows + 8, got.shape[1]), F32)],
        compiler_params=pltpu.CompilerParams(vmem_limit_bytes=VMEM_LIMIT),
        name="pack",
    )(lens, got)


def forward(lens, slots, frames, gain, w_in, w_dw, tabs, copies):
    high, low, high_t, low_t, taps_to, _ = tabs
    rows, d = frames.shape
    steps = rows // (SPAN * PER_STEP)
    freq = (rows // SPAN * POINTS, d)
    return pl.pallas_call(
        forward_kernel,
        grid=(steps,),
        out_shape=(
            sds((rows, d), BF16),
            sds((rows, d), BF16),
            sds(freq, BF16),
            sds((rows, d), F32),
            sds((3 * HALF, d), F32),
            sds((copies, 8, 128), F32),
        ),
        in_specs=[SMEM, SMEM, whole(frames.shape), whole(gain.shape), whole(w_in.shape)]
        + [whole(v.shape) for v in (high, low, high_t, low_t, taps_to, w_dw)],
        out_specs=(
            rows_of((rows, d), steps),
            rows_of((rows, d), steps),
            rows_of(freq, steps),
            rows_of((rows, d), steps),
            whole((3 * HALF, d)),
            whole((copies, 8, 128)),
        ),
        scratch_shapes=[pltpu.VMEM((2, 8, d), F32)],
        compiler_params=params(),
        name="forward",
    )(lens, slots, frames, gain, w_in, high, low, high_t, low_t, taps_to, w_dw)


def relay(got, copies):
    return pl.pallas_call(
        relay_kernel,
        out_shape=sds((copies, 8, 128), F32),
        in_specs=[pl.BlockSpec(memory_space=pltpu.VMEM)],
        out_specs=pl.BlockSpec(memory_space=pltpu.VMEM),
        name="relay",
    )(got)


def middle(total, lens, conv, dy, stats, bn_gain, bn_bias, w_out, copies):
    rows, d = conv.shape
    steps = rows // (SPAN * PER_STEP)
    part = rows_of((rows, d), steps)
    return pl.pallas_call(
        functools.partial(middle_kernel, total),
        grid=(steps,),
        out_shape=(
            sds((rows, d), BF16),
            sds((rows, d), F32),
            sds((d, d), BF16),
            sds((copies, 8, 128), F32),
        ),
        in_specs=[SMEM, part, part] + [whole(v.shape) for v in (stats, bn_gain, bn_bias, w_out)],
        out_specs=(part, part, whole((d, d)), whole((copies, 8, 128))),
        scratch_shapes=[pltpu.VMEM((2, 8, d), F32), pltpu.VMEM((rows, d), BF16), pltpu.VMEM((rows, d), BF16)],
        compiler_params=params(),
        name="middle",
    )(lens, conv, dy, stats, bn_gain, bn_bias, w_out)


def backward(total, lens, slots, frames, lin, sig, freq, conv, gbn, wf, stats, sums, bn_gain, gain, w_in, tabs):
    high, _, high_t, _, _, back = tabs
    rows, d = frames.shape
    steps = rows // (SPAN * PER_STEP)
    part = rows_of((rows, d), steps)
    return pl.pallas_call(
        functools.partial(backward_kernel, total),
        grid=(steps,),
        out_shape=(
            sds((rows, d), BF16),
            sds((d, 2 * d), BF16),
            sds((d, 128), BF16),
            sds((1, d), F32),
            sds((1, d), F32),
        ),
        in_specs=[SMEM, SMEM, whole(frames.shape), part, part, rows_of(freq.shape, steps), part, part]
        + [whole(v.shape) for v in (wf, stats, sums, bn_gain, gain, w_in, high, high_t, back)],
        out_specs=(whole((rows, d)), whole((d, 2 * d)), whole((d, 128)), whole((1, d)), whole((1, d))),
        scratch_shapes=[
            pltpu.VMEM((2 * HALF + 8, d), F32),
            pltpu.VMEM((rows, d), BF16),
            pltpu.VMEM((rows, 2 * d), BF16),
        ],
        compiler_params=params(),
        name="backward",
    )(lens, slots, frames, lin, sig, freq, conv, gbn, wf, stats, sums, bn_gain, gain, w_in, high, high_t, back)


def swapped(value, axes):
    return lax.all_to_all(value, axes, split_axis=0, concat_axis=0, tiled=True)


def to_everyone(tiles):
    return swapped(relay(swapped(tiles, FIRST), lax.axis_size(SECOND)), SECOND)


def local(frames, lengths, owners, upstream, ln_gain, w_in, w_dw, bn_gain, bn_bias, w_out):
    loaders = lax.axis_size(BUCKET)
    me = lax.axis_index(BUCKET)
    d = frames.shape[1]
    rows = frames.shape[0]
    taps = w_dw.shape[1]
    total = float(upstream.shape[0] * loaders * lax.axis_size(DP))
    lens_all = lengths.reshape(loaders, loaders)
    dest_all = owners.reshape(loaders, loaders)
    got_lens = jnp.sum(jnp.where(dest_all == me, lens_all, 0), axis=1)
    mine = lax.dynamic_index_in_dim(lens_all, me, 0, keepdims=False)
    to = lax.dynamic_index_in_dim(dest_all, me, 0, keepdims=False)
    ids = jnp.arange(loaders, dtype=jnp.int32)
    hit = to[None, :] == ids[:, None]
    lens = jnp.sum(jnp.where(hit, mine[None, :], 0), axis=1)
    slots = jnp.sum(jnp.where(hit, ids[None, :], 0), axis=1)
    tabs = tuple(jnp.asarray(v) for v in tables(taps))
    gain, bn_gain, bn_bias = (v.reshape(1, d) for v in (ln_gain, bn_gain, bn_bias))

    dy = unpack(got_lens, upstream, rows)
    dy = swapped(dy.reshape(loaders, SPAN, d), BUCKET).reshape(rows, d)
    lin, sig, freq, conv, wf, stats = forward(
        lens, slots, frames, gain, w_in, w_dw, tabs, lax.axis_size(FIRST)
    )
    stats = to_everyone(stats)
    out, gbn, gwout, sums = middle(total, lens, conv, dy, stats, bn_gain, bn_bias, w_out, lax.axis_size(FIRST))
    sums = to_everyone(sums)
    out = swapped(out.reshape(loaders, SPAN, d), BUCKET).reshape(rows, d)
    gframes, gwin, small, bias_total, gain_total = backward(
        total, lens, slots, frames, lin, sig, freq, conv, gbn, wf, stats, sums, bn_gain, gain, w_in, tabs
    )
    share = d // loaders
    grads = jnp.concatenate([gwin, gwout, small], axis=1)
    grads = swapped(grads.reshape(loaders, share, -1), BUCKET)
    grads = jnp.sum(grads.astype(F32), axis=0).astype(BF16)
    grads = swapped(jnp.broadcast_to(grads, (lax.axis_size(DP), *grads.shape)), DP)
    grads = jnp.sum(grads.astype(F32), axis=0)
    out_frames = pack(got_lens, out, upstream.shape[0])
    return (
        out_frames,
        gframes,
        grads[:, : 2 * d],
        grads[:, 2 * d : 3 * d],
        grads[:, 3 * d : 3 * d + taps],
        grads[:, 3 * d + taps],
        gain_total.reshape(d),
        bias_total.reshape(d),
    )


def solution(mesh):
    torus = Mesh(mesh.devices.reshape(4, 2, 4, 8), ("y", "c", "x", "z"))
    in_specs = (P(EVERY, None), P(DP, None), P(DP, None), P(EVERY, None)) + (P(),) * 6
    out_specs = (P(EVERY, None), P(EVERY, None), P(BUCKET, None), P(BUCKET, None), P(BUCKET, None), P(BUCKET), P(), P())
    return jax.shard_map(local, mesh=torus, in_specs=in_specs, out_specs=out_specs, check_vma=False)
```

```python
import functools
import math

import jax
import jax.numpy as jnp
import numpy as np
from jax import lax
from jax.experimental import pallas as pl
from jax.experimental.pallas import tpu as pltpu
from jax.sharding import Mesh
from jax.sharding import PartitionSpec as P

BUCKET = ("x", "z")
DP = ("y", "c")
EVERY = ("y", "c", "x", "z")


EPSILON = 1e-05
SPAN = 48
POINTS = 64
HALF = POINTS // 2
PER_DFT = 4
PER_STEP = 8
VMEM_LIMIT = 60 * 2**20

F32 = jnp.float32
BF16 = jnp.bfloat16


def dot(a, b, dims=((1,), (0,)), precision=None):
    return lax.dot_general(a, b, (dims, ((), ())), preferred_element_type=F32, precision=precision)


def tables(taps):
    f = np.arange(HALF)[:, None]
    t = np.arange(SPAN)[None, :]
    angle = 2 * np.pi * f * t / POINTS
    real = np.cos(angle) * math.sqrt(2 / POINTS)
    imag = -np.sin(angle) * math.sqrt(2 / POINTS)
    real[0] = math.sqrt(1 / POINTS)
    imag[0] = math.sqrt(1 / POINTS) * (-1.0) ** np.arange(SPAN)
    block = np.zeros((2 * HALF * PER_DFT, SPAN * PER_DFT))
    for u in range(PER_DFT):
        block[u * HALF : (u + 1) * HALF, u * SPAN : (u + 1) * SPAN] = real
        block[(PER_DFT + u) * HALF : (PER_DFT + u + 1) * HALF, u * SPAN : (u + 1) * SPAN] = imag
    lag = np.arange(taps)[None, :] - taps // 2
    turn = 2 * np.pi * f * lag / POINTS
    cos, sin = np.cos(turn), np.sin(turn)
    cos_last = cos.copy()
    cos_last[0] = np.cos(np.pi * lag[0])
    taps_to = np.concatenate([cos, sin, cos_last], axis=0)
    back = np.zeros((2 * HALF + 8, 128))
    back[:HALF, :taps] = cos
    back[HALF : 2 * HALF, :taps] = -sin
    back[HALF, :taps] = np.cos(np.pi * lag[0])
    back[2 * HALF :, taps] = 1.0
    high = block.astype(jnp.bfloat16)
    low = (block - high.astype(np.float64)).astype(jnp.bfloat16)
    return (
        high,
        low,
        np.ascontiguousarray(high.T),
        np.ascontiguousarray(low.T),
        taps_to.astype(np.float32),
        back.astype(np.float32),
    )


def masked(value, lens):
    t = lax.broadcasted_iota(jnp.int32, (SPAN, value.shape[1]), 0)
    return jnp.concatenate(
        [
            jnp.where(t < n, value[u * SPAN : (u + 1) * SPAN], jnp.zeros((), value.dtype))
            for u, n in enumerate(lens)
        ],
        axis=0,
    )


def folded(value):
    return jnp.sum(value.reshape(-1, 8, value.shape[1]), axis=0)


def as_tile(first, second):
    rows = [v[:, k * 128 : (k + 1) * 128] for v in (first, second) for k in range(4)]
    return jnp.concatenate(rows, axis=0)


def from_tile(tile):
    rows = [tile[k : k + 1] for k in range(8)]
    return (jnp.concatenate(rows[:4], axis=1), jnp.concatenate(rows[4:], axis=1))


def normalize(x, gain):
    centred = x - jnp.mean(x, axis=1, keepdims=True)
    inverse = lax.rsqrt(jnp.mean(centred * centred, axis=1, keepdims=True) + EPSILON)
    normed = centred * inverse
    return (normed * gain).astype(BF16), normed, inverse


def spread(wf, part):
    rows = wf[part * HALF : (part + 1) * HALF]
    return jnp.concatenate([rows] * PER_DFT, axis=0)


def unpack_kernel(lens_ref, upstream_ref, out_ref, wide):
    rows = upstream_ref.shape[0]
    wide[:rows, :] = upstream_ref[...].astype(F32)
    wide[rows:, :] = jnp.zeros((8, wide.shape[1]), F32)
    count = out_ref.shape[0] // SPAN

    def step(i, start):
        base = pl.multiple_of(start // 8 * 8, 8)
        window = pltpu.roll(wide[pl.ds(base, SPAN + 8), :], SPAN + 8 - start % 8, 0)
        out_ref[pl.ds(pl.multiple_of(i * SPAN, 16), SPAN), :] = window[:SPAN].astype(BF16)
        return start + lens_ref[i]

    lax.fori_loop(0, count, step, jnp.int32(0))


def pack_kernel(lens_ref, got_ref, out_ref, wide):
    count = got_ref.shape[0] // SPAN
    top = lax.broadcasted_iota(jnp.int32, (8, got_ref.shape[1]), 0)

    def step(i, start):
        base = pl.multiple_of(start // 8 * 8, 8)
        rows = got_ref[pl.ds(pl.multiple_of(i * SPAN, 16), SPAN), :].astype(F32)
        window = jnp.concatenate([rows, jnp.zeros((8, rows.shape[1]), F32)], axis=0)
        window = pltpu.roll(window, start % 8, 0)
        kept = jnp.where(top < start % 8, wide[pl.ds(base, 8), :], window[:8])
        wide[pl.ds(base, 8), :] = kept
        wide[pl.ds(base + 8, SPAN), :] = window[8:]
        return start + lens_ref[i]

    lax.fori_loop(0, count, step, jnp.int32(0))
    out_ref[...] = wide[: out_ref.shape[0], :].astype(BF16)


def step_lens(lens_ref):
    return [lens_ref[pl.program_id(0) * PER_STEP + u] for u in range(PER_STEP)]


def slot_rows(slots_ref, u):
    slot = slots_ref[pl.program_id(0) * PER_STEP + u]
    return pl.ds(pl.multiple_of(slot * SPAN, 16), SPAN)


def forward_kernel(
    lens_ref, slots_ref, frames_ref, gain_ref, win_ref, qh_ref, ql_ref, ih_ref, il_ref, to_ref, wdw_ref,
    lin_ref, sig_ref, freq_ref, conv_ref, wf_ref, stats_ref, acc,
):
    step = pl.program_id(0)

    @pl.when(step == 0)
    def _():
        wf_ref[...] = dot(to_ref[...], wdw_ref[...], ((1,), (1,)), lax.Precision.HIGHEST)
        acc[...] = jnp.zeros_like(acc)

    d = frames_ref.shape[1]
    lens = step_lens(lens_ref)
    x = jnp.concatenate([frames_ref[slot_rows(slots_ref, u), :] for u in range(PER_STEP)], axis=0)
    h, _, _ = normalize(x.astype(F32), gain_ref[...])
    a = dot(h, win_ref[...])
    lin = a[:, :d]
    sig = jax.nn.sigmoid(a[:, d:])
    lin_ref[...] = lin.astype(BF16)
    sig_ref[...] = sig.astype(BF16)
    gated = masked(lin * sig, lens).astype(BF16)
    wa, wb, wl = (spread(wf_ref[...], k) for k in range(3))
    for b in range(PER_STEP // PER_DFT):
        rows = slice(b * SPAN * PER_DFT, (b + 1) * SPAN * PER_DFT)
        part = gated[rows]
        spec = dot(qh_ref[...], part) + dot(ql_ref[...], part)
        freq_ref[b * POINTS * PER_DFT : (b + 1) * POINTS * PER_DFT, :] = spec.astype(BF16)
        re, im = spec[: HALF * PER_DFT], spec[HALF * PER_DFT :]
        turned = jnp.concatenate([re * wa - im * wb, im * wl + re * wb], axis=0)
        high = turned.astype(BF16)
        low = (turned - high.astype(F32)).astype(BF16)
        conv = dot(ih_ref[...], high) + dot(il_ref[...], high) + dot(ih_ref[...], low)
        conv_ref[rows, :] = conv
        live = masked(conv, lens[b * PER_DFT : (b + 1) * PER_DFT])
        acc[0] += folded(live)
        acc[1] += folded(live * live)

    @pl.when(step == pl.num_programs(0) - 1)
    def _():
        sums = [jnp.sum(acc[k], axis=0, keepdims=True) for k in range(2)]
        stats_ref[...] = as_tile(*sums)


def bn_terms(stats, gain_ref, total):
    first, second = from_tile(stats)
    centre = first / total
    inverse = lax.rsqrt(second / total - centre * centre + EPSILON)
    return centre, inverse


def middle_kernel(
    total, lens_ref, conv_ref, dy_ref, stats_ref, gain_ref, bias_ref, wout_ref,
    out_ref, gbn_ref, gwout_ref, sums_ref, acc, sw_all, dy_all,
):
    step = pl.program_id(0)

    @pl.when(step == 0)
    def _():
        acc[...] = jnp.zeros_like(acc)

    centre, inverse = bn_terms(stats_ref[...], gain_ref, total)
    normed = (conv_ref[...] - centre) * inverse
    value = normed * gain_ref[...] + bias_ref[...]
    sig = jax.nn.sigmoid(value)
    swished = (value * sig).astype(BF16)
    out_ref[...] = dot(swished, wout_ref[...]).astype(BF16)
    dy = masked(dy_ref[...].astype(F32), step_lens(lens_ref)).astype(BF16)
    rows = pl.ds(pl.multiple_of(step * PER_STEP * SPAN, 16), PER_STEP * SPAN)
    sw_all[rows, :] = swished
    dy_all[rows, :] = dy
    grad = dot(dy, wout_ref[...], ((1,), (1,))) * (sig * (1.0 + value * (1.0 - sig)))
    gbn_ref[...] = grad
    acc[0] += folded(grad)
    acc[1] += folded(grad * normed)

    @pl.when(step == pl.num_programs(0) - 1)
    def _():
        sums = [jnp.sum(acc[k], axis=0, keepdims=True) for k in range(2)]
        sums_ref[...] = as_tile(*sums)
        gwout_ref[...] = dot(sw_all[...], dy_all[...], ((0,), (0,))).astype(BF16)


def backward_kernel(
    total, lens_ref, slots_ref, frames_ref, lin_ref, sig_ref, freq_ref, conv_ref, gbn_ref, wf_ref, stats_ref, sums_ref,
    bn_gain_ref, gain_ref, win_ref, qh_ref, ih_ref, back_ref,
    gframes_ref, gwin_ref, small_ref, bias_ref, bn_out_ref, acc, h_all, ga_all,
):
    step = pl.program_id(0)

    @pl.when(step == 0)
    def _():
        acc[...] = jnp.zeros_like(acc)

    lens = step_lens(lens_ref)
    centre, inverse = bn_terms(stats_ref[...], None, total)
    bias_total, gain_total = from_tile(sums_ref[...])
    bias_ref[...] = bias_total
    bn_out_ref[...] = gain_total
    normed_bn = (conv_ref[...] - centre) * inverse
    scale = bn_gain_ref[...] * inverse
    grad_conv = scale * (gbn_ref[...] - bias_total / total - normed_bn * (gain_total / total))
    grad_conv = masked(grad_conv, lens).astype(BF16)
    wa, wb, wl = (spread(wf_ref[...], k) for k in range(3))
    n = HALF * PER_DFT
    edge = lax.broadcasted_iota(jnp.int32, (n, wa.shape[1]), 0) % HALF == 0
    parts = []
    for b in range(PER_STEP // PER_DFT):
        rows = slice(b * SPAN * PER_DFT, (b + 1) * SPAN * PER_DFT)
        spec = dot(qh_ref[...], grad_conv[rows])
        re, im = spec[:n], spec[n:]
        own = freq_ref[b * 2 * n : (b + 1) * 2 * n, :].astype(F32)
        own_re, own_im = own[:n], own[n:]
        both = im * own_im
        corr_re = re * own_re + jnp.where(edge, 0.0, both)
        corr_im = jnp.where(edge, both, re * own_im - im * own_re)
        acc[0:HALF] += jnp.sum(corr_re.reshape(PER_DFT, HALF, -1), axis=0)
        acc[HALF : 2 * HALF] += jnp.sum(corr_im.reshape(PER_DFT, HALF, -1), axis=0)
        turned = jnp.concatenate([re * wa + im * wb, im * wl - re * wb], axis=0).astype(BF16)
        parts.append(dot(ih_ref[...], turned))
    grad_gated = masked(jnp.concatenate(parts, axis=0), lens)
    lin = lin_ref[...].astype(F32)
    sig = sig_ref[...].astype(F32)
    first = grad_gated * sig
    grad_a = jnp.concatenate([first, first * lin * (1.0 - sig)], axis=1).astype(BF16)
    grad_h = dot(grad_a, win_ref[...], ((1,), (1,)))
    x = jnp.concatenate([frames_ref[slot_rows(slots_ref, u), :] for u in range(PER_STEP)], axis=0)
    gain = gain_ref[...]
    h, normed, inv = normalize(x.astype(F32), gain)
    rows = pl.ds(pl.multiple_of(step * PER_STEP * SPAN, 16), PER_STEP * SPAN)
    h_all[rows, :] = h
    ga_all[rows, :] = grad_a
    acc[2 * HALF :] += folded(grad_h * normed)
    scaled = grad_h * gain
    inner = jnp.mean(scaled * normed, axis=1, keepdims=True)
    grad_x = inv * (scaled - jnp.mean(scaled, axis=1, keepdims=True) - normed * inner)
    grad_x = masked(grad_x, lens).astype(BF16)
    for u in range(PER_STEP):
        gframes_ref[slot_rows(slots_ref, u), :] = grad_x[u * SPAN : (u + 1) * SPAN]

    @pl.when(step == pl.num_programs(0) - 1)
    def _():
        gwin_ref[...] = dot(h_all[...], ga_all[...], ((0,), (0,))).astype(BF16)
        small_ref[...] = dot(acc[...], back_ref[...], ((0,), (0,)), lax.Precision.HIGHEST).astype(BF16)


SMEM = pl.BlockSpec(memory_space=pltpu.SMEM)


def whole(shape):
    return pl.BlockSpec(shape, lambda i: (0,) * len(shape))


def rows_of(shape, steps):
    return pl.BlockSpec((shape[0] // steps, shape[1]), lambda i: (i, 0))


def cost(flops, moved):
    return pl.CostEstimate(flops=int(flops), bytes_accessed=int(moved), transcendentals=0)


def params():
    return pltpu.CompilerParams(dimension_semantics=("arbitrary",), vmem_limit_bytes=VMEM_LIMIT)


def sds(shape, dtype):
    return jax.ShapeDtypeStruct(shape, dtype)


def unpack(lens, upstream, rows):
    return pl.pallas_call(
        unpack_kernel,
        out_shape=sds((rows, upstream.shape[1]), BF16),
        in_specs=[SMEM, pl.BlockSpec(memory_space=pltpu.VMEM)],
        out_specs=pl.BlockSpec(memory_space=pltpu.VMEM),
        scratch_shapes=[pltpu.VMEM((upstream.shape[0] + 8, upstream.shape[1]), F32)],
        compiler_params=pltpu.CompilerParams(vmem_limit_bytes=VMEM_LIMIT),
        name="unpack",
        cost_estimate=cost(1e9, 3 * rows * upstream.shape[1]),
    )(lens, upstream)


def pack(lens, got, rows):
    return pl.pallas_call(
        pack_kernel,
        out_shape=sds((rows, got.shape[1]), BF16),
        in_specs=[SMEM, pl.BlockSpec(memory_space=pltpu.VMEM)],
        out_specs=pl.BlockSpec(memory_space=pltpu.VMEM),
        scratch_shapes=[pltpu.VMEM((rows + 8, got.shape[1]), F32)],
        compiler_params=pltpu.CompilerParams(vmem_limit_bytes=VMEM_LIMIT),
        name="pack",
        cost_estimate=cost(2e9, 6 * rows * got.shape[1]),
    )(lens, got)


def forward(lens, slots, frames, gain, w_in, w_dw, tabs):
    high, low, high_t, low_t, taps_to, _ = tabs
    rows, d = frames.shape
    steps = rows // (SPAN * PER_STEP)
    freq = (rows // SPAN * POINTS, d)
    return pl.pallas_call(
        forward_kernel,
        grid=(steps,),
        out_shape=(
            sds((rows, d), BF16),
            sds((rows, d), BF16),
            sds(freq, BF16),
            sds((rows, d), F32),
            sds((3 * HALF, d), F32),
            sds((8, 128), F32),
        ),
        in_specs=[SMEM, SMEM, whole(frames.shape), whole(gain.shape), whole(w_in.shape)]
        + [whole(v.shape) for v in (high, low, high_t, low_t, taps_to, w_dw)],
        out_specs=(
            rows_of((rows, d), steps),
            rows_of((rows, d), steps),
            rows_of(freq, steps),
            rows_of((rows, d), steps),
            whole((3 * HALF, d)),
            whole((8, 128)),
        ),
        scratch_shapes=[pltpu.VMEM((2, 8, d), F32)],
        compiler_params=params(),
        name="forward",
        cost_estimate=cost(10e9, 16 * rows * d),
    )(lens, slots, frames, gain, w_in, high, low, high_t, low_t, taps_to, w_dw)


def middle(total, lens, conv, dy, stats, bn_gain, bn_bias, w_out):
    rows, d = conv.shape
    steps = rows // (SPAN * PER_STEP)
    part = rows_of((rows, d), steps)
    return pl.pallas_call(
        functools.partial(middle_kernel, total),
        grid=(steps,),
        out_shape=(
            sds((rows, d), BF16),
            sds((rows, d), F32),
            sds((d, d), BF16),
            sds((8, 128), F32),
        ),
        in_specs=[SMEM, part, part] + [whole(v.shape) for v in (stats, bn_gain, bn_bias, w_out)],
        out_specs=(part, part, whole((d, d)), whole((8, 128))),
        scratch_shapes=[pltpu.VMEM((2, 8, d), F32), pltpu.VMEM((rows, d), BF16), pltpu.VMEM((rows, d), BF16)],
        compiler_params=params(),
        name="middle",
        cost_estimate=cost(5e9, 12 * rows * d),
    )(lens, conv, dy, stats, bn_gain, bn_bias, w_out)


def backward(total, lens, slots, frames, lin, sig, freq, conv, gbn, wf, stats, sums, bn_gain, gain, w_in, tabs):
    high, _, high_t, _, _, back = tabs
    rows, d = frames.shape
    steps = rows // (SPAN * PER_STEP)
    part = rows_of((rows, d), steps)
    return pl.pallas_call(
        functools.partial(backward_kernel, total),
        grid=(steps,),
        out_shape=(
            sds((rows, d), BF16),
            sds((d, 2 * d), BF16),
            sds((d, 128), BF16),
            sds((1, d), F32),
            sds((1, d), F32),
        ),
        in_specs=[SMEM, SMEM, whole(frames.shape), part, part, rows_of(freq.shape, steps), part, part]
        + [whole(v.shape) for v in (wf, stats, sums, bn_gain, gain, w_in, high, high_t, back)],
        out_specs=(whole((rows, d)), whole((d, 2 * d)), whole((d, 128)), whole((1, d)), whole((1, d))),
        scratch_shapes=[
            pltpu.VMEM((2 * HALF + 8, d), F32),
            pltpu.VMEM((rows, d), BF16),
            pltpu.VMEM((rows, 2 * d), BF16),
        ],
        compiler_params=params(),
        name="backward",
        cost_estimate=cost(12e9, 18 * rows * d),
    )(lens, slots, frames, lin, sig, freq, conv, gbn, wf, stats, sums, bn_gain, gain, w_in, high, high_t, back)


def swapped(value, axes):
    return lax.all_to_all(value, axes, split_axis=0, concat_axis=0, tiled=True)


def to_everyone(tile):
    return functools.reduce(lax.psum, ("c", "y", "x", "z"), tile)


def sum_of_rows(blocks, ahead):
    pair = lax.axis_size("c")
    core = lax.axis_index("c")
    count, share, width = blocks.shape
    halves = blocks.reshape(count, pair, share // pair, width)
    theirs = lax.dynamic_index_in_dim(halves, 1 - core, 1, keepdims=False)
    own = lax.dynamic_index_in_dim(halves, core, 1, keepdims=False)
    got = lax.ppermute(theirs, "c", [(0, 1), (1, 0)])
    both = (own.astype(F32) + got.astype(F32)).astype(BF16)
    both, ahead = lax.optimization_barrier((both, ahead))
    mine = jnp.sum(swapped(both, BUCKET).astype(F32), axis=0).astype(BF16)
    every = swapped(jnp.broadcast_to(mine, (lax.axis_size(DP), *mine.shape)), DP).astype(F32)
    return jnp.sum(every.reshape(-1, pair, share // pair, width), axis=0).reshape(share, width), ahead


def local(frames, lengths, owners, upstream, ln_gain, w_in, w_dw, bn_gain, bn_bias, w_out):
    loaders = lax.axis_size(BUCKET)
    me = lax.axis_index(BUCKET)
    d = frames.shape[1]
    rows = frames.shape[0]
    taps = w_dw.shape[1]
    total = float(upstream.shape[0] * loaders * lax.axis_size(DP))
    lens_all = lengths.reshape(loaders, loaders)
    dest_all = owners.reshape(loaders, loaders)
    got_lens = jnp.sum(jnp.where(dest_all == me, lens_all, 0), axis=1)
    mine = lax.dynamic_index_in_dim(lens_all, me, 0, keepdims=False)
    to = lax.dynamic_index_in_dim(dest_all, me, 0, keepdims=False)
    ids = jnp.arange(loaders, dtype=jnp.int32)
    hit = to[None, :] == ids[:, None]
    lens = jnp.sum(jnp.where(hit, mine[None, :], 0), axis=1)
    slots = jnp.sum(jnp.where(hit, ids[None, :], 0), axis=1)
    tabs = tuple(jnp.asarray(v) for v in tables(taps))
    gain, bn_gain, bn_bias = (v.reshape(1, d) for v in (ln_gain, bn_gain, bn_bias))

    dy = unpack(got_lens, upstream, rows)
    dy = swapped(dy.reshape(loaders, SPAN, d), BUCKET).reshape(rows, d)
    lin, sig, freq, conv, wf, stats = forward(lens, slots, frames, gain, w_in, w_dw, tabs)
    stats = to_everyone(stats)
    out, gbn, gwout, sums = middle(total, lens, conv, dy, stats, bn_gain, bn_bias, w_out)
    sums = to_everyone(sums)
    out = swapped(out.reshape(loaders, SPAN, d), BUCKET).reshape(rows, d)
    gframes, gwin, small, bias_total, gain_total = backward(
        total, lens, slots, frames, lin, sig, freq, conv, gbn, wf, stats, sums, bn_gain, gain, w_in, tabs
    )
    share = d // loaders
    grads = jnp.concatenate([gwin, gwout, small], axis=1)
    grads, out = sum_of_rows(grads.reshape(loaders, share, -1), out)
    out_frames = pack(got_lens, out, upstream.shape[0])
    return (
        out_frames,
        gframes,
        grads[:, : 2 * d],
        grads[:, 2 * d : 3 * d],
        grads[:, 3 * d : 3 * d + taps],
        grads[:, 3 * d + taps],
        gain_total.reshape(d),
        bias_total.reshape(d),
    )


def solution(mesh):
    torus = Mesh(mesh.devices.reshape(4, 2, 4, 8), ("y", "c", "x", "z"))
    in_specs = (P(EVERY, None), P(DP, None), P(DP, None), P(EVERY, None)) + (P(),) * 6
    out_specs = (P(EVERY, None), P(EVERY, None), P(BUCKET, None), P(BUCKET, None), P(BUCKET, None), P(BUCKET), P(), P())
    return jax.shard_map(local, mesh=torus, in_specs=in_specs, out_specs=out_specs, check_vma=False)
```

```python
import functools
import math

import jax
import jax.numpy as jnp
import numpy as np
from jax import lax
from jax.experimental import pallas as pl
from jax.experimental.pallas import tpu as pltpu
from jax.sharding import Mesh
from jax.sharding import PartitionSpec as P

BUCKET = ("x", "z")
DP = ("y", "c")
EVERY = ("y", "c", "x", "z")


EPSILON = 1e-05
SPAN = 48
POINTS = 64
HALF = POINTS // 2
PER_DFT = 4
PER_STEP = 8
VMEM_LIMIT = 60 * 2**20

F32 = jnp.float32
BF16 = jnp.bfloat16


def dot(a, b, dims=((1,), (0,)), precision=None):
    return lax.dot_general(a, b, (dims, ((), ())), preferred_element_type=F32, precision=precision)


def tables(taps):
    f = np.arange(HALF)[:, None]
    t = np.arange(SPAN)[None, :]
    angle = 2 * np.pi * f * t / POINTS
    real = np.cos(angle) * math.sqrt(2 / POINTS)
    imag = -np.sin(angle) * math.sqrt(2 / POINTS)
    real[0] = math.sqrt(1 / POINTS)
    imag[0] = math.sqrt(1 / POINTS) * (-1.0) ** np.arange(SPAN)
    block = np.zeros((2 * HALF * PER_DFT, SPAN * PER_DFT))
    for u in range(PER_DFT):
        block[u * HALF : (u + 1) * HALF, u * SPAN : (u + 1) * SPAN] = real
        block[(PER_DFT + u) * HALF : (PER_DFT + u + 1) * HALF, u * SPAN : (u + 1) * SPAN] = imag
    lag = np.arange(taps)[None, :] - taps // 2
    turn = 2 * np.pi * f * lag / POINTS
    cos, sin = np.cos(turn), np.sin(turn)
    cos_last = cos.copy()
    cos_last[0] = np.cos(np.pi * lag[0])
    taps_to = np.concatenate([cos, sin, cos_last], axis=0)
    back = np.zeros((2 * HALF, 128))
    back[:HALF, :taps] = cos
    back[HALF : 2 * HALF, :taps] = -sin
    back[HALF, :taps] = np.cos(np.pi * lag[0])
    high = block.astype(jnp.bfloat16)
    low = (block - high.astype(np.float64)).astype(jnp.bfloat16)
    return (
        high,
        low,
        np.ascontiguousarray(high.T),
        np.ascontiguousarray(low.T),
        taps_to.astype(np.float32),
        back.astype(np.float32),
    )


def masked(value, lens):
    t = lax.broadcasted_iota(jnp.int32, (SPAN, value.shape[1]), 0)
    return jnp.concatenate(
        [
            jnp.where(t < n, value[u * SPAN : (u + 1) * SPAN], jnp.zeros((), value.dtype))
            for u, n in enumerate(lens)
        ],
        axis=0,
    )


def folded(value):
    return jnp.sum(value.reshape(-1, 8, value.shape[1]), axis=0)


def as_tile(first, second):
    rows = [v[:, k * 128 : (k + 1) * 128] for v in (first, second) for k in range(4)]
    return jnp.concatenate(rows, axis=0)


def from_tile(tile):
    rows = [tile[k : k + 1] for k in range(8)]
    return (jnp.concatenate(rows[:4], axis=1), jnp.concatenate(rows[4:], axis=1))


def normalize(x, gain):
    centred = x - jnp.mean(x, axis=1, keepdims=True)
    inverse = lax.rsqrt(jnp.mean(centred * centred, axis=1, keepdims=True) + EPSILON)
    normed = centred * inverse
    return (normed * gain).astype(BF16), normed, inverse


def spread(wf, part):
    rows = wf[part * HALF : (part + 1) * HALF]
    return jnp.concatenate([rows] * PER_DFT, axis=0)


def unpack_kernel(lengths_ref, owners_ref, upstream_ref, out_ref, table_ref, wide, lens_all, dest_all, table, sem):
    loaders = lens_all.shape[0]
    me = lax.axis_index(BUCKET)
    for k in range(loaders):
        lens_all[k : k + 1, :] = lengths_ref[:, k * loaders : (k + 1) * loaders]
        dest_all[k : k + 1, :] = owners_ref[:, k * loaders : (k + 1) * loaders]
    got = jnp.sum(jnp.where(dest_all[...] == me, lens_all[...], 0), axis=1, keepdims=True)
    square = (loaders, loaders)
    hit = dest_all[pl.ds(me, 1), :] == lax.broadcasted_iota(jnp.int32, square, 0)
    lens = jnp.sum(jnp.where(hit, lens_all[pl.ds(me, 1), :], 0), axis=1, keepdims=True)
    slots = jnp.sum(jnp.where(hit, lax.broadcasted_iota(jnp.int32, square, 1), 0), axis=1, keepdims=True)
    column = lax.broadcasted_iota(jnp.int32, table_ref.shape, 1)
    table_ref[...] = jnp.where(column == 0, got, jnp.where(column == 1, lens, slots))
    copy = pltpu.make_async_copy(table_ref, table, sem)
    copy.start()
    rows = upstream_ref.shape[0]
    wide[:rows, :] = upstream_ref[...].astype(F32)
    wide[rows:, :] = jnp.zeros((8, wide.shape[1]), F32)
    copy.wait()

    def step(i, start):
        base = pl.multiple_of(start // 8 * 8, 8)
        window = pltpu.roll(wide[pl.ds(base, SPAN + 8), :], SPAN + 8 - start % 8, 0)
        out_ref[pl.ds(pl.multiple_of(i * SPAN, 16), SPAN), :] = window[:SPAN].astype(BF16)
        return start + table[i, 0]

    lax.fori_loop(0, loaders, step, jnp.int32(0))


def pack_kernel(table_ref, got_ref, out_ref, wide):
    count = got_ref.shape[0] // SPAN
    top = lax.broadcasted_iota(jnp.int32, (8, got_ref.shape[1]), 0)

    def step(i, start):
        base = pl.multiple_of(start // 8 * 8, 8)
        rows = got_ref[pl.ds(pl.multiple_of(i * SPAN, 16), SPAN), :].astype(F32)
        window = jnp.concatenate([rows, jnp.zeros((8, rows.shape[1]), F32)], axis=0)
        window = pltpu.roll(window, start % 8, 0)
        kept = jnp.where(top < start % 8, wide[pl.ds(base, 8), :], window[:8])
        wide[pl.ds(base, 8), :] = kept
        wide[pl.ds(base + 8, SPAN), :] = window[8:]
        return start + table_ref[i, 0]

    lax.fori_loop(0, count, step, jnp.int32(0))
    out_ref[...] = wide[: out_ref.shape[0], :].astype(BF16)


def step_lens(table_ref):
    return [table_ref[pl.program_id(0) * PER_STEP + u, 1] for u in range(PER_STEP)]


def slot_rows(table_ref, u):
    slot = table_ref[pl.program_id(0) * PER_STEP + u, 2]
    return pl.ds(pl.multiple_of(slot * SPAN, 16), SPAN)


def forward_kernel(
    table_ref, frames_ref, gain_ref, win_ref, qh_ref, ql_ref, ih_ref, il_ref, to_ref, wdw_ref,
    h_ref, lin_ref, sig_ref, freq_ref, conv_ref, wf_ref, stats_ref, acc,
):
    step = pl.program_id(0)

    @pl.when(step == 0)
    def _():
        wf_ref[...] = dot(to_ref[...], wdw_ref[...], ((1,), (1,)), lax.Precision.HIGHEST)
        acc[...] = jnp.zeros_like(acc)

    d = frames_ref.shape[1]
    lens = step_lens(table_ref)
    x = jnp.concatenate([frames_ref[slot_rows(table_ref, u), :] for u in range(PER_STEP)], axis=0)
    h, _, _ = normalize(x.astype(F32), gain_ref[...])
    h_ref[...] = h
    a = dot(h, win_ref[...])
    lin = a[:, :d]
    sig = jax.nn.sigmoid(a[:, d:])
    lin_ref[...] = lin.astype(BF16)
    sig_ref[...] = sig.astype(BF16)
    gated = masked(lin * sig, lens).astype(BF16)
    wa, wb, wl = (spread(wf_ref[...], k) for k in range(3))
    for b in range(PER_STEP // PER_DFT):
        rows = slice(b * SPAN * PER_DFT, (b + 1) * SPAN * PER_DFT)
        part = gated[rows]
        spec = dot(qh_ref[...], part) + dot(ql_ref[...], part)
        freq_ref[b * POINTS * PER_DFT : (b + 1) * POINTS * PER_DFT, :] = spec.astype(BF16)
        re, im = spec[: HALF * PER_DFT], spec[HALF * PER_DFT :]
        turned = jnp.concatenate([re * wa - im * wb, im * wl + re * wb], axis=0)
        high = turned.astype(BF16)
        low = (turned - high.astype(F32)).astype(BF16)
        conv = dot(ih_ref[...], high) + dot(il_ref[...], high) + dot(ih_ref[...], low)
        conv_ref[rows, :] = conv
        live = masked(conv, lens[b * PER_DFT : (b + 1) * PER_DFT])
        acc[0] += folded(live)
        acc[1] += folded(live * live)

    @pl.when(step == pl.num_programs(0) - 1)
    def _():
        sums = [jnp.sum(acc[k], axis=0, keepdims=True) for k in range(2)]
        stats_ref[...] = as_tile(*sums)


def split(value, theirs_ref, own_ref):
    blocks = value.reshape(-1, 2, 8, value.shape[1])
    first = lax.axis_index("c") == 0
    low, high = blocks[:, 0], blocks[:, 1]
    theirs_ref[...] = jnp.where(first, high, low).reshape(theirs_ref.shape).astype(BF16)
    own_ref[...] = jnp.where(first, low, high).reshape(own_ref.shape).astype(BF16)


def bn_terms(stats, total):
    first, second = from_tile(stats)
    centre = first / total
    inverse = lax.rsqrt(second / total - centre * centre + EPSILON)
    return centre, inverse


def middle_kernel(
    total, table_ref, conv_ref, dy_ref, stats_ref, gain_ref, bias_ref, wout_ref,
    out_ref, gbn_ref, theirs_ref, own_ref, sums_ref, moments_ref, acc, sw_all, dy_all,
):
    step = pl.program_id(0)

    @pl.when(step == 0)
    def _():
        acc[...] = jnp.zeros_like(acc)
        moments_ref[...] = jnp.sum(stats_ref[...], axis=0)

    centre, inverse = bn_terms(moments_ref[...], total)
    normed = (conv_ref[...] - centre) * inverse
    value = normed * gain_ref[...] + bias_ref[...]
    sig = jax.nn.sigmoid(value)
    swished = (value * sig).astype(BF16)
    out_ref[...] = dot(swished, wout_ref[...]).astype(BF16)
    dy = masked(dy_ref[...].astype(F32), step_lens(table_ref)).astype(BF16)
    rows = pl.ds(pl.multiple_of(step * PER_STEP * SPAN, 16), PER_STEP * SPAN)
    sw_all[rows, :] = swished
    dy_all[rows, :] = dy
    grad = dot(dy, wout_ref[...], ((1,), (1,))) * (sig * (1.0 + value * (1.0 - sig)))
    gbn_ref[...] = grad
    acc[0] += folded(grad)
    acc[1] += folded(grad * normed)

    @pl.when(step == pl.num_programs(0) - 1)
    def _():
        sums = [jnp.sum(acc[k], axis=0, keepdims=True) for k in range(2)]
        sums_ref[...] = as_tile(*sums)
        split(dot(sw_all[...], dy_all[...], ((0,), (0,))), theirs_ref, own_ref)


def backward_kernel(
    total, table_ref, h_ref, lin_ref, sig_ref, freq_ref, conv_ref, gbn_ref, wf_ref, stats_ref, sums_ref,
    bn_gain_ref, theirs_in, own_in, qh_ref, ih_ref, back_ref,
    grad_a_ref, theirs_ref, own_ref, bias_ref, bn_out_ref, acc, h_all, ga_all,
):
    step = pl.program_id(0)

    @pl.when(step == 0)
    def _():
        acc[...] = jnp.zeros_like(acc)

    lens = step_lens(table_ref)
    centre, inverse = bn_terms(stats_ref[...], total)
    bias_total, gain_total = from_tile(sums_ref[...])
    bias_ref[...] = bias_total
    bn_out_ref[...] = gain_total
    normed_bn = (conv_ref[...] - centre) * inverse
    scale = bn_gain_ref[...] * inverse
    grad_conv = scale * (gbn_ref[...] - bias_total / total - normed_bn * (gain_total / total))
    grad_conv = masked(grad_conv, lens).astype(BF16)
    wa, wb, wl = (spread(wf_ref[...], k) for k in range(3))
    n = HALF * PER_DFT
    edge = lax.broadcasted_iota(jnp.int32, (n, wa.shape[1]), 0) % HALF == 0
    parts = []
    for b in range(PER_STEP // PER_DFT):
        rows = slice(b * SPAN * PER_DFT, (b + 1) * SPAN * PER_DFT)
        spec = dot(qh_ref[...], grad_conv[rows])
        re, im = spec[:n], spec[n:]
        own = freq_ref[b * 2 * n : (b + 1) * 2 * n, :].astype(F32)
        own_re, own_im = own[:n], own[n:]
        both = im * own_im
        corr_re = re * own_re + jnp.where(edge, 0.0, both)
        corr_im = jnp.where(edge, both, re * own_im - im * own_re)
        acc[:HALF] += jnp.sum(corr_re.reshape(PER_DFT, HALF, -1), axis=0)
        acc[HALF:] += jnp.sum(corr_im.reshape(PER_DFT, HALF, -1), axis=0)
        turned = jnp.concatenate([re * wa + im * wb, im * wl - re * wb], axis=0).astype(BF16)
        parts.append(dot(ih_ref[...], turned))
    grad_gated = masked(jnp.concatenate(parts, axis=0), lens)
    lin = lin_ref[...].astype(F32)
    sig = sig_ref[...].astype(F32)
    first = grad_gated * sig
    grad_a = jnp.concatenate([first, first * lin * (1.0 - sig)], axis=1).astype(BF16)
    grad_a_ref[...] = grad_a
    rows = pl.ds(pl.multiple_of(step * PER_STEP * SPAN, 16), PER_STEP * SPAN)
    h_all[rows, :] = h_ref[...]
    ga_all[rows, :] = grad_a

    @pl.when(step == pl.num_programs(0) - 1)
    def _():
        d = h_all.shape[1]
        gwin, gwout, taps = slice(0, 2 * d), slice(2 * d, 3 * d), slice(3 * d, theirs_ref.shape[1])
        theirs_ref[:, gwout] = theirs_in[...]
        own_ref[:, gwout] = own_in[...]
        small = dot(acc[...], back_ref[...], ((0,), (0,)), lax.Precision.HIGHEST)
        split(small, theirs_ref.at[:, taps], own_ref.at[:, taps])
        split(dot(h_all[...], ga_all[...], ((0,), (0,))), theirs_ref.at[:, gwin], own_ref.at[:, gwin])


def inputs_kernel(table_ref, frames_ref, grad_a_ref, gain_ref, win_ref, gframes_ref):
    grad_h = dot(grad_a_ref[...], win_ref[...], ((1,), (1,)))
    x = jnp.concatenate([frames_ref[slot_rows(table_ref, u), :] for u in range(PER_STEP)], axis=0)
    gain = gain_ref[...]
    _, normed, inv = normalize(x.astype(F32), gain)
    scaled = grad_h * gain
    inner = jnp.mean(scaled * normed, axis=1, keepdims=True)
    grad_x = inv * (scaled - jnp.mean(scaled, axis=1, keepdims=True) - normed * inner)
    grad_x = masked(grad_x, step_lens(table_ref)).astype(BF16)
    for u in range(PER_STEP):
        gframes_ref[slot_rows(table_ref, u), :] = grad_x[u * SPAN : (u + 1) * SPAN]


def finish_kernel(every_ref, w_ref, gain_ref, gwin_ref, gwout_ref, gwdw_ref, gln_ref):
    count = every_ref.shape[0]
    halves = [sum(every_ref[k].astype(F32) for k in range(core, count, 2)) for core in range(2)]
    rows = jnp.concatenate(halves, axis=0)
    d = gwout_ref.shape[1]
    gwin = rows[:, : 2 * d]
    gwin_ref[...] = gwin
    gwout_ref[...] = rows[:, 2 * d : 3 * d]
    gwdw_ref[...] = rows[:, 3 * d : 3 * d + gwdw_ref.shape[1]]
    ones = jnp.ones((8, 2 * d), F32)
    dots = dot(ones, gwin * w_ref[...].astype(F32), ((1,), (1,)), lax.Precision.HIGHEST)
    gln_ref[...] = dots[:1] / gain_ref[...]


SMEM = pl.BlockSpec(memory_space=pltpu.SMEM)


def whole(shape):
    return pl.BlockSpec(shape, lambda i: (0,) * len(shape))


def rows_of(shape, steps):
    return pl.BlockSpec((shape[0] // steps, shape[1]), lambda i: (i, 0))


def cost(flops, moved):
    return pl.CostEstimate(flops=int(flops), bytes_accessed=int(moved), transcendentals=0)


def params():
    return pltpu.CompilerParams(dimension_semantics=("arbitrary",), vmem_limit_bytes=VMEM_LIMIT)


def sds(shape, dtype):
    return jax.ShapeDtypeStruct(shape, dtype)


def unpack(lengths, owners, upstream, loaders):
    rows, d = upstream.shape
    vmem = pl.BlockSpec(memory_space=pltpu.VMEM)
    return pl.pallas_call(
        unpack_kernel,
        out_shape=(sds((loaders * SPAN, d), BF16), sds((loaders, 128), jnp.int32)),
        in_specs=[vmem] * 3,
        out_specs=(vmem, vmem),
        scratch_shapes=[
            pltpu.VMEM((rows + 8, d), F32),
            pltpu.VMEM((loaders, loaders), jnp.int32),
            pltpu.VMEM((loaders, loaders), jnp.int32),
            pltpu.SMEM((loaders, 128), jnp.int32),
            pltpu.SemaphoreType.DMA,
        ],
        compiler_params=pltpu.CompilerParams(vmem_limit_bytes=VMEM_LIMIT),
        name="unpack",
        cost_estimate=cost(1e9, 6 * rows * d),
    )(lengths, owners, upstream)


def pack(table, got, rows):
    return pl.pallas_call(
        pack_kernel,
        out_shape=sds((rows, got.shape[1]), BF16),
        in_specs=[SMEM, pl.BlockSpec(memory_space=pltpu.VMEM)],
        out_specs=pl.BlockSpec(memory_space=pltpu.VMEM),
        scratch_shapes=[pltpu.VMEM((rows + 8, got.shape[1]), F32)],
        compiler_params=pltpu.CompilerParams(vmem_limit_bytes=VMEM_LIMIT),
        name="pack",
        cost_estimate=cost(2e9, 6 * rows * got.shape[1]),
    )(table, got)


def forward(table, frames, gain, w_in, w_dw, tabs):
    high, low, high_t, low_t, taps_to, _ = tabs
    rows, d = frames.shape
    steps = rows // (SPAN * PER_STEP)
    freq = (rows // SPAN * POINTS, d)
    return pl.pallas_call(
        forward_kernel,
        grid=(steps,),
        out_shape=(
            sds((rows, d), BF16),
            sds((rows, d), BF16),
            sds((rows, d), BF16),
            sds(freq, BF16),
            sds((rows, d), F32),
            sds((3 * HALF, d), F32),
            sds((8, 128), F32),
        ),
        in_specs=[SMEM, whole(frames.shape), whole(gain.shape), whole(w_in.shape)]
        + [whole(v.shape) for v in (high, low, high_t, low_t, taps_to, w_dw)],
        out_specs=(
            rows_of((rows, d), steps),
            rows_of((rows, d), steps),
            rows_of((rows, d), steps),
            rows_of(freq, steps),
            rows_of((rows, d), steps),
            whole((3 * HALF, d)),
            whole((8, 128)),
        ),
        scratch_shapes=[pltpu.VMEM((2, 8, d), F32)],
        compiler_params=params(),
        name="forward",
        cost_estimate=cost(10e9, 16 * rows * d),
    )(table, frames, gain, w_in, high, low, high_t, low_t, taps_to, w_dw)


def middle(total, table, conv, dy, stats, bn_gain, bn_bias, w_out):
    rows, d = conv.shape
    steps = rows // (SPAN * PER_STEP)
    part = rows_of((rows, d), steps)
    return pl.pallas_call(
        functools.partial(middle_kernel, total),
        grid=(steps,),
        out_shape=(
            sds((rows, d), BF16),
            sds((rows, d), F32),
            sds((d // 2, d), BF16),
            sds((d // 2, d), BF16),
            sds((8, 128), F32),
            sds((8, 128), F32),
        ),
        in_specs=[SMEM, part, part] + [whole(v.shape) for v in (stats, bn_gain, bn_bias, w_out)],
        out_specs=(part, part, whole((d // 2, d)), whole((d // 2, d)), whole((8, 128)), whole((8, 128))),
        scratch_shapes=[pltpu.VMEM((2, 8, d), F32), pltpu.VMEM((rows, d), BF16), pltpu.VMEM((rows, d), BF16)],
        compiler_params=params(),
        name="middle",
        cost_estimate=cost(5e9, 12 * rows * d),
    )(table, conv, dy, stats, bn_gain, bn_bias, w_out)


def backward(total, table, h, lin, sig, freq, conv, gbn, wf, stats, sums, bn_gain, theirs, own, tabs):
    high, _, high_t, _, _, back = tabs
    rows, d = h.shape
    width = 3 * d + back.shape[1]
    steps = rows // (SPAN * PER_STEP)
    part = rows_of((rows, d), steps)
    return pl.pallas_call(
        functools.partial(backward_kernel, total),
        grid=(steps,),
        out_shape=(
            sds((rows, 2 * d), BF16),
            sds((d // 2, width), BF16),
            sds((d // 2, width), BF16),
            sds((1, d), F32),
            sds((1, d), F32),
        ),
        in_specs=[SMEM, part, part, part, rows_of(freq.shape, steps), part, part]
        + [whole(v.shape) for v in (wf, stats, sums, bn_gain, theirs, own, high, high_t, back)],
        out_specs=(
            rows_of((rows, 2 * d), steps),
            whole((d // 2, width)),
            whole((d // 2, width)),
            whole((1, d)),
            whole((1, d)),
        ),
        scratch_shapes=[
            pltpu.VMEM((2 * HALF, d), F32),
            pltpu.VMEM((rows, d), BF16),
            pltpu.VMEM((rows, 2 * d), BF16),
        ],
        compiler_params=params(),
        name="backward",
        cost_estimate=cost(8e9, 18 * rows * d),
    )(table, h, lin, sig, freq, conv, gbn, wf, stats, sums, bn_gain, theirs, own, high, high_t, back)


def inputs_back(table, frames, grad_a, gain, w_in):
    rows, d = frames.shape
    steps = rows // (SPAN * PER_STEP)
    return pl.pallas_call(
        inputs_kernel,
        grid=(steps,),
        out_shape=sds((rows, d), BF16),
        in_specs=[SMEM, whole(frames.shape), rows_of(grad_a.shape, steps), whole(gain.shape), whole(w_in.shape)],
        out_specs=whole((rows, d)),
        compiler_params=params(),
        name="inputs_back",
        cost_estimate=cost(6e9, 12 * rows * d),
    )(table, frames, grad_a, gain, w_in)


def finish(every, w_rows, gain_rows, taps):
    share, width = w_rows.shape
    d = width // 2
    vmem = pl.BlockSpec(memory_space=pltpu.VMEM)
    return pl.pallas_call(
        finish_kernel,
        out_shape=(sds((share, width), F32), sds((share, d), F32), sds((share, taps), F32), sds((1, share), F32)),
        in_specs=[vmem] * 3,
        out_specs=(vmem,) * 4,
        compiler_params=pltpu.CompilerParams(vmem_limit_bytes=VMEM_LIMIT),
        name="finish",
    )(every, w_rows, gain_rows)


def swapped(value, axes):
    return lax.all_to_all(value, axes, split_axis=0, concat_axis=0, tiled=True)


def to_everyone(tile):
    return functools.reduce(lax.psum, ("c", "y", "x", "z"), tile)


def sum_of_rows(theirs, own, loaders, ahead):
    got = lax.ppermute(theirs, "c", [(0, 1), (1, 0)])
    both = (own.astype(F32) + got.astype(F32)).astype(BF16).reshape(loaders, -1, own.shape[1])
    both, ahead = lax.optimization_barrier((both, ahead))
    mine = jnp.sum(swapped(both, BUCKET).astype(F32), axis=0).astype(BF16)
    return swapped(jnp.broadcast_to(mine, (lax.axis_size(DP), *mine.shape)), DP), ahead


def local(frames, lengths, owners, upstream, ln_gain, w_in, w_dw, bn_gain, bn_bias, w_out):
    loaders = lax.axis_size(BUCKET)
    me = lax.axis_index(BUCKET)
    rows, d = frames.shape
    taps = w_dw.shape[1]
    share = d // loaders
    total = float(upstream.shape[0] * loaders * lax.axis_size(DP))
    tabs = tuple(jnp.asarray(v) for v in tables(taps))
    w_rows = lax.dynamic_slice_in_dim(w_in, me * share, share, 0)
    gain_rows = lax.dynamic_slice_in_dim(ln_gain, me * share, share, 0).reshape(1, share)
    gain, bn_gain, bn_bias = (v.reshape(1, d) for v in (ln_gain, bn_gain, bn_bias))

    dy, table = unpack(lengths, owners, upstream, loaders)
    dy = swapped(dy.reshape(loaders, SPAN, d), BUCKET).reshape(rows, d)
    h, lin, sig, freq, conv, wf, stats = forward(table, frames, gain, w_in, w_dw, tabs)
    stats = lax.psum(lax.psum(stats, "c"), "y")
    stats, dy = lax.optimization_barrier((stats, dy))
    stats = swapped(jnp.broadcast_to(stats, (loaders, *stats.shape)), BUCKET)
    out, gbn, theirs, own, sums, stats = middle(total, table, conv, dy, stats, bn_gain, bn_bias, w_out)
    sums = to_everyone(sums)
    out = swapped(out.reshape(loaders, SPAN, d), BUCKET).reshape(rows, d)
    grad_a, theirs, own, bias_total, gain_total = backward(
        total, table, h, lin, sig, freq, conv, gbn, wf, stats, sums, bn_gain, theirs, own, tabs
    )
    every, out = sum_of_rows(theirs, own, loaders, out)
    gframes = inputs_back(table, frames, grad_a, gain, w_in)
    out_frames = pack(table, out, upstream.shape[0])
    gwin, gwout, gwdw, gln = finish(every, w_rows, gain_rows, taps)
    return (
        out_frames,
        gframes,
        gwin,
        gwout,
        gwdw,
        gln.reshape(share),
        gain_total.reshape(d),
        bias_total.reshape(d),
    )


def solution(mesh):
    torus = Mesh(mesh.devices.reshape(4, 2, 4, 8), ("y", "c", "x", "z"))
    in_specs = (P(EVERY, None), P(DP, None), P(DP, None), P(EVERY, None)) + (P(),) * 6
    out_specs = (P(EVERY, None), P(EVERY, None), P(BUCKET, None), P(BUCKET, None), P(BUCKET, None), P(BUCKET), P(), P())
    return jax.shard_map(local, mesh=torus, in_specs=in_specs, out_specs=out_specs, check_vma=False)
```

```python
import functools
import math

import jax
import jax.numpy as jnp
import numpy as np
from jax import lax
from jax.experimental import pallas as pl
from jax.experimental.pallas import tpu as pltpu
from jax.sharding import Mesh
from jax.sharding import PartitionSpec as P

BUCKET = ("x", "z")
DP = ("y", "c")
EVERY = ("y", "c", "x", "z")


EPSILON = 1e-05
SPAN = 48
BLOCK = 64
POINTS = 64
HALF = POINTS // 2
PER_DFT = 4
PER_STEP = 8
VMEM_LIMIT = 60 * 2**20

F32 = jnp.float32
BF16 = jnp.bfloat16


def dot(a, b, dims=((1,), (0,)), precision=None):
    return lax.dot_general(a, b, (dims, ((), ())), preferred_element_type=F32, precision=precision)


def tables(taps):
    f = np.arange(HALF)[:, None]
    t = np.arange(SPAN)[None, :]
    angle = 2 * np.pi * f * t / POINTS
    real = np.cos(angle) * math.sqrt(2 / POINTS)
    imag = -np.sin(angle) * math.sqrt(2 / POINTS)
    real[0] = math.sqrt(1 / POINTS)
    imag[0] = math.sqrt(1 / POINTS) * (-1.0) ** np.arange(SPAN)
    block = np.zeros((2 * HALF * PER_DFT, SPAN * PER_DFT))
    for u in range(PER_DFT):
        block[u * HALF : (u + 1) * HALF, u * SPAN : (u + 1) * SPAN] = real
        block[(PER_DFT + u) * HALF : (PER_DFT + u + 1) * HALF, u * SPAN : (u + 1) * SPAN] = imag
    lag = np.arange(taps)[None, :] - taps // 2
    turn = 2 * np.pi * f * lag / POINTS
    cos, sin = np.cos(turn), np.sin(turn)
    cos_last = cos.copy()
    cos_last[0] = np.cos(np.pi * lag[0])
    taps_to = np.concatenate([cos, sin, cos_last], axis=0)
    back = np.zeros((2 * HALF, 128))
    back[:HALF, :taps] = cos
    back[HALF : 2 * HALF, :taps] = -sin
    back[HALF, :taps] = np.cos(np.pi * lag[0])
    high = block.astype(jnp.bfloat16)
    low = (block - high.astype(np.float64)).astype(jnp.bfloat16)
    return (
        high,
        low,
        np.ascontiguousarray(high.T),
        np.ascontiguousarray(low.T),
        taps_to.astype(np.float32),
        back.astype(np.float32),
    )


def masked(value, lens):
    t = lax.broadcasted_iota(jnp.int32, (SPAN, value.shape[1]), 0)
    return jnp.concatenate(
        [
            jnp.where(t < n, value[u * SPAN : (u + 1) * SPAN], jnp.zeros((), value.dtype))
            for u, n in enumerate(lens)
        ],
        axis=0,
    )


def folded(value):
    return jnp.sum(value.reshape(-1, 8, value.shape[1]), axis=0)


def as_tile(first, second):
    rows = [v[:, k * 128 : (k + 1) * 128] for v in (first, second) for k in range(4)]
    return jnp.concatenate(rows, axis=0)


def from_tile(tile):
    rows = [tile[k : k + 1] for k in range(8)]
    return (jnp.concatenate(rows[:4], axis=1), jnp.concatenate(rows[4:], axis=1))


def normalize(x, gain):
    centred = x - jnp.mean(x, axis=1, keepdims=True)
    inverse = lax.rsqrt(jnp.mean(centred * centred, axis=1, keepdims=True) + EPSILON)
    normed = centred * inverse
    return (normed * gain).astype(BF16), normed, inverse


def spread(wf, part):
    rows = wf[part * HALF : (part + 1) * HALF]
    return jnp.concatenate([rows] * PER_DFT, axis=0)


def unpack_kernel(lengths_ref, owners_ref, upstream_ref, out_ref, table_ref, wide, lens_all, dest_all, table, sem):
    loaders = lens_all.shape[0]
    me = lax.axis_index(BUCKET)
    for k in range(loaders):
        lens_all[k : k + 1, :] = lengths_ref[:, k * loaders : (k + 1) * loaders]
        dest_all[k : k + 1, :] = owners_ref[:, k * loaders : (k + 1) * loaders]
    got = jnp.sum(jnp.where(dest_all[...] == me, lens_all[...], 0), axis=1, keepdims=True)
    square = (loaders, loaders)
    hit = dest_all[pl.ds(me, 1), :] == lax.broadcasted_iota(jnp.int32, square, 0)
    lens = jnp.sum(jnp.where(hit, lens_all[pl.ds(me, 1), :], 0), axis=1, keepdims=True)
    slots = jnp.sum(jnp.where(hit, lax.broadcasted_iota(jnp.int32, square, 1), 0), axis=1, keepdims=True)
    column = lax.broadcasted_iota(jnp.int32, table_ref.shape, 1)
    table_ref[...] = jnp.where(column == 0, got, jnp.where(column == 1, lens, slots))
    copy = pltpu.make_async_copy(table_ref, table, sem)
    copy.start()
    rows = upstream_ref.shape[0]
    wide[:rows, :] = upstream_ref[...].astype(F32)
    wide[rows:, :] = jnp.zeros((8, wide.shape[1]), F32)
    copy.wait()

    def step(i, start):
        base = pl.multiple_of(start // 8 * 8, 8)
        window = pltpu.roll(wide[pl.ds(base, SPAN + 8), :], SPAN + 8 - start % 8, 0)
        out_ref[pl.ds(pl.multiple_of(i * SPAN, 16), SPAN), :] = window[:SPAN].astype(BF16)
        return start + table[i, 0]

    lax.fori_loop(0, loaders, step, jnp.int32(0))


def pack_kernel(table_ref, got_ref, out_ref, gwout_ref, wide):
    count = got_ref.shape[0] // BLOCK
    share = gwout_ref.shape[0]
    top = lax.broadcasted_iota(jnp.int32, (8, got_ref.shape[1]), 0)

    def step(i, start):
        base = pl.multiple_of(start // 8 * 8, 8)
        rows = got_ref[pl.ds(pl.multiple_of(i * BLOCK, 16), SPAN), :].astype(F32)
        window = jnp.concatenate([rows, jnp.zeros((8, rows.shape[1]), F32)], axis=0)
        window = pltpu.roll(window, start % 8, 0)
        kept = jnp.where(top < start % 8, wide[pl.ds(base, 8), :], window[:8])
        wide[pl.ds(base, 8), :] = kept
        wide[pl.ds(base + 8, SPAN), :] = window[8:]
        return start + table_ref[i, 0]

    lax.fori_loop(0, count, step, jnp.int32(0))
    out_ref[...] = wide[: out_ref.shape[0], :].astype(BF16)
    parts = [got_ref[k * BLOCK + SPAN : k * BLOCK + SPAN + share, :].astype(F32) for k in range(count)]
    gwout_ref[...] = sum(parts).astype(BF16)


def step_lens(table_ref):
    return [table_ref[pl.program_id(0) * PER_STEP + u, 1] for u in range(PER_STEP)]


def slot_rows(table_ref, u):
    slot = table_ref[pl.program_id(0) * PER_STEP + u, 2]
    return pl.ds(pl.multiple_of(slot * SPAN, 16), SPAN)


def forward_kernel(
    table_ref, frames_ref, gain_ref, win_ref, qh_ref, ql_ref, ih_ref, il_ref, to_ref, wdw_ref,
    h_ref, lin_ref, sig_ref, freq_ref, conv_ref, wf_ref, stats_ref, acc,
):
    step = pl.program_id(0)

    @pl.when(step == 0)
    def _():
        wf_ref[...] = dot(to_ref[...], wdw_ref[...], ((1,), (1,)), lax.Precision.HIGHEST)
        acc[...] = jnp.zeros_like(acc)

    d = frames_ref.shape[1]
    lens = step_lens(table_ref)
    x = jnp.concatenate([frames_ref[slot_rows(table_ref, u), :] for u in range(PER_STEP)], axis=0)
    h, _, _ = normalize(x.astype(F32), gain_ref[...])
    h_ref[...] = h
    a = dot(h, win_ref[...])
    lin = a[:, :d]
    sig = jax.nn.sigmoid(a[:, d:])
    lin_ref[...] = lin.astype(BF16)
    sig_ref[...] = sig.astype(BF16)
    gated = masked(lin * sig, lens).astype(BF16)
    wa, wb, wl = (spread(wf_ref[...], k) for k in range(3))
    for b in range(PER_STEP // PER_DFT):
        rows = slice(b * SPAN * PER_DFT, (b + 1) * SPAN * PER_DFT)
        part = gated[rows]
        spec = dot(qh_ref[...], part) + dot(ql_ref[...], part)
        freq_ref[b * POINTS * PER_DFT : (b + 1) * POINTS * PER_DFT, :] = spec.astype(BF16)
        re, im = spec[: HALF * PER_DFT], spec[HALF * PER_DFT :]
        turned = jnp.concatenate([re * wa - im * wb, im * wl + re * wb], axis=0)
        high = turned.astype(BF16)
        low = (turned - high.astype(F32)).astype(BF16)
        conv = dot(ih_ref[...], high) + dot(il_ref[...], high) + dot(ih_ref[...], low)
        conv_ref[rows, :] = conv
        live = masked(conv, lens[b * PER_DFT : (b + 1) * PER_DFT])
        acc[0] += folded(live)
        acc[1] += folded(live * live)

    @pl.when(step == pl.num_programs(0) - 1)
    def _():
        sums = [jnp.sum(acc[k], axis=0, keepdims=True) for k in range(2)]
        stats_ref[...] = as_tile(*sums)


def split(value, theirs_ref, own_ref):
    blocks = value.reshape(-1, 2, 8, value.shape[1])
    first = lax.axis_index("c") == 0
    low, high = blocks[:, 0], blocks[:, 1]
    theirs_ref[...] = jnp.where(first, high, low).reshape(theirs_ref.shape).astype(BF16)
    own_ref[...] = jnp.where(first, low, high).reshape(own_ref.shape).astype(BF16)


def bn_terms(stats, total):
    first, second = from_tile(stats)
    centre = first / total
    inverse = lax.rsqrt(second / total - centre * centre + EPSILON)
    return centre, inverse


def middle_kernel(
    total, table_ref, conv_ref, dy_ref, stats_ref, gain_ref, bias_ref, wout_ref,
    out_ref, gbn_ref, sums_ref, moments_ref, acc, sw_all, dy_all,
):
    step = pl.program_id(0)

    @pl.when(step == 0)
    def _():
        acc[...] = jnp.zeros_like(acc)
        moments_ref[...] = jnp.sum(stats_ref[...], axis=0)

    centre, inverse = bn_terms(moments_ref[...], total)
    normed = (conv_ref[...] - centre) * inverse
    value = normed * gain_ref[...] + bias_ref[...]
    sig = jax.nn.sigmoid(value)
    swished = (value * sig).astype(BF16)
    out = dot(swished, wout_ref[...]).astype(BF16)
    for u in range(PER_STEP):
        slot = pl.multiple_of((step * PER_STEP + u) * BLOCK, BLOCK)
        out_ref[pl.ds(slot, SPAN), :] = out[u * SPAN : (u + 1) * SPAN]
    dy = masked(dy_ref[...].astype(F32), step_lens(table_ref)).astype(BF16)
    rows = pl.ds(pl.multiple_of(step * PER_STEP * SPAN, 16), PER_STEP * SPAN)
    sw_all[rows, :] = swished
    dy_all[rows, :] = dy
    grad = dot(dy, wout_ref[...], ((1,), (1,))) * (sig * (1.0 + value * (1.0 - sig)))
    gbn_ref[...] = grad
    acc[0] += folded(grad)
    acc[1] += folded(grad * normed)

    @pl.when(step == pl.num_programs(0) - 1)
    def _():
        sums = [jnp.sum(acc[k], axis=0, keepdims=True) for k in range(2)]
        sums_ref[...] = as_tile(*sums)
        gwout = dot(sw_all[...], dy_all[...], ((0,), (0,))).astype(BF16)
        count = out_ref.shape[0] // BLOCK
        share = gwout.shape[0] // count
        for k in range(count):
            out_ref[k * BLOCK + SPAN : k * BLOCK + SPAN + share, :] = gwout[k * share : (k + 1) * share]


def backward_kernel(
    total, table_ref, h_ref, lin_ref, sig_ref, freq_ref, conv_ref, gbn_ref, wf_ref, stats_ref, sums_ref,
    bn_gain_ref, qh_ref, ih_ref, back_ref,
    grad_a_ref, theirs_ref, own_ref, bias_ref, bn_out_ref, acc, h_all, ga_all,
):
    step = pl.program_id(0)

    @pl.when(step == 0)
    def _():
        acc[...] = jnp.zeros_like(acc)

    lens = step_lens(table_ref)
    centre, inverse = bn_terms(stats_ref[...], total)
    bias_total, gain_total = from_tile(sums_ref[...])
    bias_ref[...] = bias_total
    bn_out_ref[...] = gain_total
    normed_bn = (conv_ref[...] - centre) * inverse
    scale = bn_gain_ref[...] * inverse
    grad_conv = scale * (gbn_ref[...] - bias_total / total - normed_bn * (gain_total / total))
    grad_conv = masked(grad_conv, lens).astype(BF16)
    wa, wb, wl = (spread(wf_ref[...], k) for k in range(3))
    n = HALF * PER_DFT
    edge = lax.broadcasted_iota(jnp.int32, (n, wa.shape[1]), 0) % HALF == 0
    parts = []
    for b in range(PER_STEP // PER_DFT):
        rows = slice(b * SPAN * PER_DFT, (b + 1) * SPAN * PER_DFT)
        spec = dot(qh_ref[...], grad_conv[rows])
        re, im = spec[:n], spec[n:]
        own = freq_ref[b * 2 * n : (b + 1) * 2 * n, :].astype(F32)
        own_re, own_im = own[:n], own[n:]
        both = im * own_im
        corr_re = re * own_re + jnp.where(edge, 0.0, both)
        corr_im = jnp.where(edge, both, re * own_im - im * own_re)
        acc[:HALF] += jnp.sum(corr_re.reshape(PER_DFT, HALF, -1), axis=0)
        acc[HALF:] += jnp.sum(corr_im.reshape(PER_DFT, HALF, -1), axis=0)
        turned = jnp.concatenate([re * wa + im * wb, im * wl - re * wb], axis=0).astype(BF16)
        parts.append(dot(ih_ref[...], turned))
    grad_gated = masked(jnp.concatenate(parts, axis=0), lens)
    lin = lin_ref[...].astype(F32)
    sig = sig_ref[...].astype(F32)
    first = grad_gated * sig
    grad_a = jnp.concatenate([first, first * lin * (1.0 - sig)], axis=1).astype(BF16)
    grad_a_ref[...] = grad_a
    rows = pl.ds(pl.multiple_of(step * PER_STEP * SPAN, 16), PER_STEP * SPAN)
    h_all[rows, :] = h_ref[...]
    ga_all[rows, :] = grad_a

    @pl.when(step == pl.num_programs(0) - 1)
    def _():
        d = h_all.shape[1]
        gwin, taps = slice(0, 2 * d), slice(2 * d, theirs_ref.shape[1])
        small = dot(acc[...], back_ref[...], ((0,), (0,)), lax.Precision.HIGHEST)
        split(small, theirs_ref.at[:, taps], own_ref.at[:, taps])
        split(dot(h_all[...], ga_all[...], ((0,), (0,))), theirs_ref.at[:, gwin], own_ref.at[:, gwin])


def inputs_kernel(table_ref, frames_ref, grad_a_ref, gain_ref, win_ref, gframes_ref):
    grad_h = dot(grad_a_ref[...], win_ref[...], ((1,), (1,)))
    x = jnp.concatenate([frames_ref[slot_rows(table_ref, u), :] for u in range(PER_STEP)], axis=0)
    gain = gain_ref[...]
    _, normed, inv = normalize(x.astype(F32), gain)
    scaled = grad_h * gain
    inner = jnp.mean(scaled * normed, axis=1, keepdims=True)
    grad_x = inv * (scaled - jnp.mean(scaled, axis=1, keepdims=True) - normed * inner)
    grad_x = masked(grad_x, step_lens(table_ref)).astype(BF16)
    for u in range(PER_STEP):
        gframes_ref[slot_rows(table_ref, u), :] = grad_x[u * SPAN : (u + 1) * SPAN]


def collect_kernel(got_ref, gwout_ref, out_ref):
    total = got_ref[0].astype(F32)
    for k in range(1, got_ref.shape[0]):
        total += got_ref[k].astype(F32)
    high, low = gwout_ref[:8].astype(F32), gwout_ref[8:].astype(F32)
    rows = jnp.concatenate([total, high, low], axis=1).astype(BF16)
    for k in range(out_ref.shape[0]):
        out_ref[k] = rows


def finish_kernel(every_ref, w_ref, gain_ref, gwin_ref, gwout_ref, gwdw_ref, gln_ref):
    count = every_ref.shape[0]
    d = gwout_ref.shape[1]
    width = 2 * d + 128
    halves = [sum(every_ref[k, :, :width].astype(F32) for k in range(core, count, 2)) for core in range(2)]
    rows = jnp.concatenate(halves, axis=0)
    gwin = rows[:, : 2 * d]
    gwin_ref[...] = gwin
    gwdw_ref[...] = rows[:, 2 * d : 2 * d + gwdw_ref.shape[1]]
    out = sum(every_ref[k, :, width:].astype(F32) for k in range(count))
    gwout_ref[...] = jnp.concatenate([out[:, :d], out[:, d:]], axis=0)
    ones = jnp.ones((8, 2 * d), F32)
    dots = dot(ones, gwin * w_ref[...].astype(F32), ((1,), (1,)), lax.Precision.HIGHEST)
    gln_ref[...] = dots[:1] / gain_ref[...]


SMEM = pl.BlockSpec(memory_space=pltpu.SMEM)


def whole(shape):
    return pl.BlockSpec(shape, lambda i: (0,) * len(shape))


def rows_of(shape, steps):
    return pl.BlockSpec((shape[0] // steps, shape[1]), lambda i: (i, 0))


def cost(flops, moved):
    return pl.CostEstimate(flops=int(flops), bytes_accessed=int(moved), transcendentals=0)


def params():
    return pltpu.CompilerParams(dimension_semantics=("arbitrary",), vmem_limit_bytes=VMEM_LIMIT)


def sds(shape, dtype):
    return jax.ShapeDtypeStruct(shape, dtype)


def unpack(lengths, owners, upstream, loaders):
    rows, d = upstream.shape
    vmem = pl.BlockSpec(memory_space=pltpu.VMEM)
    return pl.pallas_call(
        unpack_kernel,
        out_shape=(sds((loaders * SPAN, d), BF16), sds((loaders, 128), jnp.int32)),
        in_specs=[vmem] * 3,
        out_specs=(vmem, vmem),
        scratch_shapes=[
            pltpu.VMEM((rows + 8, d), F32),
            pltpu.VMEM((loaders, loaders), jnp.int32),
            pltpu.VMEM((loaders, loaders), jnp.int32),
            pltpu.SMEM((loaders, 128), jnp.int32),
            pltpu.SemaphoreType.DMA,
        ],
        compiler_params=pltpu.CompilerParams(vmem_limit_bytes=VMEM_LIMIT),
        name="unpack",
        cost_estimate=cost(1e9, 6 * rows * d),
    )(lengths, owners, upstream)


def pack(table, got, rows):
    d = got.shape[1]
    share = d * BLOCK // got.shape[0]
    vmem = pl.BlockSpec(memory_space=pltpu.VMEM)
    return pl.pallas_call(
        pack_kernel,
        out_shape=(sds((rows, d), BF16), sds((share, d), BF16)),
        in_specs=[SMEM, vmem],
        out_specs=(vmem, vmem),
        scratch_shapes=[pltpu.VMEM((rows + 8, d), F32)],
        compiler_params=pltpu.CompilerParams(vmem_limit_bytes=VMEM_LIMIT),
        name="pack",
        cost_estimate=cost(2e9, 6 * rows * d),
    )(table, got)


def forward(table, frames, gain, w_in, w_dw, tabs):
    high, low, high_t, low_t, taps_to, _ = tabs
    rows, d = frames.shape
    steps = rows // (SPAN * PER_STEP)
    freq = (rows // SPAN * POINTS, d)
    return pl.pallas_call(
        forward_kernel,
        grid=(steps,),
        out_shape=(
            sds((rows, d), BF16),
            sds((rows, d), BF16),
            sds((rows, d), BF16),
            sds(freq, BF16),
            sds((rows, d), F32),
            sds((3 * HALF, d), F32),
            sds((8, 128), F32),
        ),
        in_specs=[SMEM, whole(frames.shape), whole(gain.shape), whole(w_in.shape)]
        + [whole(v.shape) for v in (high, low, high_t, low_t, taps_to, w_dw)],
        out_specs=(
            rows_of((rows, d), steps),
            rows_of((rows, d), steps),
            rows_of((rows, d), steps),
            rows_of(freq, steps),
            rows_of((rows, d), steps),
            whole((3 * HALF, d)),
            whole((8, 128)),
        ),
        scratch_shapes=[pltpu.VMEM((2, 8, d), F32)],
        compiler_params=params(),
        name="forward",
        cost_estimate=cost(10e9, 16 * rows * d),
    )(table, frames, gain, w_in, high, low, high_t, low_t, taps_to, w_dw)


def middle(total, table, conv, dy, stats, bn_gain, bn_bias, w_out):
    rows, d = conv.shape
    steps = rows // (SPAN * PER_STEP)
    part = rows_of((rows, d), steps)
    return pl.pallas_call(
        functools.partial(middle_kernel, total),
        grid=(steps,),
        out_shape=(
            sds((rows // SPAN * BLOCK, d), BF16),
            sds((rows, d), F32),
            sds((8, 128), F32),
            sds((8, 128), F32),
        ),
        in_specs=[SMEM, part, part] + [whole(v.shape) for v in (stats, bn_gain, bn_bias, w_out)],
        out_specs=(whole((rows // SPAN * BLOCK, d)), part, whole((8, 128)), whole((8, 128))),
        scratch_shapes=[pltpu.VMEM((2, 8, d), F32), pltpu.VMEM((rows, d), BF16), pltpu.VMEM((rows, d), BF16)],
        compiler_params=params(),
        name="middle",
        cost_estimate=cost(5e9, 12 * rows * d),
    )(table, conv, dy, stats, bn_gain, bn_bias, w_out)


def backward(total, table, h, lin, sig, freq, conv, gbn, wf, stats, sums, bn_gain, tabs):
    high, _, high_t, _, _, back = tabs
    rows, d = h.shape
    width = 2 * d + back.shape[1]
    steps = rows // (SPAN * PER_STEP)
    part = rows_of((rows, d), steps)
    return pl.pallas_call(
        functools.partial(backward_kernel, total),
        grid=(steps,),
        out_shape=(
            sds((rows, 2 * d), BF16),
            sds((d // 2, width), BF16),
            sds((d // 2, width), BF16),
            sds((1, d), F32),
            sds((1, d), F32),
        ),
        in_specs=[SMEM, part, part, part, rows_of(freq.shape, steps), part, part]
        + [whole(v.shape) for v in (wf, stats, sums, bn_gain, high, high_t, back)],
        out_specs=(
            rows_of((rows, 2 * d), steps),
            whole((d // 2, width)),
            whole((d // 2, width)),
            whole((1, d)),
            whole((1, d)),
        ),
        scratch_shapes=[
            pltpu.VMEM((2 * HALF, d), F32),
            pltpu.VMEM((rows, d), BF16),
            pltpu.VMEM((rows, 2 * d), BF16),
        ],
        compiler_params=params(),
        name="backward",
        cost_estimate=cost(8e9, 18 * rows * d),
    )(table, h, lin, sig, freq, conv, gbn, wf, stats, sums, bn_gain, high, high_t, back)


def inputs_back(table, frames, grad_a, gain, w_in):
    rows, d = frames.shape
    steps = rows // (SPAN * PER_STEP)
    return pl.pallas_call(
        inputs_kernel,
        grid=(steps,),
        out_shape=sds((rows, d), BF16),
        in_specs=[SMEM, whole(frames.shape), rows_of(grad_a.shape, steps), whole(gain.shape), whole(w_in.shape)],
        out_specs=whole((rows, d)),
        compiler_params=params(),
        name="inputs_back",
        cost_estimate=cost(6e9, 12 * rows * d),
    )(table, frames, grad_a, gain, w_in)


def collect(got, gwout, count):
    _, share, width = got.shape
    vmem = pl.BlockSpec(memory_space=pltpu.VMEM)
    return pl.pallas_call(
        collect_kernel,
        out_shape=sds((count, share, width + 2 * gwout.shape[1]), BF16),
        in_specs=[vmem] * 2,
        out_specs=vmem,
        compiler_params=pltpu.CompilerParams(vmem_limit_bytes=VMEM_LIMIT),
        name="collect",
    )(got, gwout)


def finish(every, w_rows, gain_rows, taps):
    share, width = w_rows.shape
    d = width // 2
    vmem = pl.BlockSpec(memory_space=pltpu.VMEM)
    return pl.pallas_call(
        finish_kernel,
        out_shape=(sds((share, width), F32), sds((share, d), F32), sds((share, taps), F32), sds((1, share), F32)),
        in_specs=[vmem] * 3,
        out_specs=(vmem,) * 4,
        compiler_params=pltpu.CompilerParams(vmem_limit_bytes=VMEM_LIMIT),
        name="finish",
    )(every, w_rows, gain_rows)


def swapped(value, axes):
    return lax.all_to_all(value, axes, split_axis=0, concat_axis=0, tiled=True)


def to_everyone(tile):
    return functools.reduce(lax.psum, ("c", "y", "x", "z"), tile)


def over_bucket(theirs, own, loaders, ahead):
    got = lax.ppermute(theirs, "c", [(0, 1), (1, 0)])
    both = (own.astype(F32) + got.astype(F32)).astype(BF16).reshape(loaders, -1, own.shape[1])
    both, ahead = lax.optimization_barrier((both, ahead))
    return swapped(both, BUCKET), ahead


def local(frames, lengths, owners, upstream, ln_gain, w_in, w_dw, bn_gain, bn_bias, w_out):
    loaders = lax.axis_size(BUCKET)
    me = lax.axis_index(BUCKET)
    rows, d = frames.shape
    taps = w_dw.shape[1]
    share = d // loaders
    total = float(upstream.shape[0] * loaders * lax.axis_size(DP))
    tabs = tuple(jnp.asarray(v) for v in tables(taps))
    w_rows = lax.dynamic_slice_in_dim(w_in, me * share, share, 0)
    gain_rows = lax.dynamic_slice_in_dim(ln_gain, me * share, share, 0).reshape(1, share)
    gain, bn_gain, bn_bias = (v.reshape(1, d) for v in (ln_gain, bn_gain, bn_bias))

    dy, table = unpack(lengths, owners, upstream, loaders)
    dy = swapped(dy.reshape(loaders, SPAN, d), BUCKET).reshape(rows, d)
    h, lin, sig, freq, conv, wf, stats = forward(table, frames, gain, w_in, w_dw, tabs)
    stats = lax.psum(lax.psum(lax.psum(stats, "c"), "y"), "x")
    stats, dy = lax.optimization_barrier((stats, dy))
    stats = swapped(jnp.broadcast_to(stats, (lax.axis_size("z"), *stats.shape)), "z")
    out, gbn, sums, stats = middle(total, table, conv, dy, stats, bn_gain, bn_bias, w_out)
    sums = to_everyone(sums)
    out = swapped(out.reshape(loaders, BLOCK, d), BUCKET).reshape(loaders * BLOCK, d)
    grad_a, theirs, own, bias_total, gain_total = backward(
        total, table, h, lin, sig, freq, conv, gbn, wf, stats, sums, bn_gain, tabs
    )
    got, out = over_bucket(theirs, own, loaders, out)
    gframes = inputs_back(table, frames, grad_a, gain, w_in)
    out_frames, gwout = pack(table, out, upstream.shape[0])
    gwout, gframes = lax.optimization_barrier((gwout, gframes))
    every = swapped(collect(got, gwout, lax.axis_size(DP)), DP)
    gwin, gwout, gwdw, gln = finish(every, w_rows, gain_rows, taps)
    return (
        out_frames,
        gframes,
        gwin,
        gwout,
        gwdw,
        gln.reshape(share),
        gain_total.reshape(d),
        bias_total.reshape(d),
    )


def solution(mesh):
    torus = Mesh(mesh.devices.reshape(4, 2, 4, 8), ("y", "c", "x", "z"))
    in_specs = (P(EVERY, None), P(DP, None), P(DP, None), P(EVERY, None)) + (P(),) * 6
    out_specs = (P(EVERY, None), P(EVERY, None), P(BUCKET, None), P(BUCKET, None), P(BUCKET, None), P(BUCKET), P(), P())
    return jax.shard_map(local, mesh=torus, in_specs=in_specs, out_specs=out_specs, check_vma=False)
```

```python
import functools
import math

import jax
import jax.numpy as jnp
import numpy as np
from jax import lax
from jax.experimental import pallas as pl
from jax.experimental.pallas import tpu as pltpu
from jax.sharding import Mesh
from jax.sharding import PartitionSpec as P

BUCKET = ("x", "z")
DP = ("y", "c")
EVERY = ("y", "c", "x", "z")


EPSILON = 1e-05
SPAN = 48
POINTS = 64
HALF = POINTS // 2
PER_DFT = 4
PER_STEP = 8
VMEM_LIMIT = 60 * 2**20
SMALL_LIMIT = 16 * 2**20

F32 = jnp.float32
BF16 = jnp.bfloat16


def dot(a, b, dims=((1,), (0,)), precision=None):
    return lax.dot_general(a, b, (dims, ((), ())), preferred_element_type=F32, precision=precision)


def tables(taps):
    f = np.arange(HALF)[:, None]
    t = np.arange(SPAN)[None, :]
    angle = 2 * np.pi * f * t / POINTS
    real = np.cos(angle) * math.sqrt(2 / POINTS)
    imag = -np.sin(angle) * math.sqrt(2 / POINTS)
    real[0] = math.sqrt(1 / POINTS)
    imag[0] = math.sqrt(1 / POINTS) * (-1.0) ** np.arange(SPAN)
    block = np.zeros((2 * HALF * PER_DFT, SPAN * PER_DFT))
    for u in range(PER_DFT):
        block[u * HALF : (u + 1) * HALF, u * SPAN : (u + 1) * SPAN] = real
        block[(PER_DFT + u) * HALF : (PER_DFT + u + 1) * HALF, u * SPAN : (u + 1) * SPAN] = imag
    lag = np.arange(taps)[None, :] - taps // 2
    turn = 2 * np.pi * f * lag / POINTS
    cos, sin = np.cos(turn), np.sin(turn)
    cos_last = cos.copy()
    cos_last[0] = np.cos(np.pi * lag[0])
    taps_to = np.concatenate([cos, sin, cos_last], axis=0)
    back = np.zeros((2 * HALF, 128))
    back[:HALF, :taps] = cos
    back[HALF : 2 * HALF, :taps] = -sin
    back[HALF, :taps] = np.cos(np.pi * lag[0])
    high = block.astype(jnp.bfloat16)
    low = (block - high.astype(np.float64)).astype(jnp.bfloat16)
    return (
        high,
        low,
        np.ascontiguousarray(high.T),
        np.ascontiguousarray(low.T),
        taps_to.astype(np.float32),
        back.astype(np.float32),
    )


def masked(value, lens):
    t = lax.broadcasted_iota(jnp.int32, (SPAN, value.shape[1]), 0)
    return jnp.concatenate(
        [
            jnp.where(t < n, value[u * SPAN : (u + 1) * SPAN], jnp.zeros((), value.dtype))
            for u, n in enumerate(lens)
        ],
        axis=0,
    )


def folded(value):
    return jnp.sum(value.reshape(-1, 8, value.shape[1]), axis=0)


def as_tile(first, second):
    rows = [v[:, k * 128 : (k + 1) * 128] for v in (first, second) for k in range(4)]
    return jnp.concatenate(rows, axis=0)


def from_tile(tile):
    rows = [tile[k : k + 1] for k in range(8)]
    return (jnp.concatenate(rows[:4], axis=1), jnp.concatenate(rows[4:], axis=1))


def normalize(x, gain):
    centred = x - jnp.mean(x, axis=1, keepdims=True)
    inverse = lax.rsqrt(jnp.mean(centred * centred, axis=1, keepdims=True) + EPSILON)
    normed = centred * inverse
    return (normed * gain).astype(BF16), normed, inverse


def spread(wf, part):
    rows = wf[part * HALF : (part + 1) * HALF]
    return jnp.concatenate([rows] * PER_DFT, axis=0)


def unpack_kernel(lengths_ref, owners_ref, upstream_ref, out_ref, table_ref, wide, lens_all, dest_all, table, sem):
    loaders = lens_all.shape[0]
    me = lax.axis_index(BUCKET)
    for k in range(loaders):
        lens_all[k : k + 1, :] = lengths_ref[:, k * loaders : (k + 1) * loaders]
        dest_all[k : k + 1, :] = owners_ref[:, k * loaders : (k + 1) * loaders]
    got = jnp.sum(jnp.where(dest_all[...] == me, lens_all[...], 0), axis=1, keepdims=True)
    square = (loaders, loaders)
    hit = dest_all[pl.ds(me, 1), :] == lax.broadcasted_iota(jnp.int32, square, 0)
    lens = jnp.sum(jnp.where(hit, lens_all[pl.ds(me, 1), :], 0), axis=1, keepdims=True)
    slots = jnp.sum(jnp.where(hit, lax.broadcasted_iota(jnp.int32, square, 1), 0), axis=1, keepdims=True)
    column = lax.broadcasted_iota(jnp.int32, table_ref.shape, 1)
    table_ref[...] = jnp.where(column == 0, got, jnp.where(column == 1, lens, slots))
    copy = pltpu.make_async_copy(table_ref, table, sem)
    copy.start()
    rows = upstream_ref.shape[0]
    wide[:rows, :] = upstream_ref[...].astype(F32)
    wide[rows:, :] = jnp.zeros((8, wide.shape[1]), F32)
    copy.wait()

    def step(i, start):
        base = pl.multiple_of(start // 8 * 8, 8)
        window = pltpu.roll(wide[pl.ds(base, SPAN + 8), :], SPAN + 8 - start % 8, 0)
        out_ref[pl.ds(pl.multiple_of(i * SPAN, 16), SPAN), :] = window[:SPAN].astype(BF16)
        return start + table[i, 0]

    lax.fori_loop(0, loaders, step, jnp.int32(0))


def pack_kernel(table_ref, got_ref, out_ref, wide):
    count = got_ref.shape[0] // SPAN
    top = lax.broadcasted_iota(jnp.int32, (8, got_ref.shape[1]), 0)

    def step(i, start):
        base = pl.multiple_of(start // 8 * 8, 8)
        rows = got_ref[pl.ds(pl.multiple_of(i * SPAN, 16), SPAN), :].astype(F32)
        window = jnp.concatenate([rows, jnp.zeros((8, rows.shape[1]), F32)], axis=0)
        window = pltpu.roll(window, start % 8, 0)
        kept = jnp.where(top < start % 8, wide[pl.ds(base, 8), :], window[:8])
        wide[pl.ds(base, 8), :] = kept
        wide[pl.ds(base + 8, SPAN), :] = window[8:]
        return start + table_ref[i, 0]

    lax.fori_loop(0, count, step, jnp.int32(0))
    out_ref[...] = wide[: out_ref.shape[0], :].astype(BF16)


def step_lens(table_ref):
    return [table_ref[pl.program_id(0) * PER_STEP + u, 1] for u in range(PER_STEP)]


def slot_rows(table_ref, u):
    slot = table_ref[pl.program_id(0) * PER_STEP + u, 2]
    return pl.ds(pl.multiple_of(slot * SPAN, 16), SPAN)


def forward_kernel(
    table_ref, frames_ref, gain_ref, win_ref, qh_ref, ql_ref, ih_ref, il_ref, to_ref, wdw_ref,
    h_ref, lin_ref, sig_ref, freq_ref, conv_ref, wf_ref, stats_ref, acc,
):
    step = pl.program_id(0)

    @pl.when(step == 0)
    def _():
        wf_ref[...] = dot(to_ref[...], wdw_ref[...], ((1,), (1,)), lax.Precision.HIGHEST)
        acc[...] = jnp.zeros_like(acc)

    d = frames_ref.shape[1]
    lens = step_lens(table_ref)
    x = jnp.concatenate([frames_ref[slot_rows(table_ref, u), :] for u in range(PER_STEP)], axis=0)
    h, _, _ = normalize(x.astype(F32), gain_ref[...])
    h_ref[...] = h
    a = dot(h, win_ref[...])
    lin = a[:, :d]
    sig = jax.nn.sigmoid(a[:, d:])
    lin_ref[...] = lin.astype(BF16)
    sig_ref[...] = sig.astype(BF16)
    gated = masked(lin * sig, lens).astype(BF16)
    wa, wb, wl = (spread(wf_ref[...], k) for k in range(3))
    for b in range(PER_STEP // PER_DFT):
        rows = slice(b * SPAN * PER_DFT, (b + 1) * SPAN * PER_DFT)
        part = gated[rows]
        spec = dot(qh_ref[...], part) + dot(ql_ref[...], part)
        freq_ref[b * POINTS * PER_DFT : (b + 1) * POINTS * PER_DFT, :] = spec.astype(BF16)
        re, im = spec[: HALF * PER_DFT], spec[HALF * PER_DFT :]
        turned = jnp.concatenate([re * wa - im * wb, im * wl + re * wb], axis=0)
        high = turned.astype(BF16)
        low = (turned - high.astype(F32)).astype(BF16)
        conv = dot(ih_ref[...], high) + dot(il_ref[...], high) + dot(ih_ref[...], low)
        conv_ref[rows, :] = conv
        live = masked(conv, lens[b * PER_DFT : (b + 1) * PER_DFT])
        acc[0] += folded(live)
        acc[1] += folded(live * live)

    @pl.when(step == pl.num_programs(0) - 1)
    def _():
        sums = [jnp.sum(acc[k], axis=0, keepdims=True) for k in range(2)]
        stats_ref[...] = as_tile(*sums)


def split(value, theirs_ref, own_ref):
    blocks = value.reshape(-1, 2, 8, value.shape[1])
    first = lax.axis_index("c") == 0
    low, high = blocks[:, 0], blocks[:, 1]
    theirs_ref[...] = jnp.where(first, high, low).reshape(theirs_ref.shape).astype(BF16)
    own_ref[...] = jnp.where(first, low, high).reshape(own_ref.shape).astype(BF16)


def bn_terms(stats, total):
    first, second = from_tile(stats)
    centre = first / total
    inverse = lax.rsqrt(second / total - centre * centre + EPSILON)
    return centre, inverse


def middle_kernel(
    total, table_ref, conv_ref, dy_ref, stats_ref, gain_ref, bias_ref, wout_ref,
    swished_ref, live_dy_ref, gbn_ref, sums_ref, moments_ref, acc,
):
    step = pl.program_id(0)

    @pl.when(step == 0)
    def _():
        acc[...] = jnp.zeros_like(acc)
        moments_ref[...] = jnp.sum(stats_ref[...], axis=0)

    centre, inverse = bn_terms(moments_ref[...], total)
    normed = (conv_ref[...] - centre) * inverse
    value = normed * gain_ref[...] + bias_ref[...]
    sig = jax.nn.sigmoid(value)
    swished_ref[...] = (value * sig).astype(BF16)
    dy = masked(dy_ref[...].astype(F32), step_lens(table_ref)).astype(BF16)
    live_dy_ref[...] = dy
    grad = dot(dy, wout_ref[...], ((1,), (1,))) * (sig * (1.0 + value * (1.0 - sig)))
    gbn_ref[...] = grad
    acc[0] += folded(grad)
    acc[1] += folded(grad * normed)

    @pl.when(step == pl.num_programs(0) - 1)
    def _():
        sums = [jnp.sum(acc[k], axis=0, keepdims=True) for k in range(2)]
        sums_ref[...] = jnp.broadcast_to(as_tile(*sums)[None], sums_ref.shape)


def output_kernel(swished_ref, dy_ref, wout_ref, out_ref, theirs_ref, own_ref, sw_all, dy_all):
    step = pl.program_id(0)
    out_ref[...] = dot(swished_ref[...], wout_ref[...]).astype(BF16)
    rows = pl.ds(pl.multiple_of(step * PER_STEP * SPAN, 16), PER_STEP * SPAN)
    sw_all[rows, :] = swished_ref[...]
    dy_all[rows, :] = dy_ref[...]

    @pl.when(step == pl.num_programs(0) - 1)
    def _():
        split(dot(sw_all[...], dy_all[...], ((0,), (0,))), theirs_ref, own_ref)


def backward_kernel(
    total, table_ref, h_ref, lin_ref, sig_ref, freq_ref, conv_ref, gbn_ref, wf_ref, stats_ref, sums_ref,
    bn_gain_ref, theirs_in, own_in, qh_ref, ih_ref, back_ref,
    grad_a_ref, theirs_ref, own_ref, bias_ref, bn_out_ref, acc, h_all, ga_all,
):
    step = pl.program_id(0)

    @pl.when(step == 0)
    def _():
        acc[...] = jnp.zeros_like(acc)

    lens = step_lens(table_ref)
    centre, inverse = bn_terms(stats_ref[...], total)
    bias_total, gain_total = from_tile(sums_ref[...])
    bias_ref[...] = bias_total
    bn_out_ref[...] = gain_total
    normed_bn = (conv_ref[...] - centre) * inverse
    scale = bn_gain_ref[...] * inverse
    grad_conv = scale * (gbn_ref[...] - bias_total / total - normed_bn * (gain_total / total))
    grad_conv = masked(grad_conv, lens).astype(BF16)
    wa, wb, wl = (spread(wf_ref[...], k) for k in range(3))
    n = HALF * PER_DFT
    edge = lax.broadcasted_iota(jnp.int32, (n, wa.shape[1]), 0) % HALF == 0
    parts = []
    for b in range(PER_STEP // PER_DFT):
        rows = slice(b * SPAN * PER_DFT, (b + 1) * SPAN * PER_DFT)
        spec = dot(qh_ref[...], grad_conv[rows])
        re, im = spec[:n], spec[n:]
        own = freq_ref[b * 2 * n : (b + 1) * 2 * n, :].astype(F32)
        own_re, own_im = own[:n], own[n:]
        both = im * own_im
        corr_re = re * own_re + jnp.where(edge, 0.0, both)
        corr_im = jnp.where(edge, both, re * own_im - im * own_re)
        acc[:HALF] += jnp.sum(corr_re.reshape(PER_DFT, HALF, -1), axis=0)
        acc[HALF:] += jnp.sum(corr_im.reshape(PER_DFT, HALF, -1), axis=0)
        turned = jnp.concatenate([re * wa + im * wb, im * wl - re * wb], axis=0).astype(BF16)
        parts.append(dot(ih_ref[...], turned))
    grad_gated = masked(jnp.concatenate(parts, axis=0), lens)
    lin = lin_ref[...].astype(F32)
    sig = sig_ref[...].astype(F32)
    first = grad_gated * sig
    grad_a = jnp.concatenate([first, first * lin * (1.0 - sig)], axis=1).astype(BF16)
    grad_a_ref[...] = grad_a
    rows = pl.ds(pl.multiple_of(step * PER_STEP * SPAN, 16), PER_STEP * SPAN)
    h_all[rows, :] = h_ref[...]
    ga_all[rows, :] = grad_a

    @pl.when(step == pl.num_programs(0) - 1)
    def _():
        d = h_all.shape[1]
        gwin, gwout, taps = slice(0, 2 * d), slice(2 * d, 3 * d), slice(3 * d, theirs_ref.shape[1])
        theirs_ref[:, gwout] = theirs_in[...]
        own_ref[:, gwout] = own_in[...]
        small = dot(acc[...], back_ref[...], ((0,), (0,)), lax.Precision.HIGHEST)
        split(small, theirs_ref.at[:, taps], own_ref.at[:, taps])
        split(dot(h_all[...], ga_all[...], ((0,), (0,))), theirs_ref.at[:, gwin], own_ref.at[:, gwin])


def inputs_kernel(table_ref, frames_ref, grad_a_ref, gain_ref, win_ref, gframes_ref):
    grad_h = dot(grad_a_ref[...], win_ref[...], ((1,), (1,)))
    x = jnp.concatenate([frames_ref[slot_rows(table_ref, u), :] for u in range(PER_STEP)], axis=0)
    gain = gain_ref[...]
    _, normed, inv = normalize(x.astype(F32), gain)
    scaled = grad_h * gain
    inner = jnp.mean(scaled * normed, axis=1, keepdims=True)
    grad_x = inv * (scaled - jnp.mean(scaled, axis=1, keepdims=True) - normed * inner)
    grad_x = masked(grad_x, step_lens(table_ref)).astype(BF16)
    for u in range(PER_STEP):
        gframes_ref[slot_rows(table_ref, u), :] = grad_x[u * SPAN : (u + 1) * SPAN]


def collect_kernel(got_ref, out_ref):
    total = got_ref[0].astype(F32)
    for k in range(1, got_ref.shape[0]):
        total += got_ref[k].astype(F32)
    for k in range(out_ref.shape[0]):
        out_ref[k] = total.astype(BF16)


def finish_kernel(every_ref, w_ref, gain_ref, gwin_ref, gwout_ref, gwdw_ref, gln_ref):
    count = every_ref.shape[0]
    halves = [sum(every_ref[k].astype(F32) for k in range(core, count, 2)) for core in range(2)]
    rows = jnp.concatenate(halves, axis=0)
    d = gwout_ref.shape[1]
    gwin = rows[:, : 2 * d]
    gwin_ref[...] = gwin
    gwout_ref[...] = rows[:, 2 * d : 3 * d]
    gwdw_ref[...] = rows[:, 3 * d : 3 * d + gwdw_ref.shape[1]]
    ones = jnp.ones((8, 2 * d), F32)
    dots = dot(ones, gwin * w_ref[...].astype(F32), ((1,), (1,)), lax.Precision.HIGHEST)
    gln_ref[...] = dots[:1] / gain_ref[...]


SMEM = pl.BlockSpec(memory_space=pltpu.SMEM)


def whole(shape):
    return pl.BlockSpec(shape, lambda i: (0,) * len(shape))


def rows_of(shape, steps):
    return pl.BlockSpec((shape[0] // steps, shape[1]), lambda i: (i, 0))


def cost(flops, moved):
    return pl.CostEstimate(flops=int(flops), bytes_accessed=int(moved), transcendentals=0)


def params():
    return pltpu.CompilerParams(dimension_semantics=("arbitrary",), vmem_limit_bytes=VMEM_LIMIT)


def sds(shape, dtype):
    return jax.ShapeDtypeStruct(shape, dtype)


def unpack(lengths, owners, upstream, loaders):
    rows, d = upstream.shape
    vmem = pl.BlockSpec(memory_space=pltpu.VMEM)
    return pl.pallas_call(
        unpack_kernel,
        out_shape=(sds((loaders * SPAN, d), BF16), sds((loaders, 128), jnp.int32)),
        in_specs=[vmem] * 3,
        out_specs=(vmem, vmem),
        scratch_shapes=[
            pltpu.VMEM((rows + 8, d), F32),
            pltpu.VMEM((loaders, loaders), jnp.int32),
            pltpu.VMEM((loaders, loaders), jnp.int32),
            pltpu.SMEM((loaders, 128), jnp.int32),
            pltpu.SemaphoreType.DMA,
        ],
        compiler_params=pltpu.CompilerParams(vmem_limit_bytes=VMEM_LIMIT),
        name="unpack",
        cost_estimate=cost(1e9, 6 * rows * d),
    )(lengths, owners, upstream)


def pack(table, got, rows):
    return pl.pallas_call(
        pack_kernel,
        out_shape=sds((rows, got.shape[1]), BF16),
        in_specs=[SMEM, pl.BlockSpec(memory_space=pltpu.VMEM)],
        out_specs=pl.BlockSpec(memory_space=pltpu.VMEM),
        scratch_shapes=[pltpu.VMEM((rows + 8, got.shape[1]), F32)],
        compiler_params=pltpu.CompilerParams(vmem_limit_bytes=VMEM_LIMIT),
        name="pack",
        cost_estimate=cost(2e9, 6 * rows * got.shape[1]),
    )(table, got)


def forward(table, frames, gain, w_in, w_dw, tabs):
    high, low, high_t, low_t, taps_to, _ = tabs
    rows, d = frames.shape
    steps = rows // (SPAN * PER_STEP)
    freq = (rows // SPAN * POINTS, d)
    return pl.pallas_call(
        forward_kernel,
        grid=(steps,),
        out_shape=(
            sds((rows, d), BF16),
            sds((rows, d), BF16),
            sds((rows, d), BF16),
            sds(freq, BF16),
            sds((rows, d), F32),
            sds((3 * HALF, d), F32),
            sds((8, 128), F32),
        ),
        in_specs=[SMEM, whole(frames.shape), whole(gain.shape), whole(w_in.shape)]
        + [whole(v.shape) for v in (high, low, high_t, low_t, taps_to, w_dw)],
        out_specs=(
            rows_of((rows, d), steps),
            rows_of((rows, d), steps),
            rows_of((rows, d), steps),
            rows_of(freq, steps),
            rows_of((rows, d), steps),
            whole((3 * HALF, d)),
            whole((8, 128)),
        ),
        scratch_shapes=[pltpu.VMEM((2, 8, d), F32)],
        compiler_params=params(),
        name="forward",
        cost_estimate=cost(10e9, 16 * rows * d),
    )(table, frames, gain, w_in, high, low, high_t, low_t, taps_to, w_dw)


def middle(total, table, conv, dy, stats, bn_gain, bn_bias, w_out, copies):
    rows, d = conv.shape
    steps = rows // (SPAN * PER_STEP)
    part = rows_of((rows, d), steps)
    tiles = (copies, 8, 128)
    return pl.pallas_call(
        functools.partial(middle_kernel, total),
        grid=(steps,),
        out_shape=(
            sds((rows, d), BF16),
            sds((rows, d), BF16),
            sds((rows, d), F32),
            sds(tiles, F32),
            sds((8, 128), F32),
        ),
        in_specs=[SMEM, part, part] + [whole(v.shape) for v in (stats, bn_gain, bn_bias, w_out)],
        out_specs=(part, part, part, whole(tiles), whole((8, 128))),
        scratch_shapes=[pltpu.VMEM((2, 8, d), F32)],
        compiler_params=params(),
        name="middle",
        cost_estimate=cost(5e9, 12 * rows * d),
    )(table, conv, dy, stats, bn_gain, bn_bias, w_out)


def outputs(swished, dy, w_out):
    rows, d = swished.shape
    steps = rows // (SPAN * PER_STEP)
    part = rows_of((rows, d), steps)
    half = (d // 2, d)
    return pl.pallas_call(
        output_kernel,
        grid=(steps,),
        out_shape=(sds((rows, d), BF16), sds(half, BF16), sds(half, BF16)),
        in_specs=[part, part, whole(w_out.shape)],
        out_specs=(part, whole(half), whole(half)),
        scratch_shapes=[pltpu.VMEM((rows, d), BF16), pltpu.VMEM((rows, d), BF16)],
        compiler_params=params(),
        name="outputs",
        cost_estimate=cost(4e9, 6 * rows * d),
    )(swished, dy, w_out)


def backward(total, table, h, lin, sig, freq, conv, gbn, wf, stats, sums, bn_gain, theirs, own, tabs):
    high, _, high_t, _, _, back = tabs
    rows, d = h.shape
    width = 3 * d + back.shape[1]
    steps = rows // (SPAN * PER_STEP)
    part = rows_of((rows, d), steps)
    return pl.pallas_call(
        functools.partial(backward_kernel, total),
        grid=(steps,),
        out_shape=(
            sds((rows, 2 * d), BF16),
            sds((d // 2, width), BF16),
            sds((d // 2, width), BF16),
            sds((1, d), F32),
            sds((1, d), F32),
        ),
        in_specs=[SMEM, part, part, part, rows_of(freq.shape, steps), part, part]
        + [whole(v.shape) for v in (wf, stats, sums, bn_gain, theirs, own, high, high_t, back)],
        out_specs=(
            rows_of((rows, 2 * d), steps),
            whole((d // 2, width)),
            whole((d // 2, width)),
            whole((1, d)),
            whole((1, d)),
        ),
        scratch_shapes=[
            pltpu.VMEM((2 * HALF, d), F32),
            pltpu.VMEM((rows, d), BF16),
            pltpu.VMEM((rows, 2 * d), BF16),
        ],
        compiler_params=params(),
        name="backward",
        cost_estimate=cost(8e9, 18 * rows * d),
    )(table, h, lin, sig, freq, conv, gbn, wf, stats, sums, bn_gain, theirs, own, high, high_t, back)


def inputs_back(table, frames, grad_a, gain, w_in):
    rows, d = frames.shape
    steps = rows // (SPAN * PER_STEP)
    return pl.pallas_call(
        inputs_kernel,
        grid=(steps,),
        out_shape=sds((rows, d), BF16),
        in_specs=[SMEM, whole(frames.shape), rows_of(grad_a.shape, steps), whole(gain.shape), whole(w_in.shape)],
        out_specs=whole((rows, d)),
        compiler_params=params(),
        name="inputs_back",
        cost_estimate=cost(6e9, 12 * rows * d),
    )(table, frames, grad_a, gain, w_in)


def collect(got, count):
    vmem = pl.BlockSpec(memory_space=pltpu.VMEM)
    return pl.pallas_call(
        collect_kernel,
        out_shape=sds((count, *got.shape[1:]), BF16),
        in_specs=[vmem],
        out_specs=vmem,
        compiler_params=pltpu.CompilerParams(vmem_limit_bytes=SMALL_LIMIT),
        name="collect",
    )(got)


def finish(every, w_rows, gain_rows, taps):
    share, width = w_rows.shape
    d = width // 2
    vmem = pl.BlockSpec(memory_space=pltpu.VMEM)
    return pl.pallas_call(
        finish_kernel,
        out_shape=(sds((share, width), F32), sds((share, d), F32), sds((share, taps), F32), sds((1, share), F32)),
        in_specs=[vmem] * 3,
        out_specs=(vmem,) * 4,
        compiler_params=pltpu.CompilerParams(vmem_limit_bytes=SMALL_LIMIT),
        name="finish",
    )(every, w_rows, gain_rows)


def swapped(value, axes):
    return lax.all_to_all(value, axes, split_axis=0, concat_axis=0, tiled=True)


def over_bucket(theirs, own, loaders, ahead):
    got = lax.ppermute(theirs, "c", [(0, 1), (1, 0)])
    both = (own.astype(F32) + got.astype(F32)).astype(BF16).reshape(loaders, -1, own.shape[1])
    both, ahead = lax.optimization_barrier((both, ahead))
    return swapped(both, BUCKET), ahead


def local(frames, lengths, owners, upstream, ln_gain, w_in, w_dw, bn_gain, bn_bias, w_out):
    loaders = lax.axis_size(BUCKET)
    me = lax.axis_index(BUCKET)
    rows, d = frames.shape
    taps = w_dw.shape[1]
    share = d // loaders
    total = float(upstream.shape[0] * loaders * lax.axis_size(DP))
    tabs = tuple(jnp.asarray(v) for v in tables(taps))
    w_rows = lax.dynamic_slice_in_dim(w_in, me * share, share, 0)
    gain_rows = lax.dynamic_slice_in_dim(ln_gain, me * share, share, 0).reshape(1, share)
    gain, bn_gain, bn_bias = (v.reshape(1, d) for v in (ln_gain, bn_gain, bn_bias))

    dy, table = unpack(lengths, owners, upstream, loaders)
    dy = swapped(dy.reshape(loaders, SPAN, d), BUCKET).reshape(rows, d)
    h, lin, sig, freq, conv, wf, stats = forward(table, frames, gain, w_in, w_dw, tabs)
    stats = lax.psum(lax.psum(lax.psum(stats, "c"), "y"), "x")
    stats, dy = lax.optimization_barrier((stats, dy))
    stats = swapped(jnp.broadcast_to(stats, (lax.axis_size("z"), *stats.shape)), "z")
    swished, live_dy, gbn, sums, stats = middle(
        total, table, conv, dy, stats, bn_gain, bn_bias, w_out, lax.axis_size("z")
    )
    sums = jnp.sum(swapped(sums, "z"), axis=0)
    out, theirs, own = outputs(swished, live_dy, w_out)
    out, sums = lax.optimization_barrier((out, sums))
    out = swapped(out.reshape(loaders, SPAN, d), BUCKET).reshape(rows, d)
    sums = functools.reduce(lax.psum, ("c", "y", "x"), sums)
    grad_a, theirs, own, bias_total, gain_total = backward(
        total, table, h, lin, sig, freq, conv, gbn, wf, stats, sums, bn_gain, theirs, own, tabs
    )
    got, out = over_bucket(theirs, own, loaders, out)
    gframes = inputs_back(table, frames, grad_a, gain, w_in)
    out_frames = pack(table, out, upstream.shape[0])
    got, gframes, out_frames = lax.optimization_barrier((got, gframes, out_frames))
    every = swapped(collect(got, lax.axis_size(DP)), DP)
    gwin, gwout, gwdw, gln = finish(every, w_rows, gain_rows, taps)
    return (
        out_frames,
        gframes,
        gwin,
        gwout,
        gwdw,
        gln.reshape(share),
        gain_total.reshape(d),
        bias_total.reshape(d),
    )


def solution(mesh):
    torus = Mesh(mesh.devices.reshape(4, 2, 4, 8), ("y", "c", "x", "z"))
    in_specs = (P(EVERY, None), P(DP, None), P(DP, None), P(EVERY, None)) + (P(),) * 6
    out_specs = (P(EVERY, None), P(EVERY, None), P(BUCKET, None), P(BUCKET, None), P(BUCKET, None), P(BUCKET), P(), P())
    return jax.shard_map(local, mesh=torus, in_specs=in_specs, out_specs=out_specs, check_vma=False)
```

```python
import functools
import math

import jax
import jax.numpy as jnp
import numpy as np
from jax import lax
from jax.experimental import pallas as pl
from jax.experimental.pallas import tpu as pltpu
from jax.sharding import Mesh
from jax.sharding import PartitionSpec as P

BUCKET = ("x", "z")
DP = ("y", "c")
EVERY = ("y", "c", "x", "z")


EPSILON = 1e-05
SPAN = 48
POINTS = 64
HALF = POINTS // 2
PER_DFT = 4
PER_STEP = 8
UNROLL = 4
VMEM_LIMIT = 60 * 2**20
SMALL_LIMIT = 16 * 2**20

F32 = jnp.float32
BF16 = jnp.bfloat16


def dot(a, b, dims=((1,), (0,)), precision=None):
    return lax.dot_general(a, b, (dims, ((), ())), preferred_element_type=F32, precision=precision)


def tables(taps):
    f = np.arange(HALF)[:, None]
    t = np.arange(SPAN)[None, :]
    angle = 2 * np.pi * f * t / POINTS
    real = np.cos(angle) * math.sqrt(2 / POINTS)
    imag = -np.sin(angle) * math.sqrt(2 / POINTS)
    real[0] = math.sqrt(1 / POINTS)
    imag[0] = math.sqrt(1 / POINTS) * (-1.0) ** np.arange(SPAN)
    block = np.zeros((2 * HALF * PER_DFT, SPAN * PER_DFT))
    for u in range(PER_DFT):
        block[u * HALF : (u + 1) * HALF, u * SPAN : (u + 1) * SPAN] = real
        block[(PER_DFT + u) * HALF : (PER_DFT + u + 1) * HALF, u * SPAN : (u + 1) * SPAN] = imag
    lag = np.arange(taps)[None, :] - taps // 2
    turn = 2 * np.pi * f * lag / POINTS
    cos, sin = np.cos(turn), np.sin(turn)
    cos_last = cos.copy()
    cos_last[0] = np.cos(np.pi * lag[0])
    taps_to = np.concatenate([cos, sin, cos_last], axis=0)
    back = np.zeros((2 * HALF, 128))
    back[:HALF, :taps] = cos
    back[HALF : 2 * HALF, :taps] = -sin
    back[HALF, :taps] = np.cos(np.pi * lag[0])
    high = block.astype(jnp.bfloat16)
    low = (block - high.astype(np.float64)).astype(jnp.bfloat16)
    return (
        high,
        low,
        np.ascontiguousarray(high.T),
        np.ascontiguousarray(low.T),
        taps_to.astype(np.float32),
        back.astype(np.float32),
    )


def masked(value, lens):
    t = lax.broadcasted_iota(jnp.int32, (SPAN, value.shape[1]), 0)
    return jnp.concatenate(
        [
            jnp.where(t < n, value[u * SPAN : (u + 1) * SPAN], jnp.zeros((), value.dtype))
            for u, n in enumerate(lens)
        ],
        axis=0,
    )


def folded(value):
    return jnp.sum(value.reshape(-1, 8, value.shape[1]), axis=0)


def as_tile(first, second):
    rows = [v[:, k * 128 : (k + 1) * 128] for v in (first, second) for k in range(4)]
    return jnp.concatenate(rows, axis=0)


def from_tile(tile):
    rows = [tile[k : k + 1] for k in range(8)]
    return (jnp.concatenate(rows[:4], axis=1), jnp.concatenate(rows[4:], axis=1))


def normalize(x, gain):
    centred = x - jnp.mean(x, axis=1, keepdims=True)
    inverse = lax.rsqrt(jnp.mean(centred * centred, axis=1, keepdims=True) + EPSILON)
    normed = centred * inverse
    return (normed * gain).astype(BF16), normed, inverse


def spread(wf, part):
    rows = wf[part * HALF : (part + 1) * HALF]
    return jnp.concatenate([rows] * PER_DFT, axis=0)


def unpack_kernel(lengths_ref, owners_ref, upstream_ref, out_ref, table_ref, wide, lens_all, dest_all, table, sem):
    loaders = lens_all.shape[0]
    me = lax.axis_index(BUCKET)
    for k in range(loaders):
        lens_all[k : k + 1, :] = lengths_ref[:, k * loaders : (k + 1) * loaders]
        dest_all[k : k + 1, :] = owners_ref[:, k * loaders : (k + 1) * loaders]
    got = jnp.sum(jnp.where(dest_all[...] == me, lens_all[...], 0), axis=1, keepdims=True)
    square = (loaders, loaders)
    hit = dest_all[pl.ds(me, 1), :] == lax.broadcasted_iota(jnp.int32, square, 0)
    lens = jnp.sum(jnp.where(hit, lens_all[pl.ds(me, 1), :], 0), axis=1, keepdims=True)
    slots = jnp.sum(jnp.where(hit, lax.broadcasted_iota(jnp.int32, square, 1), 0), axis=1, keepdims=True)
    column = lax.broadcasted_iota(jnp.int32, table_ref.shape, 1)
    table_ref[...] = jnp.where(column == 0, got, jnp.where(column == 1, lens, slots))
    copy = pltpu.make_async_copy(table_ref, table, sem)
    copy.start()
    rows = upstream_ref.shape[0]
    wide[:rows, :] = upstream_ref[...].astype(F32)
    wide[rows:, :] = jnp.zeros((8, wide.shape[1]), F32)
    copy.wait()

    def step(group, start):
        for i in (group * UNROLL + k for k in range(UNROLL)):
            base = pl.multiple_of(start // 8 * 8, 8)
            window = pltpu.roll(wide[pl.ds(base, SPAN + 8), :], SPAN + 8 - start % 8, 0)
            out_ref[pl.ds(pl.multiple_of(i * SPAN, 16), SPAN), :] = window[:SPAN].astype(BF16)
            start += table[i, 0]
        return start

    lax.fori_loop(0, loaders // UNROLL, step, jnp.int32(0))


def pack_kernel(table_ref, got_ref, out_ref, wide):
    count = got_ref.shape[0] // SPAN
    top = lax.broadcasted_iota(jnp.int32, (8, got_ref.shape[1]), 0)

    def step(i, start):
        base = pl.multiple_of(start // 8 * 8, 8)
        rows = got_ref[pl.ds(pl.multiple_of(i * SPAN, 16), SPAN), :].astype(F32)
        window = jnp.concatenate([rows, jnp.zeros((8, rows.shape[1]), F32)], axis=0)
        window = pltpu.roll(window, start % 8, 0)
        kept = jnp.where(top < start % 8, wide[pl.ds(base, 8), :], window[:8])
        wide[pl.ds(base, 8), :] = kept
        wide[pl.ds(base + 8, SPAN), :] = window[8:]
        return start + table_ref[i, 0]

    lax.fori_loop(0, count, step, jnp.int32(0))
    out_ref[...] = wide[: out_ref.shape[0], :].astype(BF16)


def step_lens(table_ref):
    return [table_ref[pl.program_id(0) * PER_STEP + u, 1] for u in range(PER_STEP)]


def slot_rows(table_ref, u):
    slot = table_ref[pl.program_id(0) * PER_STEP + u, 2]
    return pl.ds(pl.multiple_of(slot * SPAN, 16), SPAN)


def forward_kernel(
    table_ref, frames_ref, gain_ref, win_ref, qh_ref, ql_ref, ih_ref, il_ref, to_ref, wdw_ref,
    h_ref, slope_ref, sig_ref, freq_ref, conv_ref, wf_ref, stats_ref, acc,
):
    step = pl.program_id(0)

    @pl.when(step == 0)
    def _():
        wf_ref[...] = dot(to_ref[...], wdw_ref[...], ((1,), (1,)), lax.Precision.HIGHEST)
        acc[...] = jnp.zeros_like(acc)

    d = frames_ref.shape[1]
    lens = step_lens(table_ref)
    x = jnp.concatenate([frames_ref[slot_rows(table_ref, u), :] for u in range(PER_STEP)], axis=0)
    h, _, _ = normalize(x.astype(F32), gain_ref[...])
    h_ref[...] = h
    a = dot(h, win_ref[...])
    lin = a[:, :d]
    sig = jax.nn.sigmoid(a[:, d:])
    slope_ref[...] = (lin * sig * (1.0 - sig)).astype(BF16)
    sig_ref[...] = sig.astype(BF16)
    gated = masked(lin * sig, lens).astype(BF16)
    wa, wb, wl = (spread(wf_ref[...], k) for k in range(3))
    for b in range(PER_STEP // PER_DFT):
        rows = slice(b * SPAN * PER_DFT, (b + 1) * SPAN * PER_DFT)
        part = gated[rows]
        spec = dot(qh_ref[...], part) + dot(ql_ref[...], part)
        freq_ref[b * POINTS * PER_DFT : (b + 1) * POINTS * PER_DFT, :] = spec.astype(BF16)
        re, im = spec[: HALF * PER_DFT], spec[HALF * PER_DFT :]
        turned = jnp.concatenate([re * wa - im * wb, im * wl + re * wb], axis=0)
        high = turned.astype(BF16)
        low = (turned - high.astype(F32)).astype(BF16)
        conv = dot(ih_ref[...], high) + dot(il_ref[...], high) + dot(ih_ref[...], low)
        conv_ref[rows, :] = conv
        live = masked(conv, lens[b * PER_DFT : (b + 1) * PER_DFT])
        acc[0] += folded(live)
        acc[1] += folded(live * live)

    @pl.when(step == pl.num_programs(0) - 1)
    def _():
        sums = [jnp.sum(acc[k], axis=0, keepdims=True) for k in range(2)]
        stats_ref[...] = as_tile(*sums)


def split(value, theirs_ref, own_ref):
    blocks = value.reshape(-1, 2, 8, value.shape[1])
    first = lax.axis_index("c") == 0
    low, high = blocks[:, 0], blocks[:, 1]
    theirs_ref[...] = jnp.where(first, high, low).reshape(theirs_ref.shape).astype(BF16)
    own_ref[...] = jnp.where(first, low, high).reshape(own_ref.shape).astype(BF16)


def bn_terms(stats, total):
    first, second = from_tile(stats)
    centre = first / total
    inverse = lax.rsqrt(second / total - centre * centre + EPSILON)
    return centre, inverse


def project_kernel(table_ref, dy_ref, wout_ref, live_dy_ref, grad_ref):
    dy = masked(dy_ref[...].astype(F32), step_lens(table_ref)).astype(BF16)
    live_dy_ref[...] = dy
    grad_ref[...] = dot(dy, wout_ref[...], ((1,), (1,)))


def middle_kernel(
    total, conv_ref, grad_ref, stats_ref, gain_ref, bias_ref,
    swished_ref, gbn_ref, sums_ref, moments_ref, acc,
):
    step = pl.program_id(0)

    @pl.when(step == 0)
    def _():
        acc[...] = jnp.zeros_like(acc)
        moments_ref[...] = jnp.sum(stats_ref[...], axis=0)

    centre, inverse = bn_terms(moments_ref[...], total)
    normed = (conv_ref[...] - centre) * inverse
    value = normed * gain_ref[...] + bias_ref[...]
    sig = jax.nn.sigmoid(value)
    swished_ref[...] = (value * sig).astype(BF16)
    grad = grad_ref[...] * (sig * (1.0 + value * (1.0 - sig)))
    gbn_ref[...] = grad
    acc[0] += folded(grad)
    acc[1] += folded(grad * normed)

    @pl.when(step == pl.num_programs(0) - 1)
    def _():
        sums = [jnp.sum(acc[k], axis=0, keepdims=True) for k in range(2)]
        sums_ref[...] = jnp.broadcast_to(as_tile(*sums)[None], sums_ref.shape)


def output_kernel(swished_ref, dy_ref, wout_ref, out_ref, theirs_ref, own_ref, sw_all, dy_all):
    step = pl.program_id(0)
    out_ref[...] = dot(swished_ref[...], wout_ref[...]).astype(BF16)
    rows = pl.ds(pl.multiple_of(step * PER_STEP * SPAN, 16), PER_STEP * SPAN)
    sw_all[rows, :] = swished_ref[...]
    dy_all[rows, :] = dy_ref[...]

    @pl.when(step == pl.num_programs(0) - 1)
    def _():
        split(dot(sw_all[...], dy_all[...], ((0,), (0,))), theirs_ref, own_ref)


def backward_kernel(
    total, table_ref, h_ref, slope_ref, sig_ref, freq_ref, conv_ref, gbn_ref, wf_ref, stats_ref, sums_ref,
    bn_gain_ref, theirs_in, own_in, qh_ref, ql_ref, ih_ref, il_ref, back_ref,
    grad_a_ref, theirs_ref, own_ref, bias_ref, bn_out_ref, acc, h_all, ga_all,
):
    step = pl.program_id(0)

    @pl.when(step == 0)
    def _():
        acc[...] = jnp.zeros_like(acc)

    lens = step_lens(table_ref)
    centre, inverse = bn_terms(stats_ref[...], total)
    bias_total, gain_total = from_tile(sums_ref[...])
    bias_ref[...] = bias_total
    bn_out_ref[...] = gain_total
    normed_bn = (conv_ref[...] - centre) * inverse
    scale = bn_gain_ref[...] * inverse
    grad_conv = scale * (gbn_ref[...] - bias_total / total - normed_bn * (gain_total / total))
    grad_conv = masked(grad_conv, lens).astype(BF16)
    wa, wb, wl = (spread(wf_ref[...], k) for k in range(3))
    n = HALF * PER_DFT
    edge = lax.broadcasted_iota(jnp.int32, (n, wa.shape[1]), 0) % HALF == 0
    parts = []
    for b in range(PER_STEP // PER_DFT):
        rows = slice(b * SPAN * PER_DFT, (b + 1) * SPAN * PER_DFT)
        spec = dot(qh_ref[...], grad_conv[rows]) + dot(ql_ref[...], grad_conv[rows])
        re, im = spec[:n], spec[n:]
        own = freq_ref[b * 2 * n : (b + 1) * 2 * n, :].astype(F32)
        own_re, own_im = own[:n], own[n:]
        both = im * own_im
        corr_re = re * own_re + jnp.where(edge, 0.0, both)
        corr_im = jnp.where(edge, both, re * own_im - im * own_re)
        acc[:HALF] += jnp.sum(corr_re.reshape(PER_DFT, HALF, -1), axis=0)
        acc[HALF:] += jnp.sum(corr_im.reshape(PER_DFT, HALF, -1), axis=0)
        turned = jnp.concatenate([re * wa + im * wb, im * wl - re * wb], axis=0).astype(BF16)
        parts.append(dot(ih_ref[...], turned) + dot(il_ref[...], turned))
    grad_gated = masked(jnp.concatenate(parts, axis=0), lens)
    grad_a = jnp.concatenate([grad_gated * s[...].astype(F32) for s in (sig_ref, slope_ref)], axis=1).astype(BF16)
    grad_a_ref[...] = grad_a
    rows = pl.ds(pl.multiple_of(step * PER_STEP * SPAN, 16), PER_STEP * SPAN)
    h_all[rows, :] = h_ref[...]
    ga_all[rows, :] = grad_a

    @pl.when(step == pl.num_programs(0) - 1)
    def _():
        d = h_all.shape[1]
        gwin, gwout, taps = slice(0, 2 * d), slice(2 * d, 3 * d), slice(3 * d, theirs_ref.shape[1])
        theirs_ref[:, gwout] = theirs_in[...]
        own_ref[:, gwout] = own_in[...]
        small = dot(acc[...], back_ref[...], ((0,), (0,)), lax.Precision.HIGHEST)
        split(small, theirs_ref.at[:, taps], own_ref.at[:, taps])
        split(dot(h_all[...], ga_all[...], ((0,), (0,))), theirs_ref.at[:, gwin], own_ref.at[:, gwin])


def inputs_kernel(table_ref, frames_ref, grad_a_ref, gain_ref, win_ref, gframes_ref):
    grad_h = dot(grad_a_ref[...], win_ref[...], ((1,), (1,)))
    x = jnp.concatenate([frames_ref[slot_rows(table_ref, u), :] for u in range(PER_STEP)], axis=0)
    gain = gain_ref[...]
    _, normed, inv = normalize(x.astype(F32), gain)
    scaled = grad_h * gain
    inner = jnp.mean(scaled * normed, axis=1, keepdims=True)
    grad_x = inv * (scaled - jnp.mean(scaled, axis=1, keepdims=True) - normed * inner)
    grad_x = masked(grad_x, step_lens(table_ref)).astype(BF16)
    for u in range(PER_STEP):
        gframes_ref[slot_rows(table_ref, u), :] = grad_x[u * SPAN : (u + 1) * SPAN]


def pair_kernel(own_ref, got_ref, both_ref):
    both_ref[...] = (own_ref[...].astype(F32) + got_ref[...].astype(F32)).astype(BF16)


def collect_kernel(got_ref, out_ref):
    total = got_ref[0].astype(F32)
    for k in range(1, got_ref.shape[0]):
        total += got_ref[k].astype(F32)
    for k in range(out_ref.shape[0]):
        out_ref[k] = total.astype(BF16)


def finish_kernel(every_ref, w_ref, gain_ref, gwin_ref, gwout_ref, gwdw_ref, gln_ref):
    count = every_ref.shape[0]
    halves = [sum(every_ref[k].astype(F32) for k in range(core, count, 2)) for core in range(2)]
    rows = jnp.concatenate(halves, axis=0)
    d = gwout_ref.shape[1]
    gwin = rows[:, : 2 * d]
    gwin_ref[...] = gwin
    gwout_ref[...] = rows[:, 2 * d : 3 * d]
    gwdw_ref[...] = rows[:, 3 * d : 3 * d + gwdw_ref.shape[1]]
    ones = jnp.ones((8, 2 * d), F32)
    dots = dot(ones, gwin * w_ref[...].astype(F32), ((1,), (1,)), lax.Precision.HIGHEST)
    gln_ref[...] = dots[:1] / gain_ref[...]


SMEM = pl.BlockSpec(memory_space=pltpu.SMEM)


def whole(shape):
    return pl.BlockSpec(shape, lambda i: (0,) * len(shape))


def rows_of(shape, steps):
    return pl.BlockSpec((shape[0] // steps, shape[1]), lambda i: (i, 0))


def cost(flops, moved):
    return pl.CostEstimate(flops=int(flops), bytes_accessed=int(moved), transcendentals=0)


def params():
    return pltpu.CompilerParams(dimension_semantics=("arbitrary",), vmem_limit_bytes=VMEM_LIMIT)


def sds(shape, dtype):
    return jax.ShapeDtypeStruct(shape, dtype)


def unpack(lengths, owners, upstream, loaders):
    rows, d = upstream.shape
    vmem = pl.BlockSpec(memory_space=pltpu.VMEM)
    return pl.pallas_call(
        unpack_kernel,
        out_shape=(sds((loaders * SPAN, d), BF16), sds((loaders, 128), jnp.int32)),
        in_specs=[vmem] * 3,
        out_specs=(vmem, vmem),
        scratch_shapes=[
            pltpu.VMEM((rows + 8, d), F32),
            pltpu.VMEM((loaders, loaders), jnp.int32),
            pltpu.VMEM((loaders, loaders), jnp.int32),
            pltpu.SMEM((loaders, 128), jnp.int32),
            pltpu.SemaphoreType.DMA,
        ],
        compiler_params=pltpu.CompilerParams(vmem_limit_bytes=VMEM_LIMIT),
        name="unpack",
        cost_estimate=cost(1e9, 6 * rows * d),
    )(lengths, owners, upstream)


def pack(table, got, rows):
    return pl.pallas_call(
        pack_kernel,
        out_shape=sds((rows, got.shape[1]), BF16),
        in_specs=[SMEM, pl.BlockSpec(memory_space=pltpu.VMEM)],
        out_specs=pl.BlockSpec(memory_space=pltpu.VMEM),
        scratch_shapes=[pltpu.VMEM((rows + 8, got.shape[1]), F32)],
        compiler_params=pltpu.CompilerParams(vmem_limit_bytes=VMEM_LIMIT),
        name="pack",
        cost_estimate=cost(2e9, 6 * rows * got.shape[1]),
    )(table, got)


def forward(table, frames, gain, w_in, w_dw, tabs):
    high, low, high_t, low_t, taps_to, _ = tabs
    rows, d = frames.shape
    steps = rows // (SPAN * PER_STEP)
    freq = (rows // SPAN * POINTS, d)
    return pl.pallas_call(
        forward_kernel,
        grid=(steps,),
        out_shape=(
            sds((rows, d), BF16),
            sds((rows, d), BF16),
            sds((rows, d), BF16),
            sds(freq, BF16),
            sds((rows, d), F32),
            sds((3 * HALF, d), F32),
            sds((8, 128), F32),
        ),
        in_specs=[SMEM, whole(frames.shape), whole(gain.shape), whole(w_in.shape)]
        + [whole(v.shape) for v in (high, low, high_t, low_t, taps_to, w_dw)],
        out_specs=(
            rows_of((rows, d), steps),
            rows_of((rows, d), steps),
            rows_of((rows, d), steps),
            rows_of(freq, steps),
            rows_of((rows, d), steps),
            whole((3 * HALF, d)),
            whole((8, 128)),
        ),
        scratch_shapes=[pltpu.VMEM((2, 8, d), F32)],
        compiler_params=params(),
        name="forward",
        cost_estimate=cost(10e9, 16 * rows * d),
    )(table, frames, gain, w_in, high, low, high_t, low_t, taps_to, w_dw)


def project(table, dy, w_out):
    rows, d = dy.shape
    steps = rows // (SPAN * PER_STEP)
    part = rows_of((rows, d), steps)
    return pl.pallas_call(
        project_kernel,
        grid=(steps,),
        out_shape=(sds((rows, d), BF16), sds((rows, d), F32)),
        in_specs=[SMEM, part, whole(w_out.shape)],
        out_specs=(part, part),
        compiler_params=params(),
        name="project",
        cost_estimate=cost(3e9, 6 * rows * d),
    )(table, dy, w_out)


def middle(total, conv, grad, stats, bn_gain, bn_bias, copies):
    rows, d = conv.shape
    steps = rows // (SPAN * PER_STEP)
    part = rows_of((rows, d), steps)
    tiles = (copies, 8, 128)
    return pl.pallas_call(
        functools.partial(middle_kernel, total),
        grid=(steps,),
        out_shape=(sds((rows, d), BF16), sds((rows, d), F32), sds(tiles, F32), sds((8, 128), F32)),
        in_specs=[part, part] + [whole(v.shape) for v in (stats, bn_gain, bn_bias)],
        out_specs=(part, part, whole(tiles), whole((8, 128))),
        scratch_shapes=[pltpu.VMEM((2, 8, d), F32)],
        compiler_params=params(),
        name="middle",
        cost_estimate=cost(4e9, 10 * rows * d),
    )(conv, grad, stats, bn_gain, bn_bias)


def outputs(swished, dy, w_out):
    rows, d = swished.shape
    steps = rows // (SPAN * PER_STEP)
    part = rows_of((rows, d), steps)
    half = (d // 2, d)
    return pl.pallas_call(
        output_kernel,
        grid=(steps,),
        out_shape=(sds((rows, d), BF16), sds(half, BF16), sds(half, BF16)),
        in_specs=[part, part, whole(w_out.shape)],
        out_specs=(part, whole(half), whole(half)),
        scratch_shapes=[pltpu.VMEM((rows, d), BF16), pltpu.VMEM((rows, d), BF16)],
        compiler_params=params(),
        name="outputs",
        cost_estimate=cost(4e9, 6 * rows * d),
    )(swished, dy, w_out)


def backward(total, table, h, slope, sig, freq, conv, gbn, wf, stats, sums, bn_gain, theirs, own, tabs):
    high, low, high_t, low_t, _, back = tabs
    rows, d = h.shape
    width = 3 * d + back.shape[1]
    steps = rows // (SPAN * PER_STEP)
    part = rows_of((rows, d), steps)
    return pl.pallas_call(
        functools.partial(backward_kernel, total),
        grid=(steps,),
        out_shape=(
            sds((rows, 2 * d), BF16),
            sds((d // 2, width), BF16),
            sds((d // 2, width), BF16),
            sds((1, d), F32),
            sds((1, d), F32),
        ),
        in_specs=[SMEM, part, part, part, rows_of(freq.shape, steps), part, part]
        + [whole(v.shape) for v in (wf, stats, sums, bn_gain, theirs, own, high, low, high_t, low_t, back)],
        out_specs=(
            rows_of((rows, 2 * d), steps),
            whole((d // 2, width)),
            whole((d // 2, width)),
            whole((1, d)),
            whole((1, d)),
        ),
        scratch_shapes=[
            pltpu.VMEM((2 * HALF, d), F32),
            pltpu.VMEM((rows, d), BF16),
            pltpu.VMEM((rows, 2 * d), BF16),
        ],
        compiler_params=params(),
        name="backward",
        cost_estimate=cost(8e9, 18 * rows * d),
    )(table, h, slope, sig, freq, conv, gbn, wf, stats, sums, bn_gain, theirs, own, high, low, high_t, low_t, back)


def inputs_back(table, frames, grad_a, gain, w_in):
    rows, d = frames.shape
    steps = rows // (SPAN * PER_STEP)
    return pl.pallas_call(
        inputs_kernel,
        grid=(steps,),
        out_shape=sds((rows, d), BF16),
        in_specs=[SMEM, whole(frames.shape), rows_of(grad_a.shape, steps), whole(gain.shape), whole(w_in.shape)],
        out_specs=whole((rows, d)),
        compiler_params=params(),
        name="inputs_back",
        cost_estimate=cost(6e9, 12 * rows * d),
    )(table, frames, grad_a, gain, w_in)


def pair_sum(own, got):
    rows, width = own.shape
    part = pl.BlockSpec((rows // 2, width), lambda i: (i, 0))
    return pl.pallas_call(
        pair_kernel,
        grid=(2,),
        out_shape=sds((rows, width), BF16),
        in_specs=[part, part],
        out_specs=part,
        compiler_params=pltpu.CompilerParams(vmem_limit_bytes=SMALL_LIMIT),
        name="pair_sum",
        cost_estimate=cost(2 * rows * width, 6 * rows * width),
    )(own, got)


def collect(got, count):
    vmem = pl.BlockSpec(memory_space=pltpu.VMEM)
    return pl.pallas_call(
        collect_kernel,
        out_shape=sds((count, *got.shape[1:]), BF16),
        in_specs=[vmem],
        out_specs=vmem,
        compiler_params=pltpu.CompilerParams(vmem_limit_bytes=SMALL_LIMIT),
        name="collect",
    )(got)


def finish(every, w_rows, gain_rows, taps):
    share, width = w_rows.shape
    d = width // 2
    vmem = pl.BlockSpec(memory_space=pltpu.VMEM)
    return pl.pallas_call(
        finish_kernel,
        out_shape=(sds((share, width), F32), sds((share, d), F32), sds((share, taps), F32), sds((1, share), F32)),
        in_specs=[vmem] * 3,
        out_specs=(vmem,) * 4,
        compiler_params=pltpu.CompilerParams(vmem_limit_bytes=SMALL_LIMIT),
        name="finish",
    )(every, w_rows, gain_rows)


def swapped(value, axes):
    return lax.all_to_all(value, axes, split_axis=0, concat_axis=0, tiled=True)


def over_bucket(theirs, own, loaders, ahead):
    got = lax.ppermute(theirs, "c", [(0, 1), (1, 0)])
    both = pair_sum(own, got).reshape(loaders, -1, own.shape[1])
    both, ahead = lax.optimization_barrier((both, ahead))
    return swapped(both, BUCKET), ahead


def local(frames, lengths, owners, upstream, ln_gain, w_in, w_dw, bn_gain, bn_bias, w_out):
    loaders = lax.axis_size(BUCKET)
    me = lax.axis_index(BUCKET)
    rows, d = frames.shape
    taps = w_dw.shape[1]
    share = d // loaders
    total = float(upstream.shape[0] * loaders * lax.axis_size(DP))
    tabs = tuple(jnp.asarray(v) for v in tables(taps))
    w_rows = lax.dynamic_slice_in_dim(w_in, me * share, share, 0)
    gain_rows = lax.dynamic_slice_in_dim(ln_gain, me * share, share, 0).reshape(1, share)
    gain, bn_gain, bn_bias = (v.reshape(1, d) for v in (ln_gain, bn_gain, bn_bias))

    dy, table = unpack(lengths, owners, upstream, loaders)
    dy = swapped(dy.reshape(loaders, SPAN, d), BUCKET).reshape(rows, d)
    h, slope, sig, freq, conv, wf, stats = forward(table, frames, gain, w_in, w_dw, tabs)
    stats = lax.psum(lax.psum(lax.psum(stats, "c"), "y"), "x")
    stats, dy = lax.optimization_barrier((stats, dy))
    stats = swapped(jnp.broadcast_to(stats, (lax.axis_size("z"), *stats.shape)), "z")
    live_dy, grad = project(table, dy, w_out)
    swished, gbn, sums, stats = middle(total, conv, grad, stats, bn_gain, bn_bias, lax.axis_size(("c", "z")))
    sums = jnp.sum(swapped(sums, ("c", "z")), axis=0)
    out, theirs, own = outputs(swished, live_dy, w_out)
    out, sums = lax.optimization_barrier((out, sums))
    out = swapped(out.reshape(loaders, SPAN, d), BUCKET).reshape(rows, d)
    sums = lax.psum(lax.psum(sums, "y"), "x")
    grad_a, theirs, own, bias_total, gain_total = backward(
        total, table, h, slope, sig, freq, conv, gbn, wf, stats, sums, bn_gain, theirs, own, tabs
    )
    got, out = over_bucket(theirs, own, loaders, out)
    gframes = inputs_back(table, frames, grad_a, gain, w_in)
    out_frames = pack(table, out, upstream.shape[0])
    got, gframes, out_frames = lax.optimization_barrier((got, gframes, out_frames))
    every = swapped(collect(got, lax.axis_size(DP)), DP)
    gwin, gwout, gwdw, gln = finish(every, w_rows, gain_rows, taps)
    return (
        out_frames,
        gframes,
        gwin,
        gwout,
        gwdw,
        gln.reshape(share),
        gain_total.reshape(d),
        bias_total.reshape(d),
    )


def solution(mesh):
    torus = Mesh(mesh.devices.reshape(4, 2, 4, 8), ("y", "c", "x", "z"))
    in_specs = (P(EVERY, None), P(DP, None), P(DP, None), P(EVERY, None)) + (P(),) * 6
    out_specs = (P(EVERY, None), P(EVERY, None), P(BUCKET, None), P(BUCKET, None), P(BUCKET, None), P(BUCKET), P(), P())
    return jax.shard_map(local, mesh=torus, in_specs=in_specs, out_specs=out_specs, check_vma=False)
```

```python
import functools
import math

import jax
import jax.numpy as jnp
import numpy as np
from jax import lax
from jax.experimental import pallas as pl
from jax.experimental.pallas import tpu as pltpu
from jax.sharding import Mesh
from jax.sharding import PartitionSpec as P

BUCKET = ("x", "z")
DP = ("y", "c")
EVERY = ("y", "c", "x", "z")


EPSILON = 1e-05
SPAN = 48
POINTS = 64
HALF = POINTS // 2
PER_DFT = 4
PER_STEP = 8
UNROLL = 4
VMEM_LIMIT = 60 * 2**20
SMALL_LIMIT = 16 * 2**20

F32 = jnp.float32
BF16 = jnp.bfloat16


def dot(a, b, dims=((1,), (0,)), precision=None):
    return lax.dot_general(a, b, (dims, ((), ())), preferred_element_type=F32, precision=precision)


def tables(taps):
    f = np.arange(HALF)[:, None]
    t = np.arange(SPAN)[None, :]
    angle = 2 * np.pi * f * t / POINTS
    real = np.cos(angle) * math.sqrt(2 / POINTS)
    imag = -np.sin(angle) * math.sqrt(2 / POINTS)
    real[0] = math.sqrt(1 / POINTS)
    imag[0] = math.sqrt(1 / POINTS) * (-1.0) ** np.arange(SPAN)
    block = np.zeros((2 * HALF * PER_DFT, SPAN * PER_DFT))
    for u in range(PER_DFT):
        block[u * HALF : (u + 1) * HALF, u * SPAN : (u + 1) * SPAN] = real
        block[(PER_DFT + u) * HALF : (PER_DFT + u + 1) * HALF, u * SPAN : (u + 1) * SPAN] = imag
    lag = np.arange(taps)[None, :] - taps // 2
    turn = 2 * np.pi * f * lag / POINTS
    cos, sin = np.cos(turn), np.sin(turn)
    cos_last = cos.copy()
    cos_last[0] = np.cos(np.pi * lag[0])
    taps_to = np.concatenate([cos, sin, cos_last], axis=0)
    back = np.zeros((2 * HALF, 128))
    back[:HALF, :taps] = cos
    back[HALF : 2 * HALF, :taps] = -sin
    back[HALF, :taps] = np.cos(np.pi * lag[0])
    high = block.astype(jnp.bfloat16)
    low = (block - high.astype(np.float64)).astype(jnp.bfloat16)
    return (
        high,
        low,
        np.ascontiguousarray(high.T),
        np.ascontiguousarray(low.T),
        taps_to.astype(np.float32),
        back.astype(np.float32),
    )


def masked(value, lens):
    t = lax.broadcasted_iota(jnp.int32, (SPAN, value.shape[1]), 0)
    return jnp.concatenate(
        [
            jnp.where(t < n, value[u * SPAN : (u + 1) * SPAN], jnp.zeros((), value.dtype))
            for u, n in enumerate(lens)
        ],
        axis=0,
    )


def folded(value):
    return jnp.sum(value.reshape(-1, 8, value.shape[1]), axis=0)


def as_tile(first, second):
    rows = [v[:, k * 128 : (k + 1) * 128] for v in (first, second) for k in range(4)]
    return jnp.concatenate(rows, axis=0)


def from_tile(tile):
    rows = [tile[k : k + 1] for k in range(8)]
    return (jnp.concatenate(rows[:4], axis=1), jnp.concatenate(rows[4:], axis=1))


def normalize(x, gain):
    centred = x - jnp.mean(x, axis=1, keepdims=True)
    inverse = lax.rsqrt(jnp.mean(centred * centred, axis=1, keepdims=True) + EPSILON)
    normed = centred * inverse
    return (normed * gain).astype(BF16), normed, inverse


def spread(wf, part):
    rows = wf[part * HALF : (part + 1) * HALF]
    return jnp.concatenate([rows] * PER_DFT, axis=0)


def unpack_kernel(lengths_ref, owners_ref, upstream_ref, out_ref, table_ref, wide, lens_all, dest_all, table, sem):
    loaders = lens_all.shape[0]
    me = lax.axis_index(BUCKET)
    for k in range(loaders):
        lens_all[k : k + 1, :] = lengths_ref[:, k * loaders : (k + 1) * loaders]
        dest_all[k : k + 1, :] = owners_ref[:, k * loaders : (k + 1) * loaders]
    got = jnp.sum(jnp.where(dest_all[...] == me, lens_all[...], 0), axis=1, keepdims=True)
    square = (loaders, loaders)
    hit = dest_all[pl.ds(me, 1), :] == lax.broadcasted_iota(jnp.int32, square, 0)
    lens = jnp.sum(jnp.where(hit, lens_all[pl.ds(me, 1), :], 0), axis=1, keepdims=True)
    slots = jnp.sum(jnp.where(hit, lax.broadcasted_iota(jnp.int32, square, 1), 0), axis=1, keepdims=True)
    column = lax.broadcasted_iota(jnp.int32, table_ref.shape, 1)
    table_ref[...] = jnp.where(column == 0, got, jnp.where(column == 1, lens, slots))
    copy = pltpu.make_async_copy(table_ref, table, sem)
    copy.start()
    rows = upstream_ref.shape[0]
    wide[:rows, :] = upstream_ref[...].astype(F32)
    wide[rows:, :] = jnp.zeros((8, wide.shape[1]), F32)
    copy.wait()

    def step(group, start):
        for i in (group * UNROLL + k for k in range(UNROLL)):
            base = pl.multiple_of(start // 8 * 8, 8)
            window = pltpu.roll(wide[pl.ds(base, SPAN + 8), :], SPAN + 8 - start % 8, 0)
            out_ref[pl.ds(pl.multiple_of(i * SPAN, 16), SPAN), :] = window[:SPAN].astype(BF16)
            start += table[i, 0]
        return start

    lax.fori_loop(0, loaders // UNROLL, step, jnp.int32(0))


def pack_kernel(table_ref, got_ref, out_ref, wide):
    count = got_ref.shape[0] // SPAN
    top = lax.broadcasted_iota(jnp.int32, (8, got_ref.shape[1]), 0)

    def step(i, start):
        base = pl.multiple_of(start // 8 * 8, 8)
        rows = got_ref[pl.ds(pl.multiple_of(i * SPAN, 16), SPAN), :].astype(F32)
        window = jnp.concatenate([rows, jnp.zeros((8, rows.shape[1]), F32)], axis=0)
        window = pltpu.roll(window, start % 8, 0)
        kept = jnp.where(top < start % 8, wide[pl.ds(base, 8), :], window[:8])
        wide[pl.ds(base, 8), :] = kept
        wide[pl.ds(base + 8, SPAN), :] = window[8:]
        return start + table_ref[i, 0]

    lax.fori_loop(0, count, step, jnp.int32(0))
    out_ref[...] = wide[: out_ref.shape[0], :].astype(BF16)


def step_lens(table_ref):
    return [table_ref[pl.program_id(0) * PER_STEP + u, 1] for u in range(PER_STEP)]


def slot_rows(table_ref, u):
    slot = table_ref[pl.program_id(0) * PER_STEP + u, 2]
    return pl.ds(pl.multiple_of(slot * SPAN, 16), SPAN)


def forward_kernel(
    table_ref, frames_ref, gain_ref, win_ref, qh_ref, ql_ref, ih_ref, il_ref, to_ref, wdw_ref,
    h_ref, slope_ref, sig_ref, freq_ref, conv_ref, wf_ref, stats_ref, acc,
):
    step = pl.program_id(0)

    @pl.when(step == 0)
    def _():
        wf_ref[...] = dot(to_ref[...], wdw_ref[...], ((1,), (1,)), lax.Precision.HIGHEST)
        acc[...] = jnp.zeros_like(acc)

    d = frames_ref.shape[1]
    lens = step_lens(table_ref)
    x = jnp.concatenate([frames_ref[slot_rows(table_ref, u), :] for u in range(PER_STEP)], axis=0)
    h, _, _ = normalize(x.astype(F32), gain_ref[...])
    h_ref[...] = h
    a = dot(h, win_ref[...])
    lin = a[:, :d]
    sig = jax.nn.sigmoid(a[:, d:])
    slope_ref[...] = (lin * sig * (1.0 - sig)).astype(BF16)
    sig_ref[...] = sig.astype(BF16)
    gated = masked(lin * sig, lens).astype(BF16)
    wa, wb, wl = (spread(wf_ref[...], k) for k in range(3))
    for b in range(PER_STEP // PER_DFT):
        rows = slice(b * SPAN * PER_DFT, (b + 1) * SPAN * PER_DFT)
        part = gated[rows]
        spec = dot(qh_ref[...], part) + dot(ql_ref[...], part)
        freq_ref[b * POINTS * PER_DFT : (b + 1) * POINTS * PER_DFT, :] = spec.astype(BF16)
        re, im = spec[: HALF * PER_DFT], spec[HALF * PER_DFT :]
        turned = jnp.concatenate([re * wa - im * wb, im * wl + re * wb], axis=0)
        high = turned.astype(BF16)
        low = (turned - high.astype(F32)).astype(BF16)
        conv = dot(ih_ref[...], high) + dot(il_ref[...], high) + dot(ih_ref[...], low)
        conv_ref[rows, :] = conv
        live = masked(conv, lens[b * PER_DFT : (b + 1) * PER_DFT])
        acc[0] += folded(live)
        acc[1] += folded(live * live)

    @pl.when(step == pl.num_programs(0) - 1)
    def _():
        sums = [jnp.sum(acc[k], axis=0, keepdims=True) for k in range(2)]
        stats_ref[...] = as_tile(*sums)


def split(value, theirs_ref, own_ref):
    blocks = value.reshape(-1, 2, 8, value.shape[1])
    first = lax.axis_index("c") == 0
    low, high = blocks[:, 0], blocks[:, 1]
    theirs_ref[...] = jnp.where(first, high, low).reshape(theirs_ref.shape).astype(BF16)
    own_ref[...] = jnp.where(first, low, high).reshape(own_ref.shape).astype(BF16)


def bn_terms(stats, total):
    first, second = from_tile(stats)
    centre = first / total
    inverse = lax.rsqrt(second / total - centre * centre + EPSILON)
    return centre, inverse


def project_kernel(table_ref, dy_ref, wout_ref, live_dy_ref, grad_ref):
    dy = masked(dy_ref[...].astype(F32), step_lens(table_ref)).astype(BF16)
    live_dy_ref[...] = dy
    grad_ref[...] = dot(dy, wout_ref[...], ((1,), (1,)))


def middle_kernel(
    total, conv_ref, grad_ref, stats_ref, gain_ref, bias_ref,
    swished_ref, gbn_ref, sums_ref, moments_ref, acc,
):
    step = pl.program_id(0)

    @pl.when(step == 0)
    def _():
        acc[...] = jnp.zeros_like(acc)
        moments_ref[...] = jnp.sum(stats_ref[...], axis=0)

    centre, inverse = bn_terms(moments_ref[...], total)
    normed = (conv_ref[...] - centre) * inverse
    value = normed * gain_ref[...] + bias_ref[...]
    sig = jax.nn.sigmoid(value)
    swished_ref[...] = (value * sig).astype(BF16)
    grad = grad_ref[...] * (sig * (1.0 + value * (1.0 - sig)))
    gbn_ref[...] = grad
    acc[0] += folded(grad)
    acc[1] += folded(grad * normed)

    @pl.when(step == pl.num_programs(0) - 1)
    def _():
        sums = [jnp.sum(acc[k], axis=0, keepdims=True) for k in range(2)]
        sums_ref[...] = jnp.broadcast_to(as_tile(*sums)[None], sums_ref.shape)


def output_kernel(swished_ref, dy_ref, wout_ref, out_ref, theirs_ref, own_ref, sw_all, dy_all):
    step = pl.program_id(0)
    out_ref[...] = dot(swished_ref[...], wout_ref[...]).astype(BF16)
    rows = pl.ds(pl.multiple_of(step * PER_STEP * SPAN, 16), PER_STEP * SPAN)
    sw_all[rows, :] = swished_ref[...]
    dy_all[rows, :] = dy_ref[...]

    @pl.when(step == pl.num_programs(0) - 1)
    def _():
        split(dot(sw_all[...], dy_all[...], ((0,), (0,))), theirs_ref, own_ref)


def backward_kernel(
    total, table_ref, h_ref, slope_ref, sig_ref, freq_ref, conv_ref, gbn_ref, wf_ref, stats_ref, sums_ref,
    bn_gain_ref, theirs_in, own_in, qh_ref, ql_ref, ih_ref, il_ref, back_ref,
    grad_a_ref, theirs_ref, own_ref, bias_ref, bn_out_ref, acc, h_all, ga_all,
):
    step = pl.program_id(0)

    @pl.when(step == 0)
    def _():
        acc[...] = jnp.zeros_like(acc)

    lens = step_lens(table_ref)
    centre, inverse = bn_terms(stats_ref[...], total)
    bias_total, gain_total = from_tile(sums_ref[...])
    bias_ref[...] = bias_total
    bn_out_ref[...] = gain_total
    normed_bn = (conv_ref[...] - centre) * inverse
    scale = bn_gain_ref[...] * inverse
    grad_conv = scale * (gbn_ref[...] - bias_total / total - normed_bn * (gain_total / total))
    grad_conv = masked(grad_conv, lens).astype(BF16)
    wa, wb, wl = (spread(wf_ref[...], k) for k in range(3))
    n = HALF * PER_DFT
    edge = lax.broadcasted_iota(jnp.int32, (n, wa.shape[1]), 0) % HALF == 0
    parts = []
    for b in range(PER_STEP // PER_DFT):
        rows = slice(b * SPAN * PER_DFT, (b + 1) * SPAN * PER_DFT)
        spec = dot(qh_ref[...], grad_conv[rows]) + dot(ql_ref[...], grad_conv[rows])
        re, im = spec[:n], spec[n:]
        own = freq_ref[b * 2 * n : (b + 1) * 2 * n, :].astype(F32)
        own_re, own_im = own[:n], own[n:]
        both = im * own_im
        corr_re = re * own_re + jnp.where(edge, 0.0, both)
        corr_im = jnp.where(edge, both, re * own_im - im * own_re)
        acc[:HALF] += jnp.sum(corr_re.reshape(PER_DFT, HALF, -1), axis=0)
        acc[HALF:] += jnp.sum(corr_im.reshape(PER_DFT, HALF, -1), axis=0)
        turned = jnp.concatenate([re * wa + im * wb, im * wl - re * wb], axis=0).astype(BF16)
        parts.append(dot(ih_ref[...], turned) + dot(il_ref[...], turned))
    grad_gated = masked(jnp.concatenate(parts, axis=0), lens)
    grad_a = jnp.concatenate([grad_gated * s[...].astype(F32) for s in (sig_ref, slope_ref)], axis=1).astype(BF16)
    grad_a_ref[...] = grad_a
    rows = pl.ds(pl.multiple_of(step * PER_STEP * SPAN, 16), PER_STEP * SPAN)
    h_all[rows, :] = h_ref[...]
    ga_all[rows, :] = grad_a

    @pl.when(step == pl.num_programs(0) - 1)
    def _():
        d = h_all.shape[1]
        gwin, gwout, taps = slice(0, 2 * d), slice(2 * d, 3 * d), slice(3 * d, theirs_ref.shape[1])
        theirs_ref[:, gwout] = theirs_in[...]
        own_ref[:, gwout] = own_in[...]
        small = dot(acc[...], back_ref[...], ((0,), (0,)), lax.Precision.HIGHEST)
        split(small, theirs_ref.at[:, taps], own_ref.at[:, taps])
        split(dot(h_all[...], ga_all[...], ((0,), (0,))), theirs_ref.at[:, gwin], own_ref.at[:, gwin])


def inputs_kernel(table_ref, frames_ref, grad_a_ref, gain_ref, win_ref, gframes_ref):
    grad_h = dot(grad_a_ref[...], win_ref[...], ((1,), (1,)))
    x = jnp.concatenate([frames_ref[slot_rows(table_ref, u), :] for u in range(PER_STEP)], axis=0)
    gain = gain_ref[...]
    _, normed, inv = normalize(x.astype(F32), gain)
    scaled = grad_h * gain
    inner = jnp.mean(scaled * normed, axis=1, keepdims=True)
    grad_x = inv * (scaled - jnp.mean(scaled, axis=1, keepdims=True) - normed * inner)
    grad_x = masked(grad_x, step_lens(table_ref)).astype(BF16)
    for u in range(PER_STEP):
        gframes_ref[slot_rows(table_ref, u), :] = grad_x[u * SPAN : (u + 1) * SPAN]


def pair_kernel(own_ref, got_ref, both_ref):
    both_ref[...] = (own_ref[...].astype(F32) + got_ref[...].astype(F32)).astype(BF16)


def collect_kernel(got_ref, out_ref):
    total = got_ref[0].astype(F32)
    for k in range(1, got_ref.shape[0]):
        total += got_ref[k].astype(F32)
    for k in range(out_ref.shape[0]):
        out_ref[k] = total.astype(BF16)


def finish_kernel(every_ref, w_ref, gain_ref, gwin_ref, gwout_ref, gwdw_ref, gln_ref):
    count = every_ref.shape[0]
    halves = [sum(every_ref[k].astype(F32) for k in range(core, count, 2)) for core in range(2)]
    rows = jnp.concatenate(halves, axis=0)
    d = gwout_ref.shape[1]
    gwin = rows[:, : 2 * d]
    gwin_ref[...] = gwin
    gwout_ref[...] = rows[:, 2 * d : 3 * d]
    gwdw_ref[...] = rows[:, 3 * d : 3 * d + gwdw_ref.shape[1]]
    ones = jnp.ones((8, 2 * d), F32)
    dots = dot(ones, gwin * w_ref[...].astype(F32), ((1,), (1,)), lax.Precision.HIGHEST)
    gln_ref[...] = dots[:1] / gain_ref[...]


SMEM = pl.BlockSpec(memory_space=pltpu.SMEM)


def whole(shape):
    return pl.BlockSpec(shape, lambda i: (0,) * len(shape))


def rows_of(shape, steps):
    return pl.BlockSpec((shape[0] // steps, shape[1]), lambda i: (i, 0))


def cost(flops, moved):
    return pl.CostEstimate(flops=int(flops), bytes_accessed=int(moved), transcendentals=0)


def params():
    return pltpu.CompilerParams(dimension_semantics=("arbitrary",), vmem_limit_bytes=VMEM_LIMIT)


def sds(shape, dtype):
    return jax.ShapeDtypeStruct(shape, dtype)


def unpack(lengths, owners, upstream, loaders):
    rows, d = upstream.shape
    vmem = pl.BlockSpec(memory_space=pltpu.VMEM)
    return pl.pallas_call(
        unpack_kernel,
        out_shape=(sds((loaders * SPAN, d), BF16), sds((loaders, 128), jnp.int32)),
        in_specs=[vmem] * 3,
        out_specs=(vmem, vmem),
        scratch_shapes=[
            pltpu.VMEM((rows + 8, d), F32),
            pltpu.VMEM((loaders, loaders), jnp.int32),
            pltpu.VMEM((loaders, loaders), jnp.int32),
            pltpu.SMEM((loaders, 128), jnp.int32),
            pltpu.SemaphoreType.DMA,
        ],
        compiler_params=pltpu.CompilerParams(vmem_limit_bytes=VMEM_LIMIT),
        name="unpack",
        cost_estimate=cost(1e9, 6 * rows * d),
    )(lengths, owners, upstream)


def pack(table, got, rows):
    return pl.pallas_call(
        pack_kernel,
        out_shape=sds((rows, got.shape[1]), BF16),
        in_specs=[SMEM, pl.BlockSpec(memory_space=pltpu.VMEM)],
        out_specs=pl.BlockSpec(memory_space=pltpu.VMEM),
        scratch_shapes=[pltpu.VMEM((rows + 8, got.shape[1]), F32)],
        compiler_params=pltpu.CompilerParams(vmem_limit_bytes=VMEM_LIMIT),
        name="pack",
        cost_estimate=cost(2e9, 6 * rows * got.shape[1]),
    )(table, got)


def forward(table, frames, gain, w_in, w_dw, tabs):
    high, low, high_t, low_t, taps_to, _ = tabs
    rows, d = frames.shape
    steps = rows // (SPAN * PER_STEP)
    freq = (rows // SPAN * POINTS, d)
    return pl.pallas_call(
        forward_kernel,
        grid=(steps,),
        out_shape=(
            sds((rows, d), BF16),
            sds((rows, d), BF16),
            sds((rows, d), BF16),
            sds(freq, BF16),
            sds((rows, d), F32),
            sds((3 * HALF, d), F32),
            sds((8, 128), F32),
        ),
        in_specs=[SMEM, whole(frames.shape), whole(gain.shape), whole(w_in.shape)]
        + [whole(v.shape) for v in (high, low, high_t, low_t, taps_to, w_dw)],
        out_specs=(
            rows_of((rows, d), steps),
            rows_of((rows, d), steps),
            rows_of((rows, d), steps),
            rows_of(freq, steps),
            rows_of((rows, d), steps),
            whole((3 * HALF, d)),
            whole((8, 128)),
        ),
        scratch_shapes=[pltpu.VMEM((2, 8, d), F32)],
        compiler_params=params(),
        name="forward",
        cost_estimate=cost(10e9, 16 * rows * d),
    )(table, frames, gain, w_in, high, low, high_t, low_t, taps_to, w_dw)


def project(table, dy, w_out):
    rows, d = dy.shape
    steps = rows // (SPAN * PER_STEP)
    part = rows_of((rows, d), steps)
    return pl.pallas_call(
        project_kernel,
        grid=(steps,),
        out_shape=(sds((rows, d), BF16), sds((rows, d), F32)),
        in_specs=[SMEM, part, whole(w_out.shape)],
        out_specs=(part, part),
        compiler_params=params(),
        name="project",
        cost_estimate=cost(3e9, 6 * rows * d),
    )(table, dy, w_out)


def middle(total, conv, grad, stats, bn_gain, bn_bias, copies):
    rows, d = conv.shape
    steps = rows // (SPAN * PER_STEP)
    part = rows_of((rows, d), steps)
    tiles = (copies, 8, 128)
    return pl.pallas_call(
        functools.partial(middle_kernel, total),
        grid=(steps,),
        out_shape=(sds((rows, d), BF16), sds((rows, d), F32), sds(tiles, F32), sds((8, 128), F32)),
        in_specs=[part, part] + [whole(v.shape) for v in (stats, bn_gain, bn_bias)],
        out_specs=(part, part, whole(tiles), whole((8, 128))),
        scratch_shapes=[pltpu.VMEM((2, 8, d), F32)],
        compiler_params=params(),
        name="middle",
        cost_estimate=cost(4e9, 10 * rows * d),
    )(conv, grad, stats, bn_gain, bn_bias)


def outputs(swished, dy, w_out):
    rows, d = swished.shape
    steps = rows // (SPAN * PER_STEP)
    part = rows_of((rows, d), steps)
    half = (d // 2, d)
    return pl.pallas_call(
        output_kernel,
        grid=(steps,),
        out_shape=(sds((rows, d), BF16), sds(half, BF16), sds(half, BF16)),
        in_specs=[part, part, whole(w_out.shape)],
        out_specs=(part, whole(half), whole(half)),
        scratch_shapes=[pltpu.VMEM((rows, d), BF16), pltpu.VMEM((rows, d), BF16)],
        compiler_params=params(),
        name="outputs",
        cost_estimate=cost(4e9, 6 * rows * d),
    )(swished, dy, w_out)


def backward(total, table, h, slope, sig, freq, conv, gbn, wf, stats, sums, bn_gain, theirs, own, tabs):
    high, low, high_t, low_t, _, back = tabs
    rows, d = h.shape
    width = 3 * d + back.shape[1]
    steps = rows // (SPAN * PER_STEP)
    part = rows_of((rows, d), steps)
    return pl.pallas_call(
        functools.partial(backward_kernel, total),
        grid=(steps,),
        out_shape=(
            sds((rows, 2 * d), BF16),
            sds((d // 2, width), BF16),
            sds((d // 2, width), BF16),
            sds((1, d), F32),
            sds((1, d), F32),
        ),
        in_specs=[SMEM, part, part, part, rows_of(freq.shape, steps), part, part]
        + [whole(v.shape) for v in (wf, stats, sums, bn_gain, theirs, own, high, low, high_t, low_t, back)],
        out_specs=(
            rows_of((rows, 2 * d), steps),
            whole((d // 2, width)),
            whole((d // 2, width)),
            whole((1, d)),
            whole((1, d)),
        ),
        scratch_shapes=[
            pltpu.VMEM((2 * HALF, d), F32),
            pltpu.VMEM((rows, d), BF16),
            pltpu.VMEM((rows, 2 * d), BF16),
        ],
        compiler_params=params(),
        name="backward",
        cost_estimate=cost(8e9, 18 * rows * d),
    )(table, h, slope, sig, freq, conv, gbn, wf, stats, sums, bn_gain, theirs, own, high, low, high_t, low_t, back)


def inputs_back(table, frames, grad_a, gain, w_in):
    rows, d = frames.shape
    steps = rows // (SPAN * PER_STEP)
    return pl.pallas_call(
        inputs_kernel,
        grid=(steps,),
        out_shape=sds((rows, d), BF16),
        in_specs=[SMEM, whole(frames.shape), rows_of(grad_a.shape, steps), whole(gain.shape), whole(w_in.shape)],
        out_specs=whole((rows, d)),
        compiler_params=params(),
        name="inputs_back",
        cost_estimate=cost(6e9, 12 * rows * d),
    )(table, frames, grad_a, gain, w_in)


def pair_sum(own, got):
    rows, width = own.shape
    part = pl.BlockSpec((rows // 2, width), lambda i: (i, 0))
    return pl.pallas_call(
        pair_kernel,
        grid=(2,),
        out_shape=sds((rows, width), BF16),
        in_specs=[part, part],
        out_specs=part,
        compiler_params=pltpu.CompilerParams(vmem_limit_bytes=VMEM_LIMIT),
        name="pair_sum",
        cost_estimate=cost(2 * rows * width, 6 * rows * width),
    )(own, got)


def collect(got, count):
    vmem = pl.BlockSpec(memory_space=pltpu.VMEM)
    return pl.pallas_call(
        collect_kernel,
        out_shape=sds((count, *got.shape[1:]), BF16),
        in_specs=[vmem],
        out_specs=vmem,
        compiler_params=pltpu.CompilerParams(vmem_limit_bytes=SMALL_LIMIT),
        name="collect",
    )(got)


def finish(every, w_rows, gain_rows, taps):
    share, width = w_rows.shape
    d = width // 2
    vmem = pl.BlockSpec(memory_space=pltpu.VMEM)
    return pl.pallas_call(
        finish_kernel,
        out_shape=(sds((share, width), F32), sds((share, d), F32), sds((share, taps), F32), sds((1, share), F32)),
        in_specs=[vmem] * 3,
        out_specs=(vmem,) * 4,
        compiler_params=pltpu.CompilerParams(vmem_limit_bytes=SMALL_LIMIT),
        name="finish",
    )(every, w_rows, gain_rows)


def swapped(value, axes):
    return lax.all_to_all(value, axes, split_axis=0, concat_axis=0, tiled=True)


def over_bucket(theirs, own, ahead, beside):
    width = own.shape[1]
    both = pair_sum(own, lax.ppermute(theirs, "c", [(0, 1), (1, 0)]))
    both, ahead = lax.optimization_barrier((both, ahead))
    got = swapped(both.reshape(lax.axis_size("x"), -1, width), "x")
    got, beside = lax.optimization_barrier((got, beside))
    return swapped(collect(got, 1).reshape(lax.axis_size("z"), -1, width), "z"), ahead, beside


def local(frames, lengths, owners, upstream, ln_gain, w_in, w_dw, bn_gain, bn_bias, w_out):
    loaders = lax.axis_size(BUCKET)
    me = lax.axis_index(BUCKET)
    rows, d = frames.shape
    taps = w_dw.shape[1]
    share = d // loaders
    total = float(upstream.shape[0] * loaders * lax.axis_size(DP))
    tabs = tuple(jnp.asarray(v) for v in tables(taps))
    w_rows = lax.dynamic_slice_in_dim(w_in, me * share, share, 0)
    gain_rows = lax.dynamic_slice_in_dim(ln_gain, me * share, share, 0).reshape(1, share)
    gain, bn_gain, bn_bias = (v.reshape(1, d) for v in (ln_gain, bn_gain, bn_bias))

    dy, table = unpack(lengths, owners, upstream, loaders)
    dy = swapped(dy.reshape(loaders, SPAN, d), BUCKET).reshape(rows, d)
    h, slope, sig, freq, conv, wf, stats = forward(table, frames, gain, w_in, w_dw, tabs)
    stats = lax.psum(lax.psum(lax.psum(stats, "c"), "y"), "x")
    stats, dy = lax.optimization_barrier((stats, dy))
    stats = swapped(jnp.broadcast_to(stats, (lax.axis_size("z"), *stats.shape)), "z")
    live_dy, grad = project(table, dy, w_out)
    swished, gbn, sums, stats = middle(total, conv, grad, stats, bn_gain, bn_bias, lax.axis_size(("c", "z")))
    sums = jnp.sum(swapped(sums, ("c", "z")), axis=0)
    out, theirs, own = outputs(swished, live_dy, w_out)
    out, sums = lax.optimization_barrier((out, sums))
    out = swapped(out.reshape(loaders, SPAN, d), BUCKET).reshape(rows, d)
    sums = lax.psum(lax.psum(sums, "y"), "x")
    grad_a, theirs, own, bias_total, gain_total = backward(
        total, table, h, slope, sig, freq, conv, gbn, wf, stats, sums, bn_gain, theirs, own, tabs
    )
    gframes = inputs_back(table, frames, grad_a, gain, w_in)
    got, out, gframes = over_bucket(theirs, own, out, gframes)
    out_frames = pack(table, out, upstream.shape[0])
    got, out_frames = lax.optimization_barrier((got, out_frames))
    every = swapped(collect(got, lax.axis_size(DP)), DP)
    gwin, gwout, gwdw, gln = finish(every, w_rows, gain_rows, taps)
    return (
        out_frames,
        gframes,
        gwin,
        gwout,
        gwdw,
        gln.reshape(share),
        gain_total.reshape(d),
        bias_total.reshape(d),
    )


def solution(mesh):
    torus = Mesh(mesh.devices.reshape(4, 2, 4, 8), ("y", "c", "x", "z"))
    in_specs = (P(EVERY, None), P(DP, None), P(DP, None), P(EVERY, None)) + (P(),) * 6
    out_specs = (P(EVERY, None), P(EVERY, None), P(BUCKET, None), P(BUCKET, None), P(BUCKET, None), P(BUCKET), P(), P())
    return jax.shard_map(local, mesh=torus, in_specs=in_specs, out_specs=out_specs, check_vma=False)
```

```python
import functools
import math

import jax
import jax.numpy as jnp
import numpy as np
from jax import lax
from jax.experimental import pallas as pl
from jax.experimental.pallas import tpu as pltpu
from jax.sharding import Mesh
from jax.sharding import PartitionSpec as P

BUCKET = ("x", "z")
DP = ("y", "c")
EVERY = ("y", "c", "x", "z")


EPSILON = 1e-05
SPAN = 48
POINTS = 64
HALF = POINTS // 2
PER_DFT = 4
PER_STEP = 16
UNROLL = 4
VMEM_LIMIT = 60 * 2**20
SMALL_LIMIT = 16 * 2**20

F32 = jnp.float32
BF16 = jnp.bfloat16


def dot(a, b, dims=((1,), (0,)), precision=None):
    return lax.dot_general(a, b, (dims, ((), ())), preferred_element_type=F32, precision=precision)


def tables(taps):
    f = np.arange(HALF)[:, None]
    t = np.arange(SPAN)[None, :]
    angle = 2 * np.pi * f * t / POINTS
    real = np.cos(angle) * math.sqrt(2 / POINTS)
    imag = -np.sin(angle) * math.sqrt(2 / POINTS)
    real[0] = math.sqrt(1 / POINTS)
    imag[0] = math.sqrt(1 / POINTS) * (-1.0) ** np.arange(SPAN)
    block = np.zeros((2 * HALF * PER_DFT, SPAN * PER_DFT))
    for u in range(PER_DFT):
        block[u * HALF : (u + 1) * HALF, u * SPAN : (u + 1) * SPAN] = real
        block[(PER_DFT + u) * HALF : (PER_DFT + u + 1) * HALF, u * SPAN : (u + 1) * SPAN] = imag
    lag = np.arange(taps)[None, :] - taps // 2
    turn = 2 * np.pi * f * lag / POINTS
    cos, sin = np.cos(turn), np.sin(turn)
    cos_last = cos.copy()
    cos_last[0] = np.cos(np.pi * lag[0])
    taps_to = np.concatenate([cos, sin, cos_last], axis=0)
    back = np.zeros((2 * HALF, 128))
    back[:HALF, :taps] = cos
    back[HALF : 2 * HALF, :taps] = -sin
    back[HALF, :taps] = np.cos(np.pi * lag[0])
    high = block.astype(jnp.bfloat16)
    low = (block - high.astype(np.float64)).astype(jnp.bfloat16)
    return (
        high,
        low,
        np.ascontiguousarray(high.T),
        np.ascontiguousarray(low.T),
        taps_to.astype(np.float32),
        back.astype(np.float32),
    )


def masked(value, lens):
    t = lax.broadcasted_iota(jnp.int32, (SPAN, value.shape[1]), 0)
    return jnp.concatenate(
        [
            jnp.where(t < n, value[u * SPAN : (u + 1) * SPAN], jnp.zeros((), value.dtype))
            for u, n in enumerate(lens)
        ],
        axis=0,
    )


def folded(value):
    return jnp.sum(value.reshape(-1, 8, value.shape[1]), axis=0)


def as_tile(first, second):
    rows = [v[:, k * 128 : (k + 1) * 128] for v in (first, second) for k in range(4)]
    return jnp.concatenate(rows, axis=0)


def from_tile(tile):
    rows = [tile[k : k + 1] for k in range(8)]
    return (jnp.concatenate(rows[:4], axis=1), jnp.concatenate(rows[4:], axis=1))


def normalize(x, gain):
    centred = x - jnp.mean(x, axis=1, keepdims=True)
    inverse = lax.rsqrt(jnp.mean(centred * centred, axis=1, keepdims=True) + EPSILON)
    normed = centred * inverse
    return (normed * gain).astype(BF16), normed, inverse


def spread(wf, part):
    rows = wf[part * HALF : (part + 1) * HALF]
    return jnp.concatenate([rows] * PER_DFT, axis=0)


def unpack_kernel(lengths_ref, owners_ref, upstream_ref, out_ref, table_ref, wide, lens_all, dest_all, table, sem):
    loaders = lens_all.shape[0]
    me = lax.axis_index(BUCKET)
    for k in range(loaders):
        lens_all[k : k + 1, :] = lengths_ref[:, k * loaders : (k + 1) * loaders]
        dest_all[k : k + 1, :] = owners_ref[:, k * loaders : (k + 1) * loaders]
    got = jnp.sum(jnp.where(dest_all[...] == me, lens_all[...], 0), axis=1, keepdims=True)
    square = (loaders, loaders)
    hit = dest_all[pl.ds(me, 1), :] == lax.broadcasted_iota(jnp.int32, square, 0)
    lens = jnp.sum(jnp.where(hit, lens_all[pl.ds(me, 1), :], 0), axis=1, keepdims=True)
    slots = jnp.sum(jnp.where(hit, lax.broadcasted_iota(jnp.int32, square, 1), 0), axis=1, keepdims=True)
    column = lax.broadcasted_iota(jnp.int32, table_ref.shape, 1)
    table_ref[...] = jnp.where(column == 0, got, jnp.where(column == 1, lens, slots))
    copy = pltpu.make_async_copy(table_ref, table, sem)
    copy.start()
    rows = upstream_ref.shape[0]
    wide[:rows, :] = upstream_ref[...].astype(F32)
    wide[rows:, :] = jnp.zeros((8, wide.shape[1]), F32)
    copy.wait()

    def step(group, start):
        for i in (group * UNROLL + k for k in range(UNROLL)):
            base = pl.multiple_of(start // 8 * 8, 8)
            window = pltpu.roll(wide[pl.ds(base, SPAN + 8), :], SPAN + 8 - start % 8, 0)
            out_ref[pl.ds(pl.multiple_of(i * SPAN, 16), SPAN), :] = window[:SPAN].astype(BF16)
            start += table[i, 0]
        return start

    lax.fori_loop(0, loaders // UNROLL, step, jnp.int32(0))


def pack_kernel(table_ref, got_ref, out_ref, wide):
    count = got_ref.shape[0] // SPAN
    top = lax.broadcasted_iota(jnp.int32, (8, got_ref.shape[1]), 0)

    def step(i, start):
        base = pl.multiple_of(start // 8 * 8, 8)
        rows = got_ref[pl.ds(pl.multiple_of(i * SPAN, 16), SPAN), :].astype(F32)
        window = jnp.concatenate([rows, jnp.zeros((8, rows.shape[1]), F32)], axis=0)
        window = pltpu.roll(window, start % 8, 0)
        kept = jnp.where(top < start % 8, wide[pl.ds(base, 8), :], window[:8])
        wide[pl.ds(base, 8), :] = kept
        wide[pl.ds(base + 8, SPAN), :] = window[8:]
        return start + table_ref[i, 0]

    lax.fori_loop(0, count, step, jnp.int32(0))
    out_ref[...] = wide[: out_ref.shape[0], :].astype(BF16)


def step_lens(table_ref):
    return [table_ref[pl.program_id(0) * PER_STEP + u, 1] for u in range(PER_STEP)]


def slot_rows(table_ref, u):
    slot = table_ref[pl.program_id(0) * PER_STEP + u, 2]
    return pl.ds(pl.multiple_of(slot * SPAN, 16), SPAN)


def forward_kernel(
    table_ref, frames_ref, gain_ref, win_ref, qh_ref, ql_ref, ih_ref, il_ref, to_ref, wdw_ref,
    h_ref, slope_ref, sig_ref, freq_ref, conv_ref, wf_ref, stats_ref, acc,
):
    step = pl.program_id(0)

    @pl.when(step == 0)
    def _():
        wf_ref[...] = dot(to_ref[...], wdw_ref[...], ((1,), (1,)), lax.Precision.HIGHEST)
        acc[...] = jnp.zeros_like(acc)

    d = frames_ref.shape[1]
    lens = step_lens(table_ref)
    x = jnp.concatenate([frames_ref[slot_rows(table_ref, u), :] for u in range(PER_STEP)], axis=0)
    h, _, _ = normalize(x.astype(F32), gain_ref[...])
    h_ref[...] = h
    a = dot(h, win_ref[...])
    lin = a[:, :d]
    sig = jax.nn.sigmoid(a[:, d:])
    slope_ref[...] = (lin * sig * (1.0 - sig)).astype(BF16)
    sig_ref[...] = sig.astype(BF16)
    gated = masked(lin * sig, lens).astype(BF16)
    wa, wb, wl = (spread(wf_ref[...], k) for k in range(3))
    for b in range(PER_STEP // PER_DFT):
        rows = slice(b * SPAN * PER_DFT, (b + 1) * SPAN * PER_DFT)
        part = gated[rows]
        spec = dot(qh_ref[...], part) + dot(ql_ref[...], part)
        freq_ref[b * POINTS * PER_DFT : (b + 1) * POINTS * PER_DFT, :] = spec.astype(BF16)
        re, im = spec[: HALF * PER_DFT], spec[HALF * PER_DFT :]
        turned = jnp.concatenate([re * wa - im * wb, im * wl + re * wb], axis=0)
        high = turned.astype(BF16)
        low = (turned - high.astype(F32)).astype(BF16)
        conv = dot(ih_ref[...], high) + dot(il_ref[...], high) + dot(ih_ref[...], low)
        conv_ref[rows, :] = conv
        live = masked(conv, lens[b * PER_DFT : (b + 1) * PER_DFT])
        acc[0] += folded(live)
        acc[1] += folded(live * live)

    @pl.when(step == pl.num_programs(0) - 1)
    def _():
        sums = [jnp.sum(acc[k], axis=0, keepdims=True) for k in range(2)]
        stats_ref[...] = as_tile(*sums)


def split(value, theirs_ref, own_ref):
    blocks = value.reshape(-1, 2, 8, value.shape[1])
    first = lax.axis_index("c") == 0
    low, high = blocks[:, 0], blocks[:, 1]
    theirs_ref[...] = jnp.where(first, high, low).reshape(theirs_ref.shape).astype(BF16)
    own_ref[...] = jnp.where(first, low, high).reshape(own_ref.shape).astype(BF16)


def bn_terms(stats, total):
    first, second = from_tile(stats)
    centre = first / total
    inverse = lax.rsqrt(second / total - centre * centre + EPSILON)
    return centre, inverse


def project_kernel(table_ref, dy_ref, wout_ref, live_dy_ref, grad_ref):
    dy = masked(dy_ref[...].astype(F32), step_lens(table_ref)).astype(BF16)
    live_dy_ref[...] = dy
    grad_ref[...] = dot(dy, wout_ref[...], ((1,), (1,)))


def middle_kernel(
    total, conv_ref, grad_ref, stats_ref, gain_ref, bias_ref,
    swished_ref, gbn_ref, sums_ref, moments_ref, acc,
):
    step = pl.program_id(0)

    @pl.when(step == 0)
    def _():
        acc[...] = jnp.zeros_like(acc)
        moments_ref[...] = jnp.sum(stats_ref[...], axis=0)

    centre, inverse = bn_terms(moments_ref[...], total)
    normed = (conv_ref[...] - centre) * inverse
    value = normed * gain_ref[...] + bias_ref[...]
    sig = jax.nn.sigmoid(value)
    swished_ref[...] = (value * sig).astype(BF16)
    grad = grad_ref[...] * (sig * (1.0 + value * (1.0 - sig)))
    gbn_ref[...] = grad
    acc[0] += folded(grad)
    acc[1] += folded(grad * normed)

    @pl.when(step == pl.num_programs(0) - 1)
    def _():
        sums = [jnp.sum(acc[k], axis=0, keepdims=True) for k in range(2)]
        sums_ref[...] = jnp.broadcast_to(as_tile(*sums)[None], sums_ref.shape)


def output_kernel(swished_ref, dy_ref, wout_ref, out_ref, theirs_ref, own_ref, sw_all, dy_all):
    step = pl.program_id(0)
    out_ref[...] = dot(swished_ref[...], wout_ref[...]).astype(BF16)
    rows = pl.ds(pl.multiple_of(step * PER_STEP * SPAN, 16), PER_STEP * SPAN)
    sw_all[rows, :] = swished_ref[...]
    dy_all[rows, :] = dy_ref[...]

    @pl.when(step == pl.num_programs(0) - 1)
    def _():
        split(dot(sw_all[...], dy_all[...], ((0,), (0,))), theirs_ref, own_ref)


def backward_kernel(
    total, table_ref, h_ref, slope_ref, sig_ref, freq_ref, conv_ref, gbn_ref, wf_ref, stats_ref, sums_ref,
    bn_gain_ref, theirs_in, own_in, qh_ref, ql_ref, ih_ref, il_ref, back_ref,
    grad_a_ref, theirs_ref, own_ref, bias_ref, bn_out_ref, acc, h_all, ga_all,
):
    step = pl.program_id(0)

    @pl.when(step == 0)
    def _():
        acc[...] = jnp.zeros_like(acc)

    lens = step_lens(table_ref)
    centre, inverse = bn_terms(stats_ref[...], total)
    bias_total, gain_total = from_tile(sums_ref[...])
    bias_ref[...] = bias_total
    bn_out_ref[...] = gain_total
    normed_bn = (conv_ref[...] - centre) * inverse
    scale = bn_gain_ref[...] * inverse
    grad_conv = scale * (gbn_ref[...] - bias_total / total - normed_bn * (gain_total / total))
    grad_conv = masked(grad_conv, lens).astype(BF16)
    wa, wb, wl = (spread(wf_ref[...], k) for k in range(3))
    n = HALF * PER_DFT
    edge = lax.broadcasted_iota(jnp.int32, (n, wa.shape[1]), 0) % HALF == 0
    parts = []
    for b in range(PER_STEP // PER_DFT):
        rows = slice(b * SPAN * PER_DFT, (b + 1) * SPAN * PER_DFT)
        spec = dot(qh_ref[...], grad_conv[rows]) + dot(ql_ref[...], grad_conv[rows])
        re, im = spec[:n], spec[n:]
        own = freq_ref[b * 2 * n : (b + 1) * 2 * n, :].astype(F32)
        own_re, own_im = own[:n], own[n:]
        both = im * own_im
        corr_re = re * own_re + jnp.where(edge, 0.0, both)
        corr_im = jnp.where(edge, both, re * own_im - im * own_re)
        acc[:HALF] += jnp.sum(corr_re.reshape(PER_DFT, HALF, -1), axis=0)
        acc[HALF:] += jnp.sum(corr_im.reshape(PER_DFT, HALF, -1), axis=0)
        turned = jnp.concatenate([re * wa + im * wb, im * wl - re * wb], axis=0).astype(BF16)
        parts.append(dot(ih_ref[...], turned) + dot(il_ref[...], turned))
    grad_gated = masked(jnp.concatenate(parts, axis=0), lens)
    grad_a = jnp.concatenate([grad_gated * s[...].astype(F32) for s in (sig_ref, slope_ref)], axis=1).astype(BF16)
    grad_a_ref[...] = grad_a
    rows = pl.ds(pl.multiple_of(step * PER_STEP * SPAN, 16), PER_STEP * SPAN)
    h_all[rows, :] = h_ref[...]
    ga_all[rows, :] = grad_a

    @pl.when(step == pl.num_programs(0) - 1)
    def _():
        d = h_all.shape[1]
        gwin, gwout, taps = slice(0, 2 * d), slice(2 * d, 3 * d), slice(3 * d, theirs_ref.shape[1])
        theirs_ref[:, gwout] = theirs_in[...]
        own_ref[:, gwout] = own_in[...]
        small = dot(acc[...], back_ref[...], ((0,), (0,)), lax.Precision.HIGHEST)
        split(small, theirs_ref.at[:, taps], own_ref.at[:, taps])
        split(dot(h_all[...], ga_all[...], ((0,), (0,))), theirs_ref.at[:, gwin], own_ref.at[:, gwin])


def inputs_kernel(table_ref, frames_ref, grad_a_ref, gain_ref, win_ref, gframes_ref):
    grad_h = dot(grad_a_ref[...], win_ref[...], ((1,), (1,)))
    x = jnp.concatenate([frames_ref[slot_rows(table_ref, u), :] for u in range(PER_STEP)], axis=0)
    gain = gain_ref[...]
    _, normed, inv = normalize(x.astype(F32), gain)
    scaled = grad_h * gain
    inner = jnp.mean(scaled * normed, axis=1, keepdims=True)
    grad_x = inv * (scaled - jnp.mean(scaled, axis=1, keepdims=True) - normed * inner)
    grad_x = masked(grad_x, step_lens(table_ref)).astype(BF16)
    for u in range(PER_STEP):
        gframes_ref[slot_rows(table_ref, u), :] = grad_x[u * SPAN : (u + 1) * SPAN]


def pair_kernel(own_ref, got_ref, both_ref):
    both_ref[...] = (own_ref[...].astype(F32) + got_ref[...].astype(F32)).astype(BF16)


def collect_kernel(got_ref, out_ref):
    total = got_ref[0].astype(F32)
    for k in range(1, got_ref.shape[0]):
        total += got_ref[k].astype(F32)
    for k in range(out_ref.shape[0]):
        out_ref[k] = total.astype(BF16)


def finish_kernel(every_ref, w_ref, gain_ref, gwin_ref, gwout_ref, gwdw_ref, gln_ref):
    count = every_ref.shape[0]
    halves = [sum(every_ref[k].astype(F32) for k in range(core, count, 2)) for core in range(2)]
    rows = jnp.concatenate(halves, axis=0)
    d = gwout_ref.shape[1]
    gwin = rows[:, : 2 * d]
    gwin_ref[...] = gwin
    gwout_ref[...] = rows[:, 2 * d : 3 * d]
    gwdw_ref[...] = rows[:, 3 * d : 3 * d + gwdw_ref.shape[1]]
    ones = jnp.ones((8, 2 * d), F32)
    dots = dot(ones, gwin * w_ref[...].astype(F32), ((1,), (1,)), lax.Precision.HIGHEST)
    gln_ref[...] = dots[:1] / gain_ref[...]


SMEM = pl.BlockSpec(memory_space=pltpu.SMEM)


def whole(shape):
    return pl.BlockSpec(shape, lambda i: (0,) * len(shape))


def rows_of(shape, steps):
    return pl.BlockSpec((shape[0] // steps, shape[1]), lambda i: (i, 0))


def cost(flops, moved):
    return pl.CostEstimate(flops=int(flops), bytes_accessed=int(moved), transcendentals=0)


def params():
    return pltpu.CompilerParams(dimension_semantics=("arbitrary",), vmem_limit_bytes=VMEM_LIMIT)


def sds(shape, dtype):
    return jax.ShapeDtypeStruct(shape, dtype)


def unpack(lengths, owners, upstream, loaders):
    rows, d = upstream.shape
    vmem = pl.BlockSpec(memory_space=pltpu.VMEM)
    return pl.pallas_call(
        unpack_kernel,
        out_shape=(sds((loaders * SPAN, d), BF16), sds((loaders, 128), jnp.int32)),
        in_specs=[vmem] * 3,
        out_specs=(vmem, vmem),
        scratch_shapes=[
            pltpu.VMEM((rows + 8, d), F32),
            pltpu.VMEM((loaders, loaders), jnp.int32),
            pltpu.VMEM((loaders, loaders), jnp.int32),
            pltpu.SMEM((loaders, 128), jnp.int32),
            pltpu.SemaphoreType.DMA,
        ],
        compiler_params=pltpu.CompilerParams(vmem_limit_bytes=VMEM_LIMIT),
        name="unpack",
        cost_estimate=cost(1e9, 6 * rows * d),
    )(lengths, owners, upstream)


def pack(table, got, rows):
    return pl.pallas_call(
        pack_kernel,
        out_shape=sds((rows, got.shape[1]), BF16),
        in_specs=[SMEM, pl.BlockSpec(memory_space=pltpu.VMEM)],
        out_specs=pl.BlockSpec(memory_space=pltpu.VMEM),
        scratch_shapes=[pltpu.VMEM((rows + 8, got.shape[1]), F32)],
        compiler_params=pltpu.CompilerParams(vmem_limit_bytes=VMEM_LIMIT),
        name="pack",
        cost_estimate=cost(2e9, 6 * rows * got.shape[1]),
    )(table, got)


def forward(table, frames, gain, w_in, w_dw, tabs):
    high, low, high_t, low_t, taps_to, _ = tabs
    rows, d = frames.shape
    steps = rows // (SPAN * PER_STEP)
    freq = (rows // SPAN * POINTS, d)
    return pl.pallas_call(
        forward_kernel,
        grid=(steps,),
        out_shape=(
            sds((rows, d), BF16),
            sds((rows, d), BF16),
            sds((rows, d), BF16),
            sds(freq, BF16),
            sds((rows, d), F32),
            sds((3 * HALF, d), F32),
            sds((8, 128), F32),
        ),
        in_specs=[SMEM, whole(frames.shape), whole(gain.shape), whole(w_in.shape)]
        + [whole(v.shape) for v in (high, low, high_t, low_t, taps_to, w_dw)],
        out_specs=(
            rows_of((rows, d), steps),
            rows_of((rows, d), steps),
            rows_of((rows, d), steps),
            rows_of(freq, steps),
            rows_of((rows, d), steps),
            whole((3 * HALF, d)),
            whole((8, 128)),
        ),
        scratch_shapes=[pltpu.VMEM((2, 8, d), F32)],
        compiler_params=params(),
        name="forward",
        cost_estimate=cost(10e9, 16 * rows * d),
    )(table, frames, gain, w_in, high, low, high_t, low_t, taps_to, w_dw)


def project(table, dy, w_out):
    rows, d = dy.shape
    steps = rows // (SPAN * PER_STEP)
    part = rows_of((rows, d), steps)
    return pl.pallas_call(
        project_kernel,
        grid=(steps,),
        out_shape=(sds((rows, d), BF16), sds((rows, d), F32)),
        in_specs=[SMEM, part, whole(w_out.shape)],
        out_specs=(part, part),
        compiler_params=params(),
        name="project",
        cost_estimate=cost(3e9, 6 * rows * d),
    )(table, dy, w_out)


def middle(total, conv, grad, stats, bn_gain, bn_bias, copies):
    rows, d = conv.shape
    steps = rows // (SPAN * PER_STEP)
    part = rows_of((rows, d), steps)
    tiles = (copies, 8, 128)
    return pl.pallas_call(
        functools.partial(middle_kernel, total),
        grid=(steps,),
        out_shape=(sds((rows, d), BF16), sds((rows, d), F32), sds(tiles, F32), sds((8, 128), F32)),
        in_specs=[part, part] + [whole(v.shape) for v in (stats, bn_gain, bn_bias)],
        out_specs=(part, part, whole(tiles), whole((8, 128))),
        scratch_shapes=[pltpu.VMEM((2, 8, d), F32)],
        compiler_params=params(),
        name="middle",
        cost_estimate=cost(4e9, 10 * rows * d),
    )(conv, grad, stats, bn_gain, bn_bias)


def outputs(swished, dy, w_out):
    rows, d = swished.shape
    steps = rows // (SPAN * PER_STEP)
    part = rows_of((rows, d), steps)
    half = (d // 2, d)
    return pl.pallas_call(
        output_kernel,
        grid=(steps,),
        out_shape=(sds((rows, d), BF16), sds(half, BF16), sds(half, BF16)),
        in_specs=[part, part, whole(w_out.shape)],
        out_specs=(part, whole(half), whole(half)),
        scratch_shapes=[pltpu.VMEM((rows, d), BF16), pltpu.VMEM((rows, d), BF16)],
        compiler_params=params(),
        name="outputs",
        cost_estimate=cost(4e9, 6 * rows * d),
    )(swished, dy, w_out)


def backward(total, table, h, slope, sig, freq, conv, gbn, wf, stats, sums, bn_gain, theirs, own, tabs):
    high, low, high_t, low_t, _, back = tabs
    rows, d = h.shape
    width = 3 * d + back.shape[1]
    steps = rows // (SPAN * PER_STEP)
    part = rows_of((rows, d), steps)
    return pl.pallas_call(
        functools.partial(backward_kernel, total),
        grid=(steps,),
        out_shape=(
            sds((rows, 2 * d), BF16),
            sds((d // 2, width), BF16),
            sds((d // 2, width), BF16),
            sds((1, d), F32),
            sds((1, d), F32),
        ),
        in_specs=[SMEM, part, part, part, rows_of(freq.shape, steps), part, part]
        + [whole(v.shape) for v in (wf, stats, sums, bn_gain, theirs, own, high, low, high_t, low_t, back)],
        out_specs=(
            rows_of((rows, 2 * d), steps),
            whole((d // 2, width)),
            whole((d // 2, width)),
            whole((1, d)),
            whole((1, d)),
        ),
        scratch_shapes=[
            pltpu.VMEM((2 * HALF, d), F32),
            pltpu.VMEM((rows, d), BF16),
            pltpu.VMEM((rows, 2 * d), BF16),
        ],
        compiler_params=params(),
        name="backward",
        cost_estimate=cost(8e9, 18 * rows * d),
    )(table, h, slope, sig, freq, conv, gbn, wf, stats, sums, bn_gain, theirs, own, high, low, high_t, low_t, back)


def inputs_back(table, frames, grad_a, gain, w_in):
    rows, d = frames.shape
    steps = rows // (SPAN * PER_STEP)
    return pl.pallas_call(
        inputs_kernel,
        grid=(steps,),
        out_shape=sds((rows, d), BF16),
        in_specs=[SMEM, whole(frames.shape), rows_of(grad_a.shape, steps), whole(gain.shape), whole(w_in.shape)],
        out_specs=whole((rows, d)),
        compiler_params=params(),
        name="inputs_back",
        cost_estimate=cost(6e9, 12 * rows * d),
    )(table, frames, grad_a, gain, w_in)


def pair_sum(own, got):
    rows, width = own.shape
    part = pl.BlockSpec((rows // 2, width), lambda i: (i, 0))
    return pl.pallas_call(
        pair_kernel,
        grid=(2,),
        out_shape=sds((rows, width), BF16),
        in_specs=[part, part],
        out_specs=part,
        compiler_params=pltpu.CompilerParams(vmem_limit_bytes=SMALL_LIMIT),
        name="pair_sum",
        cost_estimate=cost(2 * rows * width, 6 * rows * width),
    )(own, got)


def collect(got, count):
    vmem = pl.BlockSpec(memory_space=pltpu.VMEM)
    return pl.pallas_call(
        collect_kernel,
        out_shape=sds((count, *got.shape[1:]), BF16),
        in_specs=[vmem],
        out_specs=vmem,
        compiler_params=pltpu.CompilerParams(vmem_limit_bytes=SMALL_LIMIT),
        name="collect",
    )(got)


def finish(every, w_rows, gain_rows, taps):
    share, width = w_rows.shape
    d = width // 2
    vmem = pl.BlockSpec(memory_space=pltpu.VMEM)
    return pl.pallas_call(
        finish_kernel,
        out_shape=(sds((share, width), F32), sds((share, d), F32), sds((share, taps), F32), sds((1, share), F32)),
        in_specs=[vmem] * 3,
        out_specs=(vmem,) * 4,
        compiler_params=pltpu.CompilerParams(vmem_limit_bytes=SMALL_LIMIT),
        name="finish",
    )(every, w_rows, gain_rows)


def swapped(value, axes):
    return lax.all_to_all(value, axes, split_axis=0, concat_axis=0, tiled=True)


def over_bucket(theirs, own, loaders, ahead):
    got = lax.ppermute(theirs, "c", [(0, 1), (1, 0)])
    both = pair_sum(own, got).reshape(loaders, -1, own.shape[1])
    both, ahead = lax.optimization_barrier((both, ahead))
    return swapped(both, BUCKET), ahead


def local(frames, lengths, owners, upstream, ln_gain, w_in, w_dw, bn_gain, bn_bias, w_out):
    loaders = lax.axis_size(BUCKET)
    me = lax.axis_index(BUCKET)
    rows, d = frames.shape
    taps = w_dw.shape[1]
    share = d // loaders
    total = float(upstream.shape[0] * loaders * lax.axis_size(DP))
    tabs = tuple(jnp.asarray(v) for v in tables(taps))
    w_rows = lax.dynamic_slice_in_dim(w_in, me * share, share, 0)
    gain_rows = lax.dynamic_slice_in_dim(ln_gain, me * share, share, 0).reshape(1, share)
    gain, bn_gain, bn_bias = (v.reshape(1, d) for v in (ln_gain, bn_gain, bn_bias))

    dy, table = unpack(lengths, owners, upstream, loaders)
    dy = swapped(dy.reshape(loaders, SPAN, d), BUCKET).reshape(rows, d)
    h, slope, sig, freq, conv, wf, stats = forward(table, frames, gain, w_in, w_dw, tabs)
    stats = lax.psum(lax.psum(lax.psum(stats, "c"), "y"), "x")
    stats, dy = lax.optimization_barrier((stats, dy))
    stats = swapped(jnp.broadcast_to(stats, (lax.axis_size("z"), *stats.shape)), "z")
    live_dy, grad = project(table, dy, w_out)
    swished, gbn, sums, stats = middle(total, conv, grad, stats, bn_gain, bn_bias, lax.axis_size(("c", "z")))
    sums = jnp.sum(swapped(sums, ("c", "z")), axis=0)
    out, theirs, own = outputs(swished, live_dy, w_out)
    out, sums = lax.optimization_barrier((out, sums))
    out = swapped(out.reshape(loaders, SPAN, d), BUCKET).reshape(rows, d)
    sums = lax.psum(lax.psum(sums, "y"), "x")
    grad_a, theirs, own, bias_total, gain_total = backward(
        total, table, h, slope, sig, freq, conv, gbn, wf, stats, sums, bn_gain, theirs, own, tabs
    )
    got, out = over_bucket(theirs, own, loaders, out)
    gframes = inputs_back(table, frames, grad_a, gain, w_in)
    out_frames = pack(table, out, upstream.shape[0])
    got, gframes, out_frames = lax.optimization_barrier((got, gframes, out_frames))
    every = swapped(collect(got, lax.axis_size(DP)), DP)
    gwin, gwout, gwdw, gln = finish(every, w_rows, gain_rows, taps)
    return (
        out_frames,
        gframes,
        gwin,
        gwout,
        gwdw,
        gln.reshape(share),
        gain_total.reshape(d),
        bias_total.reshape(d),
    )


def solution(mesh):
    torus = Mesh(mesh.devices.reshape(4, 2, 4, 8), ("y", "c", "x", "z"))
    in_specs = (P(EVERY, None), P(DP, None), P(DP, None), P(EVERY, None)) + (P(),) * 6
    out_specs = (P(EVERY, None), P(EVERY, None), P(BUCKET, None), P(BUCKET, None), P(BUCKET, None), P(BUCKET), P(), P())
    return jax.shard_map(local, mesh=torus, in_specs=in_specs, out_specs=out_specs, check_vma=False)
```

```python
import functools
import math

import jax
import jax.numpy as jnp
import numpy as np
from jax import lax
from jax.experimental import pallas as pl
from jax.experimental.pallas import tpu as pltpu
from jax.sharding import Mesh
from jax.sharding import PartitionSpec as P

BUCKET = ("x", "z")
DP = ("y", "c")
EVERY = ("y", "c", "x", "z")


EPSILON = 1e-05
SPAN = 48
POINTS = 64
HALF = POINTS // 2
PER_DFT = 4
PER_STEP = 16
UNROLL = 8
VMEM_LIMIT = 60 * 2**20
SMALL_LIMIT = 16 * 2**20

F32 = jnp.float32
BF16 = jnp.bfloat16


def dot(a, b, dims=((1,), (0,)), precision=None):
    return lax.dot_general(a, b, (dims, ((), ())), preferred_element_type=F32, precision=precision)


def tables(taps):
    f = np.arange(HALF)[:, None]
    t = np.arange(SPAN)[None, :]
    angle = 2 * np.pi * f * t / POINTS
    real = np.cos(angle) * math.sqrt(2 / POINTS)
    imag = -np.sin(angle) * math.sqrt(2 / POINTS)
    real[0] = math.sqrt(1 / POINTS)
    imag[0] = math.sqrt(1 / POINTS) * (-1.0) ** np.arange(SPAN)
    block = np.zeros((2 * HALF * PER_DFT, SPAN * PER_DFT))
    for u in range(PER_DFT):
        block[u * HALF : (u + 1) * HALF, u * SPAN : (u + 1) * SPAN] = real
        block[(PER_DFT + u) * HALF : (PER_DFT + u + 1) * HALF, u * SPAN : (u + 1) * SPAN] = imag
    lag = np.arange(taps)[None, :] - taps // 2
    turn = 2 * np.pi * f * lag / POINTS
    cos, sin = np.cos(turn), np.sin(turn)
    cos_last = cos.copy()
    cos_last[0] = np.cos(np.pi * lag[0])
    taps_to = np.concatenate([cos, sin, cos_last], axis=0)
    back = np.zeros((2 * HALF, 128))
    back[:HALF, :taps] = cos
    back[HALF : 2 * HALF, :taps] = -sin
    back[HALF, :taps] = np.cos(np.pi * lag[0])
    high = block.astype(jnp.bfloat16)
    low = (block - high.astype(np.float64)).astype(jnp.bfloat16)
    return (
        high,
        low,
        np.ascontiguousarray(high.T),
        np.ascontiguousarray(low.T),
        taps_to.astype(np.float32),
        back.astype(np.float32),
    )


def masked(value, lens):
    t = lax.broadcasted_iota(jnp.int32, (SPAN, value.shape[1]), 0)
    return jnp.concatenate(
        [
            jnp.where(t < n, value[u * SPAN : (u + 1) * SPAN], jnp.zeros((), value.dtype))
            for u, n in enumerate(lens)
        ],
        axis=0,
    )


def folded(value):
    return jnp.sum(value.reshape(-1, 8, value.shape[1]), axis=0)


def as_tile(first, second):
    rows = [v[:, k * 128 : (k + 1) * 128] for v in (first, second) for k in range(4)]
    return jnp.concatenate(rows, axis=0)


def from_tile(tile):
    rows = [tile[k : k + 1] for k in range(8)]
    return (jnp.concatenate(rows[:4], axis=1), jnp.concatenate(rows[4:], axis=1))


def normalize(x, gain):
    centred = x - jnp.mean(x, axis=1, keepdims=True)
    inverse = lax.rsqrt(jnp.mean(centred * centred, axis=1, keepdims=True) + EPSILON)
    normed = centred * inverse
    return (normed * gain).astype(BF16), normed, inverse


def spread(wf, part):
    rows = wf[part * HALF : (part + 1) * HALF]
    return jnp.concatenate([rows] * PER_DFT, axis=0)


def unpack_kernel(lengths_ref, owners_ref, upstream_ref, out_ref, table_ref, wide, lens_all, dest_all, table, sem):
    loaders = lens_all.shape[0]
    me = lax.axis_index(BUCKET)
    for k in range(loaders):
        lens_all[k : k + 1, :] = lengths_ref[:, k * loaders : (k + 1) * loaders]
        dest_all[k : k + 1, :] = owners_ref[:, k * loaders : (k + 1) * loaders]
    got = jnp.sum(jnp.where(dest_all[...] == me, lens_all[...], 0), axis=1, keepdims=True)
    square = (loaders, loaders)
    hit = dest_all[pl.ds(me, 1), :] == lax.broadcasted_iota(jnp.int32, square, 0)
    lens = jnp.sum(jnp.where(hit, lens_all[pl.ds(me, 1), :], 0), axis=1, keepdims=True)
    slots = jnp.sum(jnp.where(hit, lax.broadcasted_iota(jnp.int32, square, 1), 0), axis=1, keepdims=True)
    column = lax.broadcasted_iota(jnp.int32, table_ref.shape, 1)
    table_ref[...] = jnp.where(column == 0, got, jnp.where(column == 1, lens, slots))
    copy = pltpu.make_async_copy(table_ref, table, sem)
    copy.start()
    rows = upstream_ref.shape[0]
    wide[:rows, :] = upstream_ref[...].astype(F32)
    wide[rows:, :] = jnp.zeros((8, wide.shape[1]), F32)
    copy.wait()

    def step(group, start):
        for i in (group * UNROLL + k for k in range(UNROLL)):
            base = pl.multiple_of(start // 8 * 8, 8)
            window = pltpu.roll(wide[pl.ds(base, SPAN + 8), :], SPAN + 8 - start % 8, 0)
            out_ref[pl.ds(pl.multiple_of(i * SPAN, 16), SPAN), :] = window[:SPAN].astype(BF16)
            start += table[i, 0]
        return start

    lax.fori_loop(0, loaders // UNROLL, step, jnp.int32(0))


def pack_kernel(table_ref, got_ref, out_ref, wide):
    count = got_ref.shape[0] // SPAN
    top = lax.broadcasted_iota(jnp.int32, (8, got_ref.shape[1]), 0)

    def step(i, start):
        base = pl.multiple_of(start // 8 * 8, 8)
        rows = got_ref[pl.ds(pl.multiple_of(i * SPAN, 16), SPAN), :].astype(F32)
        window = jnp.concatenate([rows, jnp.zeros((8, rows.shape[1]), F32)], axis=0)
        window = pltpu.roll(window, start % 8, 0)
        kept = jnp.where(top < start % 8, wide[pl.ds(base, 8), :], window[:8])
        wide[pl.ds(base, 8), :] = kept
        wide[pl.ds(base + 8, SPAN), :] = window[8:]
        return start + table_ref[i, 0]

    lax.fori_loop(0, count, step, jnp.int32(0))
    out_ref[...] = wide[: out_ref.shape[0], :].astype(BF16)


def step_lens(table_ref):
    return [table_ref[pl.program_id(0) * PER_STEP + u, 1] for u in range(PER_STEP)]


def slot_rows(table_ref, u):
    slot = table_ref[pl.program_id(0) * PER_STEP + u, 2]
    return pl.ds(pl.multiple_of(slot * SPAN, 16), SPAN)


def forward_kernel(
    table_ref, frames_ref, gain_ref, win_ref, qh_ref, ql_ref, ih_ref, il_ref, to_ref, wdw_ref,
    h_ref, slope_ref, sig_ref, freq_ref, conv_ref, wf_ref, stats_ref, acc,
):
    step = pl.program_id(0)

    @pl.when(step == 0)
    def _():
        wf_ref[...] = dot(to_ref[...], wdw_ref[...], ((1,), (1,)), lax.Precision.HIGHEST)
        acc[...] = jnp.zeros_like(acc)

    d = frames_ref.shape[1]
    lens = step_lens(table_ref)
    x = jnp.concatenate([frames_ref[slot_rows(table_ref, u), :] for u in range(PER_STEP)], axis=0)
    h, _, _ = normalize(x.astype(F32), gain_ref[...])
    h_ref[...] = h
    a = dot(h, win_ref[...])
    lin = a[:, :d]
    sig = jax.nn.sigmoid(a[:, d:])
    slope_ref[...] = (lin * sig * (1.0 - sig)).astype(BF16)
    sig_ref[...] = sig.astype(BF16)
    gated = masked(lin * sig, lens).astype(BF16)
    wa, wb, wl = (spread(wf_ref[...], k) for k in range(3))
    for b in range(PER_STEP // PER_DFT):
        rows = slice(b * SPAN * PER_DFT, (b + 1) * SPAN * PER_DFT)
        part = gated[rows]
        spec = dot(qh_ref[...], part) + dot(ql_ref[...], part)
        freq_ref[b * POINTS * PER_DFT : (b + 1) * POINTS * PER_DFT, :] = spec.astype(BF16)
        re, im = spec[: HALF * PER_DFT], spec[HALF * PER_DFT :]
        turned = jnp.concatenate([re * wa - im * wb, im * wl + re * wb], axis=0)
        high = turned.astype(BF16)
        low = (turned - high.astype(F32)).astype(BF16)
        conv = dot(ih_ref[...], high) + dot(il_ref[...], high) + dot(ih_ref[...], low)
        conv_ref[rows, :] = conv
        live = masked(conv, lens[b * PER_DFT : (b + 1) * PER_DFT])
        acc[0] += folded(live)
        acc[1] += folded(live * live)

    @pl.when(step == pl.num_programs(0) - 1)
    def _():
        sums = [jnp.sum(acc[k], axis=0, keepdims=True) for k in range(2)]
        stats_ref[...] = jnp.broadcast_to(as_tile(*sums)[None], stats_ref.shape)


def split(value, theirs_ref, own_ref):
    blocks = value.reshape(-1, 2, 8, value.shape[1])
    first = lax.axis_index("c") == 0
    low, high = blocks[:, 0], blocks[:, 1]
    theirs_ref[...] = jnp.where(first, high, low).reshape(theirs_ref.shape).astype(BF16)
    own_ref[...] = jnp.where(first, low, high).reshape(own_ref.shape).astype(BF16)


def bn_terms(stats, total):
    first, second = from_tile(stats)
    centre = first / total
    inverse = lax.rsqrt(second / total - centre * centre + EPSILON)
    return centre, inverse


def project_kernel(table_ref, dy_ref, wout_ref, live_dy_ref, grad_ref):
    dy = masked(dy_ref[...].astype(F32), step_lens(table_ref)).astype(BF16)
    live_dy_ref[...] = dy
    grad_ref[...] = dot(dy, wout_ref[...], ((1,), (1,)))


def middle_kernel(
    total, conv_ref, grad_ref, stats_ref, gain_ref, bias_ref,
    swished_ref, gbn_ref, sums_ref, moments_ref, acc,
):
    step = pl.program_id(0)

    @pl.when(step == 0)
    def _():
        acc[...] = jnp.zeros_like(acc)
        moments_ref[...] = jnp.sum(stats_ref[...], axis=0)

    centre, inverse = bn_terms(moments_ref[...], total)
    normed = (conv_ref[...] - centre) * inverse
    value = normed * gain_ref[...] + bias_ref[...]
    sig = jax.nn.sigmoid(value)
    swished_ref[...] = (value * sig).astype(BF16)
    grad = grad_ref[...] * (sig * (1.0 + value * (1.0 - sig)))
    gbn_ref[...] = grad
    acc[0] += folded(grad)
    acc[1] += folded(grad * normed)

    @pl.when(step == pl.num_programs(0) - 1)
    def _():
        sums = [jnp.sum(acc[k], axis=0, keepdims=True) for k in range(2)]
        sums_ref[...] = jnp.broadcast_to(as_tile(*sums)[None], sums_ref.shape)


def output_kernel(swished_ref, dy_ref, wout_ref, out_ref, theirs_ref, own_ref, sw_all, dy_all):
    step = pl.program_id(0)
    out_ref[...] = dot(swished_ref[...], wout_ref[...]).astype(BF16)
    rows = pl.ds(pl.multiple_of(step * PER_STEP * SPAN, 16), PER_STEP * SPAN)
    sw_all[rows, :] = swished_ref[...]
    dy_all[rows, :] = dy_ref[...]

    @pl.when(step == pl.num_programs(0) - 1)
    def _():
        split(dot(sw_all[...], dy_all[...], ((0,), (0,))), theirs_ref, own_ref)


def backward_kernel(
    total, table_ref, h_ref, slope_ref, sig_ref, freq_ref, conv_ref, gbn_ref, wf_ref, stats_ref, sums_ref,
    bn_gain_ref, theirs_in, own_in, qh_ref, ql_ref, ih_ref, il_ref, back_ref,
    grad_a_ref, theirs_ref, own_ref, bias_ref, bn_out_ref, acc, h_all, ga_all,
):
    step = pl.program_id(0)

    @pl.when(step == 0)
    def _():
        acc[...] = jnp.zeros_like(acc)

    lens = step_lens(table_ref)
    centre, inverse = bn_terms(stats_ref[...], total)
    bias_total, gain_total = from_tile(sums_ref[...])
    bias_ref[...] = bias_total
    bn_out_ref[...] = gain_total
    normed_bn = (conv_ref[...] - centre) * inverse
    scale = bn_gain_ref[...] * inverse
    grad_conv = scale * (gbn_ref[...] - bias_total / total - normed_bn * (gain_total / total))
    grad_conv = masked(grad_conv, lens).astype(BF16)
    wa, wb, wl = (spread(wf_ref[...], k) for k in range(3))
    n = HALF * PER_DFT
    edge = lax.broadcasted_iota(jnp.int32, (n, wa.shape[1]), 0) % HALF == 0
    parts = []
    for b in range(PER_STEP // PER_DFT):
        rows = slice(b * SPAN * PER_DFT, (b + 1) * SPAN * PER_DFT)
        spec = dot(qh_ref[...], grad_conv[rows]) + dot(ql_ref[...], grad_conv[rows])
        re, im = spec[:n], spec[n:]
        own = freq_ref[b * 2 * n : (b + 1) * 2 * n, :].astype(F32)
        own_re, own_im = own[:n], own[n:]
        both = im * own_im
        corr_re = re * own_re + jnp.where(edge, 0.0, both)
        corr_im = jnp.where(edge, both, re * own_im - im * own_re)
        acc[:HALF] += jnp.sum(corr_re.reshape(PER_DFT, HALF, -1), axis=0)
        acc[HALF:] += jnp.sum(corr_im.reshape(PER_DFT, HALF, -1), axis=0)
        turned = jnp.concatenate([re * wa + im * wb, im * wl - re * wb], axis=0).astype(BF16)
        parts.append(dot(ih_ref[...], turned) + dot(il_ref[...], turned))
    grad_gated = masked(jnp.concatenate(parts, axis=0), lens)
    grad_a = jnp.concatenate([grad_gated * s[...].astype(F32) for s in (sig_ref, slope_ref)], axis=1).astype(BF16)
    grad_a_ref[...] = grad_a
    rows = pl.ds(pl.multiple_of(step * PER_STEP * SPAN, 16), PER_STEP * SPAN)
    h_all[rows, :] = h_ref[...]
    ga_all[rows, :] = grad_a

    @pl.when(step == pl.num_programs(0) - 1)
    def _():
        d = h_all.shape[1]
        gwin, gwout, taps = slice(0, 2 * d), slice(2 * d, 3 * d), slice(3 * d, theirs_ref.shape[1])
        theirs_ref[:, gwout] = theirs_in[...]
        own_ref[:, gwout] = own_in[...]
        small = dot(acc[...], back_ref[...], ((0,), (0,)), lax.Precision.HIGHEST)
        split(small, theirs_ref.at[:, taps], own_ref.at[:, taps])
        split(dot(h_all[...], ga_all[...], ((0,), (0,))), theirs_ref.at[:, gwin], own_ref.at[:, gwin])


def inputs_kernel(table_ref, frames_ref, grad_a_ref, gain_ref, win_ref, gframes_ref):
    grad_h = dot(grad_a_ref[...], win_ref[...], ((1,), (1,)))
    x = jnp.concatenate([frames_ref[slot_rows(table_ref, u), :] for u in range(PER_STEP)], axis=0)
    gain = gain_ref[...]
    _, normed, inv = normalize(x.astype(F32), gain)
    scaled = grad_h * gain
    inner = jnp.mean(scaled * normed, axis=1, keepdims=True)
    grad_x = inv * (scaled - jnp.mean(scaled, axis=1, keepdims=True) - normed * inner)
    grad_x = masked(grad_x, step_lens(table_ref)).astype(BF16)
    for u in range(PER_STEP):
        gframes_ref[slot_rows(table_ref, u), :] = grad_x[u * SPAN : (u + 1) * SPAN]


def pair_kernel(own_ref, got_ref, both_ref):
    both_ref[...] = (own_ref[...].astype(F32) + got_ref[...].astype(F32)).astype(BF16)


def collect_kernel(got_ref, out_ref):
    total = got_ref[0].astype(F32)
    for k in range(1, got_ref.shape[0]):
        total += got_ref[k].astype(F32)
    for k in range(out_ref.shape[0]):
        out_ref[k] = total.astype(BF16)


def finish_kernel(every_ref, w_ref, gain_ref, gwin_ref, gwout_ref, gwdw_ref, gln_ref):
    count = every_ref.shape[0]
    halves = [sum(every_ref[k].astype(F32) for k in range(core, count, 2)) for core in range(2)]
    rows = jnp.concatenate(halves, axis=0)
    d = gwout_ref.shape[1]
    gwin = rows[:, : 2 * d]
    gwin_ref[...] = gwin
    gwout_ref[...] = rows[:, 2 * d : 3 * d]
    gwdw_ref[...] = rows[:, 3 * d : 3 * d + gwdw_ref.shape[1]]
    ones = jnp.ones((8, 2 * d), F32)
    dots = dot(ones, gwin * w_ref[...].astype(F32), ((1,), (1,)), lax.Precision.HIGHEST)
    gln_ref[...] = dots[:1] / gain_ref[...]


SMEM = pl.BlockSpec(memory_space=pltpu.SMEM)


def whole(shape):
    return pl.BlockSpec(shape, lambda i: (0,) * len(shape))


def rows_of(shape, steps):
    return pl.BlockSpec((shape[0] // steps, shape[1]), lambda i: (i, 0))


def cost(flops, moved):
    return pl.CostEstimate(flops=int(flops), bytes_accessed=int(moved), transcendentals=0)


def params():
    return pltpu.CompilerParams(dimension_semantics=("arbitrary",), vmem_limit_bytes=VMEM_LIMIT)


def sds(shape, dtype):
    return jax.ShapeDtypeStruct(shape, dtype)


def unpack(lengths, owners, upstream, loaders):
    rows, d = upstream.shape
    vmem = pl.BlockSpec(memory_space=pltpu.VMEM)
    return pl.pallas_call(
        unpack_kernel,
        out_shape=(sds((loaders * SPAN, d), BF16), sds((loaders, 128), jnp.int32)),
        in_specs=[vmem] * 3,
        out_specs=(vmem, vmem),
        scratch_shapes=[
            pltpu.VMEM((rows + 8, d), F32),
            pltpu.VMEM((loaders, loaders), jnp.int32),
            pltpu.VMEM((loaders, loaders), jnp.int32),
            pltpu.SMEM((loaders, 128), jnp.int32),
            pltpu.SemaphoreType.DMA,
        ],
        compiler_params=pltpu.CompilerParams(vmem_limit_bytes=VMEM_LIMIT),
        name="unpack",
        cost_estimate=cost(1e9, 6 * rows * d),
    )(lengths, owners, upstream)


def pack(table, got, rows):
    return pl.pallas_call(
        pack_kernel,
        out_shape=sds((rows, got.shape[1]), BF16),
        in_specs=[SMEM, pl.BlockSpec(memory_space=pltpu.VMEM)],
        out_specs=pl.BlockSpec(memory_space=pltpu.VMEM),
        scratch_shapes=[pltpu.VMEM((rows + 8, got.shape[1]), F32)],
        compiler_params=pltpu.CompilerParams(vmem_limit_bytes=VMEM_LIMIT),
        name="pack",
        cost_estimate=cost(2e9, 6 * rows * got.shape[1]),
    )(table, got)


def forward(table, frames, gain, w_in, w_dw, tabs, copies):
    high, low, high_t, low_t, taps_to, _ = tabs
    rows, d = frames.shape
    steps = rows // (SPAN * PER_STEP)
    freq = (rows // SPAN * POINTS, d)
    return pl.pallas_call(
        forward_kernel,
        grid=(steps,),
        out_shape=(
            sds((rows, d), BF16),
            sds((rows, d), BF16),
            sds((rows, d), BF16),
            sds(freq, BF16),
            sds((rows, d), F32),
            sds((3 * HALF, d), F32),
            sds((copies, 8, 128), F32),
        ),
        in_specs=[SMEM, whole(frames.shape), whole(gain.shape), whole(w_in.shape)]
        + [whole(v.shape) for v in (high, low, high_t, low_t, taps_to, w_dw)],
        out_specs=(
            rows_of((rows, d), steps),
            rows_of((rows, d), steps),
            rows_of((rows, d), steps),
            rows_of(freq, steps),
            rows_of((rows, d), steps),
            whole((3 * HALF, d)),
            whole((copies, 8, 128)),
        ),
        scratch_shapes=[pltpu.VMEM((2, 8, d), F32)],
        compiler_params=params(),
        name="forward",
        cost_estimate=cost(10e9, 16 * rows * d),
    )(table, frames, gain, w_in, high, low, high_t, low_t, taps_to, w_dw)


def project(table, dy, w_out):
    rows, d = dy.shape
    steps = rows // (SPAN * PER_STEP)
    part = rows_of((rows, d), steps)
    return pl.pallas_call(
        project_kernel,
        grid=(steps,),
        out_shape=(sds((rows, d), BF16), sds((rows, d), F32)),
        in_specs=[SMEM, part, whole(w_out.shape)],
        out_specs=(part, part),
        compiler_params=params(),
        name="project",
        cost_estimate=cost(3e9, 6 * rows * d),
    )(table, dy, w_out)


def middle(total, conv, grad, stats, bn_gain, bn_bias, copies):
    rows, d = conv.shape
    steps = rows // (SPAN * PER_STEP)
    part = rows_of((rows, d), steps)
    tiles = (copies, 8, 128)
    return pl.pallas_call(
        functools.partial(middle_kernel, total),
        grid=(steps,),
        out_shape=(sds((rows, d), BF16), sds((rows, d), F32), sds(tiles, F32), sds((8, 128), F32)),
        in_specs=[part, part] + [whole(v.shape) for v in (stats, bn_gain, bn_bias)],
        out_specs=(part, part, whole(tiles), whole((8, 128))),
        scratch_shapes=[pltpu.VMEM((2, 8, d), F32)],
        compiler_params=params(),
        name="middle",
        cost_estimate=cost(4e9, 10 * rows * d),
    )(conv, grad, stats, bn_gain, bn_bias)


def outputs(swished, dy, w_out):
    rows, d = swished.shape
    steps = rows // (SPAN * PER_STEP)
    part = rows_of((rows, d), steps)
    half = (d // 2, d)
    return pl.pallas_call(
        output_kernel,
        grid=(steps,),
        out_shape=(sds((rows, d), BF16), sds(half, BF16), sds(half, BF16)),
        in_specs=[part, part, whole(w_out.shape)],
        out_specs=(part, whole(half), whole(half)),
        scratch_shapes=[pltpu.VMEM((rows, d), BF16), pltpu.VMEM((rows, d), BF16)],
        compiler_params=params(),
        name="outputs",
        cost_estimate=cost(4e9, 6 * rows * d),
    )(swished, dy, w_out)


def backward(total, table, h, slope, sig, freq, conv, gbn, wf, stats, sums, bn_gain, theirs, own, tabs):
    high, low, high_t, low_t, _, back = tabs
    rows, d = h.shape
    width = 3 * d + back.shape[1]
    steps = rows // (SPAN * PER_STEP)
    part = rows_of((rows, d), steps)
    return pl.pallas_call(
        functools.partial(backward_kernel, total),
        grid=(steps,),
        out_shape=(
            sds((rows, 2 * d), BF16),
            sds((d // 2, width), BF16),
            sds((d // 2, width), BF16),
            sds((1, d), F32),
            sds((1, d), F32),
        ),
        in_specs=[SMEM, part, part, part, rows_of(freq.shape, steps), part, part]
        + [whole(v.shape) for v in (wf, stats, sums, bn_gain, theirs, own, high, low, high_t, low_t, back)],
        out_specs=(
            rows_of((rows, 2 * d), steps),
            whole((d // 2, width)),
            whole((d // 2, width)),
            whole((1, d)),
            whole((1, d)),
        ),
        scratch_shapes=[
            pltpu.VMEM((2 * HALF, d), F32),
            pltpu.VMEM((rows, d), BF16),
            pltpu.VMEM((rows, 2 * d), BF16),
        ],
        compiler_params=params(),
        name="backward",
        cost_estimate=cost(8e9, 18 * rows * d),
    )(table, h, slope, sig, freq, conv, gbn, wf, stats, sums, bn_gain, theirs, own, high, low, high_t, low_t, back)


def inputs_back(table, frames, grad_a, gain, w_in):
    rows, d = frames.shape
    steps = rows // (SPAN * PER_STEP)
    return pl.pallas_call(
        inputs_kernel,
        grid=(steps,),
        out_shape=sds((rows, d), BF16),
        in_specs=[SMEM, whole(frames.shape), rows_of(grad_a.shape, steps), whole(gain.shape), whole(w_in.shape)],
        out_specs=whole((rows, d)),
        compiler_params=params(),
        name="inputs_back",
        cost_estimate=cost(6e9, 12 * rows * d),
    )(table, frames, grad_a, gain, w_in)


def pair_sum(own, got):
    rows, width = own.shape
    part = pl.BlockSpec((rows // 2, width), lambda i: (i, 0))
    return pl.pallas_call(
        pair_kernel,
        grid=(2,),
        out_shape=sds((rows, width), BF16),
        in_specs=[part, part],
        out_specs=part,
        compiler_params=pltpu.CompilerParams(vmem_limit_bytes=SMALL_LIMIT),
        name="pair_sum",
        cost_estimate=cost(2 * rows * width, 6 * rows * width),
    )(own, got)


def collect(got, count):
    vmem = pl.BlockSpec(memory_space=pltpu.VMEM)
    return pl.pallas_call(
        collect_kernel,
        out_shape=sds((count, *got.shape[1:]), BF16),
        in_specs=[vmem],
        out_specs=vmem,
        compiler_params=pltpu.CompilerParams(vmem_limit_bytes=SMALL_LIMIT),
        name="collect",
    )(got)


def finish(every, w_rows, gain_rows, taps):
    share, width = w_rows.shape
    d = width // 2
    vmem = pl.BlockSpec(memory_space=pltpu.VMEM)
    return pl.pallas_call(
        finish_kernel,
        out_shape=(sds((share, width), F32), sds((share, d), F32), sds((share, taps), F32), sds((1, share), F32)),
        in_specs=[vmem] * 3,
        out_specs=(vmem,) * 4,
        compiler_params=pltpu.CompilerParams(vmem_limit_bytes=SMALL_LIMIT),
        name="finish",
    )(every, w_rows, gain_rows)


def swapped(value, axes):
    return lax.all_to_all(value, axes, split_axis=0, concat_axis=0, tiled=True)


def over_bucket(theirs, own, loaders, ahead):
    got = lax.ppermute(theirs, "c", [(0, 1), (1, 0)])
    both = pair_sum(own, got).reshape(loaders, -1, own.shape[1])
    both, ahead = lax.optimization_barrier((both, ahead))
    return swapped(both, BUCKET), ahead


def local(frames, lengths, owners, upstream, ln_gain, w_in, w_dw, bn_gain, bn_bias, w_out):
    loaders = lax.axis_size(BUCKET)
    me = lax.axis_index(BUCKET)
    rows, d = frames.shape
    taps = w_dw.shape[1]
    share = d // loaders
    total = float(upstream.shape[0] * loaders * lax.axis_size(DP))
    tabs = tuple(jnp.asarray(v) for v in tables(taps))
    w_rows = lax.dynamic_slice_in_dim(w_in, me * share, share, 0)
    gain_rows = lax.dynamic_slice_in_dim(ln_gain, me * share, share, 0).reshape(1, share)
    gain, bn_gain, bn_bias = (v.reshape(1, d) for v in (ln_gain, bn_gain, bn_bias))

    dy, table = unpack(lengths, owners, upstream, loaders)
    dy = swapped(dy.reshape(loaders, SPAN, d), BUCKET).reshape(rows, d)
    h, slope, sig, freq, conv, wf, stats = forward(table, frames, gain, w_in, w_dw, tabs, lax.axis_size("z"))
    stats = lax.psum(lax.psum(lax.psum(stats, "c"), "y"), "x")
    stats, dy = lax.optimization_barrier((stats, dy))
    stats = swapped(stats, "z")
    live_dy, grad = project(table, dy, w_out)
    swished, gbn, sums, stats = middle(total, conv, grad, stats, bn_gain, bn_bias, lax.axis_size(("c", "z")))
    sums = jnp.sum(swapped(sums, ("c", "z")), axis=0)
    out, theirs, own = outputs(swished, live_dy, w_out)
    out, sums = lax.optimization_barrier((out, sums))
    out = swapped(out.reshape(loaders, SPAN, d), BUCKET).reshape(rows, d)
    sums = lax.psum(lax.psum(sums, "y"), "x")
    grad_a, theirs, own, bias_total, gain_total = backward(
        total, table, h, slope, sig, freq, conv, gbn, wf, stats, sums, bn_gain, theirs, own, tabs
    )
    got, out = over_bucket(theirs, own, loaders, out)
    gframes = inputs_back(table, frames, grad_a, gain, w_in)
    out_frames = pack(table, out, upstream.shape[0])
    got, gframes, out_frames = lax.optimization_barrier((got, gframes, out_frames))
    every = swapped(collect(got, lax.axis_size(DP)), DP)
    gwin, gwout, gwdw, gln = finish(every, w_rows, gain_rows, taps)
    return (
        out_frames,
        gframes,
        gwin,
        gwout,
        gwdw,
        gln.reshape(share),
        gain_total.reshape(d),
        bias_total.reshape(d),
    )


def solution(mesh):
    torus = Mesh(mesh.devices.reshape(4, 2, 4, 8), ("y", "c", "x", "z"))
    in_specs = (P(EVERY, None), P(DP, None), P(DP, None), P(EVERY, None)) + (P(),) * 6
    out_specs = (P(EVERY, None), P(EVERY, None), P(BUCKET, None), P(BUCKET, None), P(BUCKET, None), P(BUCKET), P(), P())
    return jax.shard_map(local, mesh=torus, in_specs=in_specs, out_specs=out_specs, check_vma=False)
```

```python
import functools
import math

import jax
import jax.numpy as jnp
import numpy as np
from jax import lax
from jax.experimental import pallas as pl
from jax.experimental.pallas import tpu as pltpu
from jax.sharding import Mesh
from jax.sharding import PartitionSpec as P

BUCKET = ("x", "z")
DP = ("y", "c")
EVERY = ("y", "c", "x", "z")


EPSILON = 1e-05
SPAN = 48
POINTS = 64
HALF = POINTS // 2
PER_DFT = 4
PER_STEP = 16
UNROLL = 4
VMEM_LIMIT = 60 * 2**20
SMALL_LIMIT = 16 * 2**20

F32 = jnp.float32
BF16 = jnp.bfloat16


def dot(a, b, dims=((1,), (0,)), precision=None):
    return lax.dot_general(a, b, (dims, ((), ())), preferred_element_type=F32, precision=precision)


def tables(taps):
    f = np.arange(HALF)[:, None]
    t = np.arange(SPAN)[None, :]
    angle = 2 * np.pi * f * t / POINTS
    real = np.cos(angle) * math.sqrt(2 / POINTS)
    imag = -np.sin(angle) * math.sqrt(2 / POINTS)
    real[0] = math.sqrt(1 / POINTS)
    imag[0] = math.sqrt(1 / POINTS) * (-1.0) ** np.arange(SPAN)
    block = np.zeros((2 * HALF * PER_DFT, SPAN * PER_DFT))
    for u in range(PER_DFT):
        block[u * HALF : (u + 1) * HALF, u * SPAN : (u + 1) * SPAN] = real
        block[(PER_DFT + u) * HALF : (PER_DFT + u + 1) * HALF, u * SPAN : (u + 1) * SPAN] = imag
    lag = np.arange(taps)[None, :] - taps // 2
    turn = 2 * np.pi * f * lag / POINTS
    cos, sin = np.cos(turn), np.sin(turn)
    cos_last = cos.copy()
    cos_last[0] = np.cos(np.pi * lag[0])
    taps_to = np.concatenate([cos, sin, cos_last], axis=0)
    back = np.zeros((2 * HALF, 128))
    back[:HALF, :taps] = cos
    back[HALF : 2 * HALF, :taps] = -sin
    back[HALF, :taps] = np.cos(np.pi * lag[0])
    high = block.astype(jnp.bfloat16)
    low = (block - high.astype(np.float64)).astype(jnp.bfloat16)
    return (
        high,
        low,
        np.ascontiguousarray(high.T),
        np.ascontiguousarray(low.T),
        taps_to.astype(np.float32),
        back.astype(np.float32),
    )


def masked(value, lens):
    t = lax.broadcasted_iota(jnp.int32, (SPAN, value.shape[1]), 0)
    return jnp.concatenate(
        [
            jnp.where(t < n, value[u * SPAN : (u + 1) * SPAN], jnp.zeros((), value.dtype))
            for u, n in enumerate(lens)
        ],
        axis=0,
    )


def folded(value):
    return jnp.sum(value.reshape(-1, 8, value.shape[1]), axis=0)


def as_tile(first, second):
    rows = [v[:, k * 128 : (k + 1) * 128] for v in (first, second) for k in range(4)]
    return jnp.concatenate(rows, axis=0)


def from_tile(tile):
    rows = [tile[k : k + 1] for k in range(8)]
    return (jnp.concatenate(rows[:4], axis=1), jnp.concatenate(rows[4:], axis=1))


def normalize(x, gain):
    centred = x - jnp.mean(x, axis=1, keepdims=True)
    inverse = lax.rsqrt(jnp.mean(centred * centred, axis=1, keepdims=True) + EPSILON)
    normed = centred * inverse
    return (normed * gain).astype(BF16), normed, inverse


def spread(wf, part):
    rows = wf[part * HALF : (part + 1) * HALF]
    return jnp.concatenate([rows] * PER_DFT, axis=0)


def unpack_kernel(lengths_ref, owners_ref, upstream_ref, out_ref, table_ref, wide, lens_all, dest_all, table, sem):
    loaders = lens_all.shape[0]
    me = lax.axis_index(BUCKET)
    for k in range(loaders):
        lens_all[k : k + 1, :] = lengths_ref[:, k * loaders : (k + 1) * loaders]
        dest_all[k : k + 1, :] = owners_ref[:, k * loaders : (k + 1) * loaders]
    got = jnp.sum(jnp.where(dest_all[...] == me, lens_all[...], 0), axis=1, keepdims=True)
    square = (loaders, loaders)
    hit = dest_all[pl.ds(me, 1), :] == lax.broadcasted_iota(jnp.int32, square, 0)
    lens = jnp.sum(jnp.where(hit, lens_all[pl.ds(me, 1), :], 0), axis=1, keepdims=True)
    slots = jnp.sum(jnp.where(hit, lax.broadcasted_iota(jnp.int32, square, 1), 0), axis=1, keepdims=True)
    column = lax.broadcasted_iota(jnp.int32, table_ref.shape, 1)
    table_ref[...] = jnp.where(column == 0, got, jnp.where(column == 1, lens, slots))
    copy = pltpu.make_async_copy(table_ref, table, sem)
    copy.start()
    rows = upstream_ref.shape[0]
    wide[:rows, :] = upstream_ref[...].astype(F32)
    wide[rows:, :] = jnp.zeros((8, wide.shape[1]), F32)
    copy.wait()

    def step(group, start):
        for i in (group * UNROLL + k for k in range(UNROLL)):
            base = pl.multiple_of(start // 8 * 8, 8)
            window = pltpu.roll(wide[pl.ds(base, SPAN + 8), :], SPAN + 8 - start % 8, 0)
            out_ref[pl.ds(pl.multiple_of(i * SPAN, 16), SPAN), :] = window[:SPAN].astype(BF16)
            start += table[i, 0]
        return start

    lax.fori_loop(0, loaders // UNROLL, step, jnp.int32(0))


def pack_kernel(table_ref, got_ref, out_ref, wide):
    count = got_ref.shape[0] // SPAN
    top = lax.broadcasted_iota(jnp.int32, (8, got_ref.shape[1]), 0)

    def step(i, start):
        base = pl.multiple_of(start // 8 * 8, 8)
        rows = got_ref[pl.ds(pl.multiple_of(i * SPAN, 16), SPAN), :].astype(F32)
        window = jnp.concatenate([rows, jnp.zeros((8, rows.shape[1]), F32)], axis=0)
        window = pltpu.roll(window, start % 8, 0)
        kept = jnp.where(top < start % 8, wide[pl.ds(base, 8), :], window[:8])
        wide[pl.ds(base, 8), :] = kept
        wide[pl.ds(base + 8, SPAN), :] = window[8:]
        return start + table_ref[i, 0]

    lax.fori_loop(0, count, step, jnp.int32(0))
    out_ref[...] = wide[: out_ref.shape[0], :].astype(BF16)


def step_lens(table_ref):
    return [table_ref[pl.program_id(0) * PER_STEP + u, 1] for u in range(PER_STEP)]


def slot_rows(table_ref, u):
    slot = table_ref[pl.program_id(0) * PER_STEP + u, 2]
    return pl.ds(pl.multiple_of(slot * SPAN, 16), SPAN)


def forward_kernel(
    table_ref, frames_ref, gain_ref, win_ref, qh_ref, ql_ref, ih_ref, il_ref, to_ref, wdw_ref,
    h_ref, slope_ref, sig_ref, freq_ref, conv_ref, wf_ref, stats_ref, acc,
):
    step = pl.program_id(0)

    @pl.when(step == 0)
    def _():
        wf_ref[...] = dot(to_ref[...], wdw_ref[...], ((1,), (1,)), lax.Precision.HIGHEST)
        acc[...] = jnp.zeros_like(acc)

    d = frames_ref.shape[1]
    lens = step_lens(table_ref)
    x = jnp.concatenate([frames_ref[slot_rows(table_ref, u), :] for u in range(PER_STEP)], axis=0)
    h, _, _ = normalize(x.astype(F32), gain_ref[...])
    h_ref[...] = h
    a = dot(h, win_ref[...])
    lin = a[:, :d]
    sig = jax.nn.sigmoid(a[:, d:])
    slope_ref[...] = (lin * sig * (1.0 - sig)).astype(BF16)
    sig_ref[...] = sig.astype(BF16)
    gated = masked(lin * sig, lens).astype(BF16)
    wa, wb, wl = (spread(wf_ref[...], k) for k in range(3))
    for b in range(PER_STEP // PER_DFT):
        rows = slice(b * SPAN * PER_DFT, (b + 1) * SPAN * PER_DFT)
        part = gated[rows]
        spec = dot(qh_ref[...], part) + dot(ql_ref[...], part)
        freq_ref[b * POINTS * PER_DFT : (b + 1) * POINTS * PER_DFT, :] = spec.astype(BF16)
        re, im = spec[: HALF * PER_DFT], spec[HALF * PER_DFT :]
        turned = jnp.concatenate([re * wa - im * wb, im * wl + re * wb], axis=0)
        high = turned.astype(BF16)
        low = (turned - high.astype(F32)).astype(BF16)
        conv = dot(ih_ref[...], high) + dot(il_ref[...], high) + dot(ih_ref[...], low)
        conv_ref[rows, :] = conv
        live = masked(conv, lens[b * PER_DFT : (b + 1) * PER_DFT])
        acc[0] += folded(live)
        acc[1] += folded(live * live)

    @pl.when(step == pl.num_programs(0) - 1)
    def _():
        sums = [jnp.sum(acc[k], axis=0, keepdims=True) for k in range(2)]
        stats_ref[...] = as_tile(*sums)


def split(value, theirs_ref, own_ref):
    blocks = value.reshape(-1, 2, 8, value.shape[1])
    first = lax.axis_index("c") == 0
    low, high = blocks[:, 0], blocks[:, 1]
    theirs_ref[...] = jnp.where(first, high, low).reshape(theirs_ref.shape).astype(BF16)
    own_ref[...] = jnp.where(first, low, high).reshape(own_ref.shape).astype(BF16)


def bn_terms(stats, total):
    first, second = from_tile(stats)
    centre = first / total
    inverse = lax.rsqrt(second / total - centre * centre + EPSILON)
    return centre, inverse


def project_kernel(table_ref, dy_ref, wout_ref, live_dy_ref, grad_ref):
    dy = masked(dy_ref[...].astype(F32), step_lens(table_ref)).astype(BF16)
    live_dy_ref[...] = dy
    grad_ref[...] = dot(dy, wout_ref[...], ((1,), (1,)))


def middle_kernel(
    total, conv_ref, grad_ref, stats_ref, gain_ref, bias_ref,
    swished_ref, gbn_ref, sums_ref, moments_ref, acc,
):
    step = pl.program_id(0)

    @pl.when(step == 0)
    def _():
        acc[...] = jnp.zeros_like(acc)
        moments_ref[...] = jnp.sum(stats_ref[...], axis=0)

    centre, inverse = bn_terms(moments_ref[...], total)
    normed = (conv_ref[...] - centre) * inverse
    value = normed * gain_ref[...] + bias_ref[...]
    sig = jax.nn.sigmoid(value)
    swished_ref[...] = (value * sig).astype(BF16)
    grad = grad_ref[...] * (sig * (1.0 + value * (1.0 - sig)))
    gbn_ref[...] = grad
    acc[0] += folded(grad)
    acc[1] += folded(grad * normed)

    @pl.when(step == pl.num_programs(0) - 1)
    def _():
        sums = [jnp.sum(acc[k], axis=0, keepdims=True) for k in range(2)]
        sums_ref[...] = jnp.broadcast_to(as_tile(*sums)[None], sums_ref.shape)


def output_kernel(swished_ref, dy_ref, wout_ref, out_ref, theirs_ref, own_ref):
    out_ref[...] = dot(swished_ref[...], wout_ref[...]).astype(BF16)
    split(dot(swished_ref[...], dy_ref[...], ((0,), (0,))), theirs_ref, own_ref)


def backward_kernel(
    total, table_ref, h_ref, slope_ref, sig_ref, freq_ref, conv_ref, gbn_ref, wf_ref, stats_ref, sums_ref,
    bn_gain_ref, theirs_in, own_in, qh_ref, ql_ref, ih_ref, il_ref, back_ref,
    grad_a_ref, theirs_ref, own_ref, bias_ref, bn_out_ref, acc, h_all, ga_all,
):
    step = pl.program_id(0)

    @pl.when(step == 0)
    def _():
        acc[...] = jnp.zeros_like(acc)

    lens = step_lens(table_ref)
    centre, inverse = bn_terms(stats_ref[...], total)
    bias_total, gain_total = from_tile(sums_ref[...])
    bias_ref[...] = bias_total
    bn_out_ref[...] = gain_total
    normed_bn = (conv_ref[...] - centre) * inverse
    scale = bn_gain_ref[...] * inverse
    grad_conv = scale * (gbn_ref[...] - bias_total / total - normed_bn * (gain_total / total))
    grad_conv = masked(grad_conv, lens).astype(BF16)
    wa, wb, wl = (spread(wf_ref[...], k) for k in range(3))
    n = HALF * PER_DFT
    edge = lax.broadcasted_iota(jnp.int32, (n, wa.shape[1]), 0) % HALF == 0
    parts = []
    for b in range(PER_STEP // PER_DFT):
        rows = slice(b * SPAN * PER_DFT, (b + 1) * SPAN * PER_DFT)
        spec = dot(qh_ref[...], grad_conv[rows]) + dot(ql_ref[...], grad_conv[rows])
        re, im = spec[:n], spec[n:]
        own = freq_ref[b * 2 * n : (b + 1) * 2 * n, :].astype(F32)
        own_re, own_im = own[:n], own[n:]
        both = im * own_im
        corr_re = re * own_re + jnp.where(edge, 0.0, both)
        corr_im = jnp.where(edge, both, re * own_im - im * own_re)
        acc[:HALF] += jnp.sum(corr_re.reshape(PER_DFT, HALF, -1), axis=0)
        acc[HALF:] += jnp.sum(corr_im.reshape(PER_DFT, HALF, -1), axis=0)
        turned = jnp.concatenate([re * wa + im * wb, im * wl - re * wb], axis=0).astype(BF16)
        parts.append(dot(ih_ref[...], turned) + dot(il_ref[...], turned))
    grad_gated = masked(jnp.concatenate(parts, axis=0), lens)
    grad_a = jnp.concatenate([grad_gated * s[...].astype(F32) for s in (sig_ref, slope_ref)], axis=1).astype(BF16)
    grad_a_ref[...] = grad_a
    rows = pl.ds(pl.multiple_of(step * PER_STEP * SPAN, 16), PER_STEP * SPAN)
    h_all[rows, :] = h_ref[...]
    ga_all[rows, :] = grad_a

    @pl.when(step == pl.num_programs(0) - 1)
    def _():
        d = h_all.shape[1]
        gwin, gwout, taps = slice(0, 2 * d), slice(2 * d, 3 * d), slice(3 * d, theirs_ref.shape[1])
        theirs_ref[:, gwout] = theirs_in[...]
        own_ref[:, gwout] = own_in[...]
        small = dot(acc[...], back_ref[...], ((0,), (0,)), lax.Precision.HIGHEST)
        split(small, theirs_ref.at[:, taps], own_ref.at[:, taps])
        split(dot(h_all[...], ga_all[...], ((0,), (0,))), theirs_ref.at[:, gwin], own_ref.at[:, gwin])


def inputs_kernel(table_ref, frames_ref, grad_a_ref, gain_ref, win_ref, gframes_ref):
    grad_h = dot(grad_a_ref[...], win_ref[...], ((1,), (1,)))
    x = jnp.concatenate([frames_ref[slot_rows(table_ref, u), :] for u in range(PER_STEP)], axis=0)
    gain = gain_ref[...]
    _, normed, inv = normalize(x.astype(F32), gain)
    scaled = grad_h * gain
    inner = jnp.mean(scaled * normed, axis=1, keepdims=True)
    grad_x = inv * (scaled - jnp.mean(scaled, axis=1, keepdims=True) - normed * inner)
    grad_x = masked(grad_x, step_lens(table_ref)).astype(BF16)
    for u in range(PER_STEP):
        gframes_ref[slot_rows(table_ref, u), :] = grad_x[u * SPAN : (u + 1) * SPAN]


def pair_kernel(own_ref, got_ref, both_ref):
    both_ref[...] = (own_ref[...].astype(F32) + got_ref[...].astype(F32)).astype(BF16)


def collect_kernel(got_ref, out_ref):
    total = got_ref[0].astype(F32)
    for k in range(1, got_ref.shape[0]):
        total += got_ref[k].astype(F32)
    for k in range(out_ref.shape[0]):
        out_ref[k] = total.astype(BF16)


def finish_kernel(every_ref, w_ref, gain_ref, gwin_ref, gwout_ref, gwdw_ref, gln_ref):
    count = every_ref.shape[0]
    halves = [sum(every_ref[k].astype(F32) for k in range(core, count, 2)) for core in range(2)]
    rows = jnp.concatenate(halves, axis=0)
    d = gwout_ref.shape[1]
    gwin = rows[:, : 2 * d]
    gwin_ref[...] = gwin
    gwout_ref[...] = rows[:, 2 * d : 3 * d]
    gwdw_ref[...] = rows[:, 3 * d : 3 * d + gwdw_ref.shape[1]]
    ones = jnp.ones((8, 2 * d), F32)
    dots = dot(ones, gwin * w_ref[...].astype(F32), ((1,), (1,)), lax.Precision.HIGHEST)
    gln_ref[...] = dots[:1] / gain_ref[...]


SMEM = pl.BlockSpec(memory_space=pltpu.SMEM)


def whole(shape):
    return pl.BlockSpec(shape, lambda i: (0,) * len(shape))


def rows_of(shape, steps):
    return pl.BlockSpec((shape[0] // steps, shape[1]), lambda i: (i, 0))


def cost(flops, moved):
    return pl.CostEstimate(flops=int(flops), bytes_accessed=int(moved), transcendentals=0)


def params():
    return pltpu.CompilerParams(dimension_semantics=("arbitrary",), vmem_limit_bytes=VMEM_LIMIT)


def sds(shape, dtype):
    return jax.ShapeDtypeStruct(shape, dtype)


def unpack(lengths, owners, upstream, loaders):
    rows, d = upstream.shape
    vmem = pl.BlockSpec(memory_space=pltpu.VMEM)
    return pl.pallas_call(
        unpack_kernel,
        out_shape=(sds((loaders * SPAN, d), BF16), sds((loaders, 128), jnp.int32)),
        in_specs=[vmem] * 3,
        out_specs=(vmem, vmem),
        scratch_shapes=[
            pltpu.VMEM((rows + 8, d), F32),
            pltpu.VMEM((loaders, loaders), jnp.int32),
            pltpu.VMEM((loaders, loaders), jnp.int32),
            pltpu.SMEM((loaders, 128), jnp.int32),
            pltpu.SemaphoreType.DMA,
        ],
        compiler_params=pltpu.CompilerParams(vmem_limit_bytes=VMEM_LIMIT),
        name="unpack",
        cost_estimate=cost(1e9, 6 * rows * d),
    )(lengths, owners, upstream)


def pack(table, got, rows):
    return pl.pallas_call(
        pack_kernel,
        out_shape=sds((rows, got.shape[1]), BF16),
        in_specs=[SMEM, pl.BlockSpec(memory_space=pltpu.VMEM)],
        out_specs=pl.BlockSpec(memory_space=pltpu.VMEM),
        scratch_shapes=[pltpu.VMEM((rows + 8, got.shape[1]), F32)],
        compiler_params=pltpu.CompilerParams(vmem_limit_bytes=VMEM_LIMIT),
        name="pack",
        cost_estimate=cost(2e9, 6 * rows * got.shape[1]),
    )(table, got)


def forward(table, frames, gain, w_in, w_dw, tabs):
    high, low, high_t, low_t, taps_to, _ = tabs
    rows, d = frames.shape
    steps = rows // (SPAN * PER_STEP)
    freq = (rows // SPAN * POINTS, d)
    return pl.pallas_call(
        forward_kernel,
        grid=(steps,),
        out_shape=(
            sds((rows, d), BF16),
            sds((rows, d), BF16),
            sds((rows, d), BF16),
            sds(freq, BF16),
            sds((rows, d), F32),
            sds((3 * HALF, d), F32),
            sds((8, 128), F32),
        ),
        in_specs=[SMEM, whole(frames.shape), whole(gain.shape), whole(w_in.shape)]
        + [whole(v.shape) for v in (high, low, high_t, low_t, taps_to, w_dw)],
        out_specs=(
            rows_of((rows, d), steps),
            rows_of((rows, d), steps),
            rows_of((rows, d), steps),
            rows_of(freq, steps),
            rows_of((rows, d), steps),
            whole((3 * HALF, d)),
            whole((8, 128)),
        ),
        scratch_shapes=[pltpu.VMEM((2, 8, d), F32)],
        compiler_params=params(),
        name="forward",
        cost_estimate=cost(10e9, 16 * rows * d),
    )(table, frames, gain, w_in, high, low, high_t, low_t, taps_to, w_dw)


def project(table, dy, w_out):
    rows, d = dy.shape
    steps = rows // (SPAN * PER_STEP)
    part = rows_of((rows, d), steps)
    return pl.pallas_call(
        project_kernel,
        grid=(steps,),
        out_shape=(sds((rows, d), BF16), sds((rows, d), F32)),
        in_specs=[SMEM, part, whole(w_out.shape)],
        out_specs=(part, part),
        compiler_params=params(),
        name="project",
        cost_estimate=cost(3e9, 6 * rows * d),
    )(table, dy, w_out)


def middle(total, conv, grad, stats, bn_gain, bn_bias, copies):
    rows, d = conv.shape
    steps = rows // (SPAN * PER_STEP)
    part = rows_of((rows, d), steps)
    tiles = (copies, 8, 128)
    return pl.pallas_call(
        functools.partial(middle_kernel, total),
        grid=(steps,),
        out_shape=(sds((rows, d), BF16), sds((rows, d), F32), sds(tiles, F32), sds((8, 128), F32)),
        in_specs=[part, part] + [whole(v.shape) for v in (stats, bn_gain, bn_bias)],
        out_specs=(part, part, whole(tiles), whole((8, 128))),
        scratch_shapes=[pltpu.VMEM((2, 8, d), F32)],
        compiler_params=params(),
        name="middle",
        cost_estimate=cost(4e9, 10 * rows * d),
    )(conv, grad, stats, bn_gain, bn_bias)


def outputs(swished, dy, w_out):
    rows, d = swished.shape
    part = whole((rows, d))
    half = (d // 2, d)
    return pl.pallas_call(
        output_kernel,
        grid=(1,),
        out_shape=(sds((rows, d), BF16), sds(half, BF16), sds(half, BF16)),
        in_specs=[part, part, whole(w_out.shape)],
        out_specs=(part, whole(half), whole(half)),
        compiler_params=params(),
        name="outputs",
        cost_estimate=cost(4e9, 6 * rows * d),
    )(swished, dy, w_out)


def backward(total, table, h, slope, sig, freq, conv, gbn, wf, stats, sums, bn_gain, theirs, own, tabs):
    high, low, high_t, low_t, _, back = tabs
    rows, d = h.shape
    width = 3 * d + back.shape[1]
    steps = rows // (SPAN * PER_STEP)
    part = rows_of((rows, d), steps)
    return pl.pallas_call(
        functools.partial(backward_kernel, total),
        grid=(steps,),
        out_shape=(
            sds((rows, 2 * d), BF16),
            sds((d // 2, width), BF16),
            sds((d // 2, width), BF16),
            sds((1, d), F32),
            sds((1, d), F32),
        ),
        in_specs=[SMEM, part, part, part, rows_of(freq.shape, steps), part, part]
        + [whole(v.shape) for v in (wf, stats, sums, bn_gain, theirs, own, high, low, high_t, low_t, back)],
        out_specs=(
            rows_of((rows, 2 * d), steps),
            whole((d // 2, width)),
            whole((d // 2, width)),
            whole((1, d)),
            whole((1, d)),
        ),
        scratch_shapes=[
            pltpu.VMEM((2 * HALF, d), F32),
            pltpu.VMEM((rows, d), BF16),
            pltpu.VMEM((rows, 2 * d), BF16),
        ],
        compiler_params=params(),
        name="backward",
        cost_estimate=cost(8e9, 18 * rows * d),
    )(table, h, slope, sig, freq, conv, gbn, wf, stats, sums, bn_gain, theirs, own, high, low, high_t, low_t, back)


def inputs_back(table, frames, grad_a, gain, w_in):
    rows, d = frames.shape
    steps = rows // (SPAN * PER_STEP)
    return pl.pallas_call(
        inputs_kernel,
        grid=(steps,),
        out_shape=sds((rows, d), BF16),
        in_specs=[SMEM, whole(frames.shape), rows_of(grad_a.shape, steps), whole(gain.shape), whole(w_in.shape)],
        out_specs=whole((rows, d)),
        compiler_params=params(),
        name="inputs_back",
        cost_estimate=cost(6e9, 12 * rows * d),
    )(table, frames, grad_a, gain, w_in)


def pair_sum(own, got):
    rows, width = own.shape
    part = pl.BlockSpec((rows // 2, width), lambda i: (i, 0))
    return pl.pallas_call(
        pair_kernel,
        grid=(2,),
        out_shape=sds((rows, width), BF16),
        in_specs=[part, part],
        out_specs=part,
        compiler_params=pltpu.CompilerParams(vmem_limit_bytes=SMALL_LIMIT),
        name="pair_sum",
        cost_estimate=cost(2 * rows * width, 6 * rows * width),
    )(own, got)


def collect(got, count):
    vmem = pl.BlockSpec(memory_space=pltpu.VMEM)
    return pl.pallas_call(
        collect_kernel,
        out_shape=sds((count, *got.shape[1:]), BF16),
        in_specs=[vmem],
        out_specs=vmem,
        compiler_params=pltpu.CompilerParams(vmem_limit_bytes=SMALL_LIMIT),
        name="collect",
    )(got)


def finish(every, w_rows, gain_rows, taps):
    share, width = w_rows.shape
    d = width // 2
    vmem = pl.BlockSpec(memory_space=pltpu.VMEM)
    return pl.pallas_call(
        finish_kernel,
        out_shape=(sds((share, width), F32), sds((share, d), F32), sds((share, taps), F32), sds((1, share), F32)),
        in_specs=[vmem] * 3,
        out_specs=(vmem,) * 4,
        compiler_params=pltpu.CompilerParams(vmem_limit_bytes=SMALL_LIMIT),
        name="finish",
    )(every, w_rows, gain_rows)


def swapped(value, axes):
    return lax.all_to_all(value, axes, split_axis=0, concat_axis=0, tiled=True)


def over_bucket(theirs, own, loaders, ahead):
    got = lax.ppermute(theirs, "c", [(0, 1), (1, 0)])
    both = pair_sum(own, got).reshape(loaders, -1, own.shape[1])
    both, ahead = lax.optimization_barrier((both, ahead))
    return swapped(both, BUCKET), ahead


def local(frames, lengths, owners, upstream, ln_gain, w_in, w_dw, bn_gain, bn_bias, w_out):
    loaders = lax.axis_size(BUCKET)
    me = lax.axis_index(BUCKET)
    rows, d = frames.shape
    taps = w_dw.shape[1]
    share = d // loaders
    total = float(upstream.shape[0] * loaders * lax.axis_size(DP))
    tabs = tuple(jnp.asarray(v) for v in tables(taps))
    w_rows = lax.dynamic_slice_in_dim(w_in, me * share, share, 0)
    gain_rows = lax.dynamic_slice_in_dim(ln_gain, me * share, share, 0).reshape(1, share)
    gain, bn_gain, bn_bias = (v.reshape(1, d) for v in (ln_gain, bn_gain, bn_bias))

    dy, table = unpack(lengths, owners, upstream, loaders)
    dy = swapped(dy.reshape(loaders, SPAN, d), BUCKET).reshape(rows, d)
    h, slope, sig, freq, conv, wf, stats = forward(table, frames, gain, w_in, w_dw, tabs)
    stats = lax.psum(lax.psum(lax.psum(stats, "c"), "y"), "x")
    stats, dy = lax.optimization_barrier((stats, dy))
    stats = swapped(jnp.broadcast_to(stats, (lax.axis_size("z"), *stats.shape)), "z")
    live_dy, grad = project(table, dy, w_out)
    swished, gbn, sums, stats = middle(total, conv, grad, stats, bn_gain, bn_bias, lax.axis_size(("c", "z")))
    sums = jnp.sum(swapped(sums, ("c", "z")), axis=0)
    out, theirs, own = outputs(swished, live_dy, w_out)
    out, sums = lax.optimization_barrier((out, sums))
    out = swapped(out.reshape(loaders, SPAN, d), BUCKET).reshape(rows, d)
    sums = lax.psum(lax.psum(sums, "y"), "x")
    grad_a, theirs, own, bias_total, gain_total = backward(
        total, table, h, slope, sig, freq, conv, gbn, wf, stats, sums, bn_gain, theirs, own, tabs
    )
    got, out = over_bucket(theirs, own, loaders, out)
    gframes = inputs_back(table, frames, grad_a, gain, w_in)
    out_frames = pack(table, out, upstream.shape[0])
    got, gframes, out_frames = lax.optimization_barrier((got, gframes, out_frames))
    every = swapped(collect(got, lax.axis_size(DP)), DP)
    gwin, gwout, gwdw, gln = finish(every, w_rows, gain_rows, taps)
    return (
        out_frames,
        gframes,
        gwin,
        gwout,
        gwdw,
        gln.reshape(share),
        gain_total.reshape(d),
        bias_total.reshape(d),
    )


def solution(mesh):
    torus = Mesh(mesh.devices.reshape(4, 2, 4, 8), ("y", "c", "x", "z"))
    in_specs = (P(EVERY, None), P(DP, None), P(DP, None), P(EVERY, None)) + (P(),) * 6
    out_specs = (P(EVERY, None), P(EVERY, None), P(BUCKET, None), P(BUCKET, None), P(BUCKET, None), P(BUCKET), P(), P())
    return jax.shard_map(local, mesh=torus, in_specs=in_specs, out_specs=out_specs, check_vma=False)
```
